256 devices in a mesh: dp: 2 (over core), lon: 16 (over x, y), lat: 8 (over z).
Axes of the slice: x: 4, y: 4, z: 8, core: 2. Of those that a mesh axis runs over, the one named last changes fastest.
Arguments:
- obs_values: bfloat16 [2, 16, 8, 64, 16, 512], P('dp', 'lon', 'lat'), may hold values from -6 to 6
- obs_coords: float32 [2, 16, 8, 64, 2, 512], P('dp', 'lon', 'lat'), may hold values from -0.5 to 15.5
- obs_dest: int32 [2, 16, 8, 64], P('dp', 'lon', 'lat'), may hold values from 0 to 127, as said below
- obs_count: int32 [2, 16, 8, 64], P('dp', 'lon', 'lat'), may hold values from 1 to 512
- embed_weight: bfloat16 [17, 256], replicated, may hold values from -1.5 to 1.5
- patch_weight: bfloat16 [1024, 256], replicated, may hold values from -0.1875 to 0.1875
- depth_kernel: bfloat16 [2, 49, 256], replicated, may hold values from -0.875 to 0.875
- expand_weight: bfloat16 [2, 256, 1024], replicated, may hold values from -0.375 to 0.375
- reduce_weight: bfloat16 [2, 1024, 256], replicated, may hold values from -0.1875 to 0.1875
- out_cotangent: bfloat16 [2, 128, 64, 256], P('dp', 'lon', 'lat'), may hold values from -0.125 to 0.125
Outputs:
- features: bfloat16 [2, 128, 64, 256], P('dp', 'lon', 'lat')
- grad_embed: float32 [17, 256], replicated
- grad_patch: float32 [1024, 256], replicated
- grad_kernel: float32 [2, 49, 256], replicated
- grad_expand: float32 [2, 256, 1024], replicated
- grad_reduce: float32 [2, 1024, 256], replicated
The draws below stay inside these ranges and needn't reach their ends.
Inputs may be any that keep to these rules, and one draw needn't show every extreme that they name: `obs_dest`: the 64 ids of one device are distinct; in every window some tile is named by every device of that window.
All inputs are finite; a program needn't handle non-finite values.
Results may differ from the reference program's by a relative error of at most 0.02.
Values may be sent and summed in bfloat16 or wider, within the bound.
A program may use at most 64 MiB of HBM per device.

```python
import math
import jax
import jax.numpy as jnp
from jax import lax

CH = 256
HID = 1024
OBSF = 16
ROWS = 512
KSIDE = 7
BLOCKS = 2
TILE = 16
WINDOWS = 2
LON_TILES = 16
LAT_TILES = 8
TILES = 128
NBLK = 64
DEVICES = 256


def draw_obs_dest(key, part):
    subkeys = jax.random.split(jax.random.fold_in(key, 17), 4)
    indices = jnp.arange(TILES, dtype=jnp.int32)
    levels = jax.random.randint(subkeys[0], (WINDOWS, TILES), 0, 4)
    hottest = jax.random.randint(subkeys[1], (WINDOWS, 1), 0, TILES)
    levels = jnp.where(indices[None, :] == hottest, 8, levels)
    jitter = jax.random.randint(subkeys[2], (WINDOWS, TILES, TILES), 0, 16)
    scores = (levels[:, None, :] * 16 + jitter) * TILES + indices[None, None, :]
    chosen = lax.top_k(scores, NBLK)[1].astype(jnp.int32)
    shuffle = jax.random.randint(subkeys[3], (WINDOWS, TILES, NBLK), 0, 1024) * NBLK + jnp.arange(NBLK, dtype=jnp.int32)
    slot_order = jnp.argsort(shuffle, axis=-1)
    picked = jnp.take_along_axis(chosen, slot_order, axis=-1)
    return picked.reshape(WINDOWS, LON_TILES, LAT_TILES, NBLK).astype(jnp.int32)


def draw_obs_count(key, part):
    raw_counts = jax.random.randint(jax.random.fold_in(key, 29), (WINDOWS, LON_TILES, LAT_TILES, NBLK), 1, ROWS + ROWS // 2 + 1)
    return jnp.minimum(raw_counts, ROWS).astype(jnp.int32)


def block_levels(key, shape, cuts, low, top_value):
    level = 1.0
    for dim, parts in cuts:
        heights = jax.random.uniform(jax.random.fold_in(jax.random.fold_in(key, 6), dim), (parts,), jnp.float32, low / len(cuts), top_value / len(cuts))
        level = level * jnp.repeat(jnp.exp(heights), shape[dim] // parts).reshape((-1,) + (1,) * (len(shape) - 1 - dim))
    return level


def bell_draw(rng, extent, scale, limit, shards=(), kind=jnp.bfloat16):
    factor_of = block_levels(rng, extent, shards, -0.22, 0.18) if shards else 1.0
    entries = jax.random.normal(rng, extent, jnp.float32) * scale * factor_of
    return jnp.minimum(jnp.maximum(entries, -limit), limit).astype(kind)


def setup_inputs(seed: int = 0) -> dict:
    seeds = jax.random.split(jax.random.key(seed), 11)
    return {
        "obs_values": bell_draw(seeds[0], (WINDOWS, LON_TILES, LAT_TILES, NBLK, OBSF, ROWS), 1.0, 6.0, ((0, 2), (1, 16), (2, 8))),
        "obs_coords": jnp.clip(-0.5 + 16.0 * jax.random.uniform(seeds[1], (WINDOWS, LON_TILES, LAT_TILES, NBLK, 2, ROWS), jnp.float32) ** block_levels(seeds[1], (WINDOWS, LON_TILES, LAT_TILES, NBLK, 2, ROWS), ((0, 2), (1, 16), (2, 8)), -0.2, 0.2), -0.5, 15.5),
        "obs_dest": draw_obs_dest(jax.random.fold_in(seeds[10], 71), 0),
        "obs_count": draw_obs_count(jax.random.fold_in(seeds[10], 71), 0),
        "embed_weight": bell_draw(seeds[4], (OBSF + 1, CH), (OBSF + 1) ** -0.5, 1.5),
        "patch_weight": bell_draw(seeds[5], (4 * CH, CH), (4 * CH) ** -0.5, 0.1875),
        "depth_kernel": bell_draw(seeds[6], (BLOCKS, KSIDE * KSIDE, CH), (KSIDE * KSIDE) ** -0.5, 0.875),
        "expand_weight": bell_draw(seeds[7], (BLOCKS, CH, HID), CH ** -0.5, 0.375),
        "reduce_weight": bell_draw(seeds[8], (BLOCKS, HID, CH), HID ** -0.5, 0.1875),
        "out_cotangent": bell_draw(seeds[9], (WINDOWS, LON_TILES * (TILE // 2), LAT_TILES * (TILE // 2), CH), ((DEVICES * (TILE // 2) * (TILE // 2)) ** -0.5), 0.125, ((0, 2), (1, 16), (2, 8))),
    }


LENGTH_SCALE = 0.7

def layer_norm(field):
    center = lax.optimization_barrier(jnp.mean(field, axis=-1, keepdims=True))
    spread = lax.optimization_barrier(jnp.mean(jnp.square(field - center), axis=-1, keepdims=True))
    return (field - center) * lax.rsqrt(spread + 1e-05)

def exact_gelu(field):
    return jax.nn.gelu(field, approximate=False)

def encode_group(block_values, block_coords, row_counts, tile_side):
    chan_len = block_values.shape[1]
    row_len = block_values.shape[2]
    positions = jnp.arange(row_len, dtype=jnp.int32)
    live = (positions[None, :] < row_counts[:, None].astype(jnp.int32)).astype(jnp.float32).reshape(-1)
    cells = jnp.arange(tile_side).astype(jnp.float32)
    inverse = 0.5 / (LENGTH_SCALE * LENGTH_SCALE)
    lon_pos = block_coords[:, 0, :].reshape(-1)
    lat_pos = block_coords[:, 1, :].reshape(-1)
    lon_factor = jnp.exp(-jnp.square(lon_pos[None, :] - cells[:, None]) * inverse) * live[None, :]
    lat_factor = jnp.exp(-jnp.square(lat_pos[None, :] - cells[:, None]) * inverse).astype(jnp.bfloat16)
    data = jnp.transpose(block_values, (1, 0, 2)).reshape(chan_len, -1).astype(jnp.float32)
    data = jnp.concatenate([data, jnp.ones((1, data.shape[1]), jnp.float32)], axis=0)
    weighted = (data[:, None, :] * lon_factor[None, :, :]).astype(jnp.bfloat16)
    flat = weighted.reshape((chan_len + 1) * tile_side, -1)
    product = lax.dot_general(lat_factor, flat, (((1,), (1,)), ((), ())), preferred_element_type=jnp.float32)
    product = product.reshape(tile_side, chan_len + 1, tile_side)
    return jnp.transpose(product, (1, 2, 0))

def finish_tile(sums):
    density = sums[-1]
    scaled = sums[:-1] * lax.rsqrt(1.0 + density)[None]
    channels = jnp.concatenate([scaled, 0.25 * jnp.log1p(density)[None]], axis=0)
    return jnp.transpose(channels, (1, 2, 0)).astype(jnp.bfloat16)

def to_patches(field):
    batch_len, lon_len, lat_len, chan_len = field.shape
    grouped = field.reshape(batch_len, lon_len // 2, 2, lat_len // 2, 2, chan_len)
    grouped = jnp.transpose(grouped, (0, 1, 3, 2, 4, 5))
    return grouped.reshape(batch_len * (lon_len // 2) * (lat_len // 2), 4 * chan_len)

def from_patches(flat, batch_len, lon_len, lat_len, chan_len):
    grouped = flat.reshape(batch_len, lon_len // 2, lat_len // 2, 2, 2, chan_len)
    grouped = jnp.transpose(grouped, (0, 1, 3, 2, 4, 5))
    return grouped.reshape(batch_len, lon_len, lat_len, chan_len)

def depthwise(padded, kernel):
    kernel_side = int(math.isqrt(kernel.shape[0]))
    lon_len = padded.shape[1] - kernel_side + 1
    lat_len = padded.shape[2] - kernel_side + 1
    running = jnp.zeros((padded.shape[0], lon_len, lat_len, padded.shape[3]), jnp.float32)
    for tap_row in range(kernel_side):
        for tap_col in range(kernel_side):
            running = running + padded[:, tap_row:tap_row + lon_len, tap_col:tap_col + lat_len, :] * kernel[tap_row * kernel_side + tap_col]
    return running

def kernel_grad(padded, grad_out):
    kernel_side = padded.shape[1] - grad_out.shape[1] + 1
    lon_len = grad_out.shape[1]
    lat_len = grad_out.shape[2]
    taps = []
    for tap_row in range(kernel_side):
        for tap_col in range(kernel_side):
            piece = padded[:, tap_row:tap_row + lon_len, tap_col:tap_col + lat_len, :]
            taps.append(lax.optimization_barrier(jnp.sum(piece * grad_out, axis=(0, 1, 2))))
    return jnp.stack(taps)

def input_grad(grad_padded, kernel):
    kernel_side = int(math.isqrt(kernel.shape[0]))
    lon_len = grad_padded.shape[1] - kernel_side + 1
    lat_len = grad_padded.shape[2] - kernel_side + 1
    twice = 2 * (kernel_side // 2)
    running = jnp.zeros((grad_padded.shape[0], lon_len, lat_len, grad_padded.shape[3]), jnp.float32)
    for tap_row in range(kernel_side):
        for tap_col in range(kernel_side):
            row_start = twice - tap_row
            col_start = twice - tap_col
            running = running + grad_padded[:, row_start:row_start + lon_len, col_start:col_start + lat_len, :] * kernel[tap_row * kernel_side + tap_col]
    return running

def stem_forward(encoded, embed_weight, patch_weight):
    batch_len, lon_len, lat_len, chan_in = encoded.shape
    embedded = jnp.dot(encoded.reshape(-1, chan_in), embed_weight, preferred_element_type=jnp.float32)
    embedded = embedded.reshape(batch_len, lon_len, lat_len, -1)
    normed_grid = layer_norm(embedded).astype(jnp.bfloat16)
    first = jnp.dot(to_patches(normed_grid), patch_weight, preferred_element_type=jnp.float32).astype(jnp.bfloat16)
    first = first.reshape(batch_len, lon_len // 2, lat_len // 2, -1)
    return (embedded, normed_grid, first)

def block_forward(state, padded, kernel, expand, reduce_weight):
    chan_len = state.shape[3]
    depth_out = depthwise(padded.astype(jnp.float32), kernel.astype(jnp.float32))
    normed = layer_norm(depth_out).astype(jnp.bfloat16)
    act = jnp.dot(normed.reshape(-1, chan_len), expand, preferred_element_type=jnp.float32)
    hidden = exact_gelu(act).astype(jnp.bfloat16)
    branch = jnp.dot(hidden, reduce_weight, preferred_element_type=jnp.float32).reshape(state.shape)
    following = (state.astype(jnp.float32) + branch).astype(jnp.bfloat16)
    return (following, (depth_out, normed, act, hidden))

def block_backward(grad_next, padded, stored, kernel, expand, reduce_weight, extend):
    depth_out, normed, act, hidden = stored
    chan_len = grad_next.shape[3]
    grad_flat = grad_next.reshape(-1, chan_len)
    g_reduce = jnp.dot(hidden.T, grad_flat, preferred_element_type=jnp.float32)
    grad_hidden = jnp.dot(grad_flat, reduce_weight.T, preferred_element_type=jnp.float32)
    grad_act = jax.vjp(exact_gelu, act)[1](grad_hidden)[0].astype(jnp.bfloat16)
    g_expand = jnp.dot(normed.reshape(-1, chan_len).T, grad_act, preferred_element_type=jnp.float32)
    grad_normed = jnp.dot(grad_act, expand.T, preferred_element_type=jnp.float32).reshape(grad_next.shape)
    grad_depth = jax.vjp(layer_norm, depth_out)[1](grad_normed)[0]
    g_kernel = kernel_grad(padded.astype(jnp.float32), grad_depth)
    grad_state = grad_next.astype(jnp.float32) + input_grad(extend(grad_depth), kernel.astype(jnp.float32))
    return (grad_state.astype(jnp.bfloat16), g_kernel, g_expand, g_reduce)

def stem_backward(grad_first, encoded, embedded, normed_grid, embed_weight, patch_weight):
    batch_len, lon_len, lat_len, chan_in = encoded.shape
    chan_len = grad_first.shape[3]
    grad_flat = grad_first.reshape(-1, chan_len)
    g_patch = jnp.dot(to_patches(normed_grid).T, grad_flat, preferred_element_type=jnp.float32)
    grad_normed = jnp.dot(grad_flat, patch_weight.T, preferred_element_type=jnp.float32)
    grad_normed = from_patches(grad_normed, batch_len, lon_len, lat_len, chan_len)
    grad_embedded = jax.vjp(layer_norm, embedded)[1](grad_normed)[0].astype(jnp.bfloat16)
    g_embed = jnp.dot(encoded.reshape(-1, chan_in).T, grad_embedded.reshape(-1, chan_len), preferred_element_type=jnp.float32)
    return (g_embed, g_patch)

def pad_grid(field):
    reach = KSIDE // 2
    wrapped = jnp.pad(field, ((0, 0), (reach, reach), (0, 0), (0, 0)), mode='wrap')
    return jnp.pad(wrapped, ((0, 0), (0, 0), (reach, reach), (0, 0)))

def source_step(carry, pieces):
    block_values, block_coords, dest_tiles, row_counts = pieces

    def one_block(single_values, single_coords, single_count):
        return encode_group(single_values[None], single_coords[None], single_count[None], TILE)
    terms = jax.vmap(one_block)(block_values, block_coords, row_counts)
    return (carry.at[dest_tiles.astype(jnp.int32)].add(terms), None)

def reference(obs_values, obs_coords, obs_dest, obs_count, embed_weight, patch_weight, depth_kernel, expand_weight, reduce_weight, out_cotangent):
    window_grids = []
    for window in range(WINDOWS):
        block_values = obs_values[window].reshape(TILES, NBLK, OBSF, ROWS)
        block_coords = obs_coords[window].reshape(TILES, NBLK, 2, ROWS)
        dest_tiles = obs_dest[window].reshape(TILES, NBLK)
        row_counts = obs_count[window].reshape(TILES, NBLK)
        start = jnp.zeros((TILES, OBSF + 1, TILE, TILE), jnp.float32)
        sums, unused = lax.scan(source_step, start, (block_values, block_coords, dest_tiles, row_counts))
        tile_grids = jax.vmap(finish_tile)(sums)
        grid = tile_grids.reshape(LON_TILES, LAT_TILES, TILE, TILE, OBSF + 1)
        grid = jnp.transpose(grid, (0, 2, 1, 3, 4)).reshape(LON_TILES * TILE, LAT_TILES * TILE, OBSF + 1)
        window_grids.append(grid)
    encoded = jnp.stack(window_grids)
    embedded, normed_grid, state = stem_forward(encoded, embed_weight, patch_weight)
    records = []
    for index in range(BLOCKS):
        padded = pad_grid(state)
        following, stored = block_forward(state, padded, depth_kernel[index], expand_weight[index], reduce_weight[index])
        records.append((padded, stored))
        state = following
    features = state
    cotangent = out_cotangent
    kernels = [None] * BLOCKS
    expands = [None] * BLOCKS
    reduces = [None] * BLOCKS
    for index in reversed(range(BLOCKS)):
        padded, stored = records[index]
        cotangent, kernels[index], expands[index], reduces[index] = block_backward(cotangent, padded, stored, depth_kernel[index], expand_weight[index], reduce_weight[index], pad_grid)
    g_embed, g_patch = stem_backward(cotangent, encoded, embedded, normed_grid, embed_weight, patch_weight)
    return (features, g_embed, g_patch, jnp.stack(kernels), jnp.stack(expands), jnp.stack(reduces))
```

```python
import functools
import math

import jax
import jax.numpy as jnp
from jax import lax
from jax.experimental import pallas as pl
from jax.experimental.pallas import tpu as pltpu
from jax.sharding import PartitionSpec as P

MESH = pl.DeviceIdType.MESH
F32 = jnp.float32
BF16 = jnp.bfloat16
OBSF = 16
KSIDE = 7
REACH = 3
TILE = 16
SIDE = 8
CELLS = 64
CH = 256
HID = 1024
INVERSE = 0.5 / (0.7 * 0.7)
PADW = 16
NT = (((1,), (1,)), ((), ()))
TN = (((0,), (0,)), ((), ()))


def dot(a, b, dims=(((1,), (0,)), ((), ()))):
    return lax.dot_general(a, b, dims, preferred_element_type=F32)


def encode_kernel(nx, ny, nz, dest_ref, count_ref, values_ref, coords_ref, p0_ref, p1_ref, dens_ref):
    p0_ref[...] = jnp.zeros_like(p0_ref)
    p1_ref[...] = jnp.zeros_like(p1_ref)
    dens_ref[...] = jnp.zeros_like(dens_ref)
    rows = values_ref.shape[2]
    order = lax.broadcasted_iota(jnp.int32, (TILE, rows), 0)
    cell = (2 * (order % SIDE) + order // SIDE).astype(F32)
    lane = lax.broadcasted_iota(jnp.int32, (TILE, rows), 1)
    ones = jnp.ones((OBSF, rows), BF16)

    def one_block(block, carry):
        tile = dest_ref[block]
        pair = coords_ref[block]
        a = jnp.exp(-jnp.square(pair[0:1, :] - cell) * INVERSE)
        a = jnp.where(lane < count_ref[block], a, 0.0)
        b = jnp.exp(-jnp.square(pair[1:2, :] - cell) * INVERSE)
        parts = []
        for i in range(2):
            for j in range(2):
                left = a[i * SIDE : (i + 1) * SIDE]
                right = b[j * SIDE : (j + 1) * SIDE]
                parts.append((left[:, None, :] * right[None]).reshape(CELLS, rows))
        weight = jnp.concatenate(parts, axis=0).astype(BF16)
        sums = dot(jnp.concatenate([values_ref[block], ones], axis=0), weight, NT)
        lon = tile // nz
        lat = tile % nz
        x = lon // ny
        y = lon % ny
        p0_ref[lon * (nz + 1) + lat] = sums[:OBSF, :128].astype(BF16)
        p1_ref[(y * nx + x) * nz + lat] = sums[:OBSF, 128:].astype(BF16)
        dens_ref[lon, pl.ds(lat, 1), :] = sums[OBSF : OBSF + 1, :128]
        dens_ref[lon, pl.ds(SIDE + lat, 1), :] = sums[OBSF : OBSF + 1, 128:]
        return carry

    lax.fori_loop(0, values_ref.shape[0], one_block, 0, unroll=2)
    for lon in range(nx * ny):
        p0_ref[lon * (nz + 1) + nz] = dens_ref[lon].astype(BF16)


def encode(nx, ny, nz, dest, count, values, coords):
    lon = nx * ny
    return pl.pallas_call(
        functools.partial(encode_kernel, nx, ny, nz),
        out_shape=(
            jax.ShapeDtypeStruct((lon * (nz + 1), 16, 128), BF16),
            jax.ShapeDtypeStruct((lon * nz, 16, 128), BF16),
        ),
        in_specs=[pl.BlockSpec(memory_space=pltpu.SMEM)] * 2 + [pl.BlockSpec(memory_space=pltpu.VMEM)] * 2,
        out_specs=(pl.BlockSpec(memory_space=pltpu.VMEM),) * 2,
        scratch_shapes=[pltpu.VMEM((lon, 16, 128), F32)],
        compiler_params=pltpu.CompilerParams(vmem_limit_bytes=32 * 2**20),
    )(dest, count, values, coords)


def normalise(field):
    center = jnp.mean(field, axis=-1, keepdims=True)
    shifted = field - center
    scale = lax.rsqrt(jnp.mean(jnp.square(shifted), axis=-1, keepdims=True) + 1e-05)
    return shifted * scale, scale


def normalise_grad(normed, scale, grad):
    return scale * (
        grad
        - jnp.mean(grad, axis=-1, keepdims=True)
        - normed * jnp.mean(grad * normed, axis=-1, keepdims=True)
    )


def cdf(field):
    return 0.5 * (1.0 + lax.erf(field * math.sqrt(0.5)))


def group_sizes(nx, ny, nz, np_half, nq_half):
    return np_half // (nx * ny), nq_half // (nx * ny)


def group_scratch(nx, ny, nz, n_p, n_q, scatter):
    up, uq = n_p // (nx * ny), n_q // (nx * ny)

    def units(*lead):
        return pltpu.VMEM(tuple(lead) + (16, 128), BF16)

    plan = {
        "gp": units(2, n_p), "gq": units(2, n_q),
        "cp": units(n_p), "cq": units(n_q),
        "sp": units(n_p), "sq": units(n_q),
        "l1p": units(nx - 1, n_p // nx), "l1q": units(ny - 1, n_q // ny),
        "s2p": units(n_p // nx), "s2q": units(n_q // ny),
        "l2p": units(ny - 1, up), "l2q": units(nx - 1, uq),
        "s3": units(up + uq),
        "fp": units(2, n_p), "fq": units(2, n_q),
    }
    if scatter:
        piece = (up + uq) // nz
        plan["l3"] = units(nz - 1, piece)
        plan["f3"] = units(nz, piece)
    else:
        plan["l3"] = units(nz, up + uq)
    return plan


GROUPS = (("A", 64, 64, True), ("B", 64, 64, True), ("C", 64, 16, False))


def scratch_plan(nx, ny, nz):
    def units(*lead):
        return pltpu.VMEM(tuple(lead) + (16, 128), BF16)

    plan = {
        "r0": units(nx - 1, ny * (nz + 1)), "r1": units(ny - 1, nx * nz),
        "q0": units(ny * (nz + 1)), "q1": units(nx * nz),
        "t0": units(ny - 1, nz + 1), "t1": units(nx - 1, nz),
        "zbuf": units(nz, 3), "zr": units(nz - 1, 3),
        "dens": pltpu.VMEM((16, 128), F32),
        "ew": pltpu.VMEM((32, CH), F32),
        "kg": pltpu.VMEM((112, CH), F32),
        "eg": pltpu.VMEM((32, CH), F32),
        "tap": pltpu.VMEM((KSIDE * KSIDE, 8, CH), F32),
    }
    for k in range(4):
        plan["halo_src%d" % k] = pltpu.VMEM((2, CELLS, CH), BF16)
        plan["halo_dst%d" % k] = pltpu.VMEM((8, CELLS // 2, CH), BF16)
        plan["pad%d" % k] = pltpu.VMEM((2, 14 * PADW, 128), F32)
    plan["cols"] = pltpu.VMEM((CELLS, CH), F32)
    for name, n_p, n_q, scatter in GROUPS:
        for key, value in group_scratch(nx, ny, nz, n_p, n_q, scatter).items():
            plan[name + key] = value
    return plan


def copy_count(nx, ny, nz):
    total = 2 * (nx + ny - 2) + (nz - 1) + 4 * 8
    for _, _, _, scatter in GROUPS:
        total += 2 * 2 + 4 * (nx + ny - 2) + (nz - 1) * (2 if scatter else 1)
    return total


HALOS = tuple((i, j) for i in (-1, 0, 1) for j in (-1, 0, 1) if (i, j) != (0, 0))


def net_kernel(nx, ny, nz, names, *refs):
    (p0, p1, embed_w, patch_w, depth_k, expand_w, reduce_w, cot,
     feat, o_embed, o_patch, o_kernel, o_expand, o_reduce) = refs[:14]
    s = dict(zip(names, refs[14:]))
    send_sem, recv_sem = refs[14 + len(names):]
    core = lax.axis_index("dp")
    lon = lax.axis_index("lon")
    z = lax.axis_index("lat")
    x = lon // ny
    y = lon % ny
    nlon = nx * ny

    def at_core():
        return (1 - core, lon, z)

    def at_x(d):
        return (core, ((x + d) % nx) * ny + y, z)

    def at_y(d):
        return (core, x * ny + (y + d) % ny, z)

    def at_z(d):
        return (core, lon, (z + d) % nz)

    def at_halo(i, j):
        return (core, (lon + i + nlon) % nlon, (z + j + nz) % nz)

    barrier = pltpu.get_barrier_semaphore()
    peers = [at_core()] + [at_x(d) for d in range(1, nx)] + [at_y(d) for d in range(1, ny)]
    peers += [at_z(d) for d in range(1, nz)] + [at_halo(i, j) for i, j in HALOS]
    for peer in peers:
        pl.semaphore_signal(barrier, inc=1, device_id=peer, device_id_type=MESH)
    pl.semaphore_wait(barrier, len(peers))

    sent = []

    def push(src, dst, device, land=None):
        index = len(sent)

        def make(target):
            return pltpu.make_async_remote_copy(
                src_ref=src, dst_ref=target, send_sem=send_sem.at[index], recv_sem=recv_sem.at[index],
                device_id=device, device_id_type=MESH,
            )

        copy = make(dst)
        copy.start()
        sent.append(copy)
        return copy if land is None else make(land)

    def settle(copies):
        for copy in copies:
            copy.wait_recv()

    def spread(src, land, size, count, target):
        position = {"x": x, "y": y}[target]
        where = {"x": at_x, "y": at_y}[target]
        return [
            push(src.at[pl.ds(((position + d) % count) * size, size)], land.at[d - 1], where(d))
            for d in range(1, count)
        ]

    def fold(out, first, land, count, offset, size, step):
        for i in range(0, size, step):
            total = first[pl.ds(offset + i, step)].astype(F32)
            for d in range(count - 1):
                total = total + land[d, i : i + step].astype(F32)
            out[i : i + step] = total.astype(BF16)

    w0, w1 = nz + 1, nz
    copies = spread(p0, s["r0"], ny * w0, nx, "x") + spread(p1, s["r1"], nx * w1, ny, "y")
    s["ew"][...] = jnp.zeros_like(s["ew"])
    s["ew"][0 : OBSF + 1, :] = embed_w[...].astype(F32)
    s["kg"][...] = jnp.zeros_like(s["kg"])
    embed_m = s["ew"][...].astype(BF16)
    settle(copies)
    fold(s["q0"], p0, s["r0"], nx, x * (ny * w0), ny * w0, w0)
    fold(s["q1"], p1, s["r1"], ny, y * (nx * w1), nx * w1, w1)
    copies = spread(s["q0"], s["t0"], w0, ny, "y") + spread(s["q1"], s["t1"], w1, nx, "x")
    settle(copies)
    total0 = s["q0"][pl.ds(y * w0, w0)].astype(F32)
    for d in range(ny - 1):
        total0 = total0 + s["t0"][d].astype(F32)
    total0 = total0.astype(BF16)
    total1 = s["q1"][pl.ds(x * w1, w1)].astype(F32)
    for d in range(nx - 1):
        total1 = total1 + s["t1"][d].astype(F32)
    total1 = total1.astype(BF16)
    for k in range(nz):
        s["zbuf"][k, 0] = total0[k]
        s["zbuf"][k, 1] = total1[k]
        s["zbuf"][k, 2] = total0[nz]
    copies = [push(s["zbuf"].at[(z + d) % nz], s["zr"].at[d - 1], at_z(d)) for d in range(1, nz)]
    settle(copies)
    sums = s["zbuf"][z].astype(F32)
    for d in range(nz - 1):
        sums = sums + s["zr"][d].astype(F32)
    s["dens"][...] = sums[2]
    density = jnp.concatenate([s["dens"][pl.ds(z, 1), :], s["dens"][pl.ds(SIDE + z, 1), :]], axis=1)
    scaled = jnp.concatenate([sums[0], sums[1]], axis=1) * lax.rsqrt(1.0 + density)
    level = jnp.where(
        lax.broadcasted_iota(jnp.int32, (16, CH), 0) == 0,
        jnp.broadcast_to(0.25 * jnp.log(1.0 + density), (16, CH)), 0.0,
    )
    encoded = jnp.concatenate([scaled, level], axis=0).astype(BF16)

    grid_hat, grid_scale = normalise(dot(encoded, embed_m, TN))
    normed_grid = grid_hat.astype(BF16)
    first = jnp.zeros((CELLS, CH), F32)
    for i in range(4):
        first = first + dot(normed_grid[i * CELLS : (i + 1) * CELLS], patch_w[i * CH : (i + 1) * CH, :])
    state = first.astype(BF16)

    def halo_send(which, field):
        src, dst = s["halo_src%d" % which], s["halo_dst%d" % which]
        src[0] = field.astype(BF16)
        src[1] = jnp.swapaxes(field.reshape(SIDE, SIDE, CH), 0, 1).reshape(CELLS, CH).astype(BF16)
        found = []
        for index, (i, j) in enumerate(HALOS):
            if j == 0:
                piece = src.at[0, pl.ds(32 if i > 0 else 0, 32)]
            else:
                piece = src.at[1, pl.ds(32 if j > 0 else 0, 32)]
            found.append(push(piece, dst.at[index], at_halo(i, j)))
        return found

    def pad_inner(which, field):
        pad = s["pad%d" % which]
        pad[...] = jnp.zeros_like(pad)
        for p in range(SIDE):
            for h in range(2):
                pad[h, pl.ds((REACH + p) * PADW + REACH, SIDE), :] = field[
                    p * SIDE : (p + 1) * SIDE, h * 128 : (h + 1) * 128
                ]

    def halo_wait(which, copies):
        pad, dst = s["pad%d" % which], s["halo_dst%d" % which]
        settle(copies)
        for index, (i, j) in enumerate(HALOS):
            if j == 0:
                for r in range(REACH):
                    if i > 0:
                        row, at = r, 1 + r
                    else:
                        row, at = REACH + SIDE + r, r
                    strip = dst[index].astype(F32)[at * SIDE : (at + 1) * SIDE]
                    for h in range(2):
                        pad[h, pl.ds(row * PADW + REACH, SIDE), :] = strip[:, h * 128 : (h + 1) * 128]
                continue
            inside = (z > 0) if j > 0 else (z < nz - 1)
            keep = jnp.where(inside, 1.0, 0.0).astype(F32)
            block = dst[index].astype(F32) * keep
            for r in range(REACH):
                if j > 0:
                    column, at = r, 1 + r
                else:
                    column, at = REACH + SIDE + r, r
                strip = block[at * SIDE : (at + 1) * SIDE]
                if i == 0:
                    top, strip = REACH, strip
                elif i > 0:
                    top, strip = 0, strip[SIDE - REACH :]
                else:
                    top, strip = REACH + SIDE, strip[:REACH]
                for h in range(2):
                    pad[h, pl.ds(top * PADW + column, strip.shape[0], PADW), :] = strip[:, h * 128 : (h + 1) * 128]

    def window(which, column):
        pad = s["pad%d" % which]
        return jnp.stack(
            [
                jnp.concatenate([pad[h, pl.ds(p * PADW + column, SIDE), :] for h in range(2)], axis=1)
                for p in range(14)
            ],
            axis=0,
        )

    def convolve(which, kernel, flip):
        total = jnp.zeros((SIDE, SIDE, CH), F32)
        for b in range(KSIDE):
            part = window(which, b)
            for a in range(KSIDE):
                tap = KSIDE * a + b
                if flip:
                    tap = KSIDE * KSIDE - 1 - tap
                total = total + part[a : a + SIDE] * kernel[tap : tap + 1, :].reshape(1, 1, CH)
        return total.reshape(CELLS, CH)

    def kernel_grad(which, grad, row):
        grad = grad.reshape(SIDE, SIDE, CH)
        for b in range(KSIDE):
            part = window(which, b)
            for a in range(KSIDE):
                s["tap"][KSIDE * a + b] = jnp.sum(part[a : a + SIDE] * grad, axis=0)
        s["kg"][row : row + KSIDE * KSIDE, :] = jnp.sum(s["tap"][...], axis=1)

    stored = []
    for k in range(2):
        field = state.astype(F32)
        copies = halo_send(k, field)
        pad_inner(k, field)
        kernel = depth_k[k].astype(F32)
        halo_wait(k, copies)
        hat, scale = normalise(convolve(k, kernel, False))
        normed = hat.astype(BF16)
        act = dot(normed, expand_w[k])
        share = cdf(act)
        hidden = (act * share).astype(BF16)
        state = (field + dot(hidden, reduce_w[k])).astype(BF16)
        slope = share + act * jnp.exp(-0.5 * jnp.square(act)) * (1.0 / math.sqrt(2.0 * math.pi))
        stored.append((hat, scale, normed, hidden, slope))
    feat[...] = state

    progress = {}

    def group(name):
        return next(entry for entry in GROUPS if entry[0] == name)

    def begin(name):
        gp, gq = s[name + "gp"], s[name + "gq"]
        progress[name] = [
            push(gp.at[1 - core], s[name + "cp"], at_core()),
            push(gq.at[1 - core], s[name + "cq"], at_core()),
        ]

    def stage_first(name):
        _, n_p, n_q, _ = group(name)
        settle(progress[name])
        for key, n in (("p", n_p), ("q", n_q)):
            own, got, out = s[name + "g" + key], s[name + "c" + key], s[name + "s" + key]

            def body(i, carry, own=own, got=got, out=out):
                at = pl.ds(pl.multiple_of(i * 8, 8), 8)
                out[at] = (own[core, at].astype(F32) + got[at].astype(F32)).astype(BF16)
                return carry

            lax.fori_loop(0, n // 8, body, 0)
        progress[name] = spread(s[name + "sp"], s[name + "l1p"], n_p // nx, nx, "x") + spread(
            s[name + "sq"], s[name + "l1q"], n_q // ny, ny, "y"
        )

    def stage_second(name):
        _, n_p, n_q, _ = group(name)
        settle(progress[name])
        fold(s[name + "s2p"], s[name + "sp"], s[name + "l1p"], nx, x * (n_p // nx), n_p // nx, min(8, n_p // nx))
        fold(s[name + "s2q"], s[name + "sq"], s[name + "l1q"], ny, y * (n_q // ny), n_q // ny, min(8, n_q // ny))
        progress[name] = spread(s[name + "s2p"], s[name + "l2p"], n_p // nlon, ny, "y") + spread(
            s[name + "s2q"], s[name + "l2q"], n_q // nlon, nx, "x"
        )

    def stage_third(name):
        _, n_p, n_q, scatter = group(name)
        up, uq = n_p // nlon, n_q // nlon
        settle(progress[name])
        s3 = s[name + "s3"]
        fold(s3.at[pl.ds(0, up)], s[name + "s2p"], s[name + "l2p"], ny, y * up, up, min(8, up))
        fold(s3.at[pl.ds(up, uq)], s[name + "s2q"], s[name + "l2q"], nx, x * uq, uq, min(8, uq))
        l3 = s[name + "l3"]
        if scatter:
            piece = (up + uq) // nz
            progress[name] = [
                push(s3.at[pl.ds(((z + d) % nz) * piece, piece)], l3.at[d - 1], at_z(d)) for d in range(1, nz)
            ]
        else:
            l3[z] = s3[...]
            progress[name] = [push(s3, l3.at[z], at_z(d), l3.at[(z + nz - d) % nz]) for d in range(1, nz)]

    def stage_gather(name):
        _, n_p, n_q, _ = group(name)
        piece = (n_p + n_q) // (nlon * nz)
        settle(progress[name])
        s3, l3, f3 = s[name + "s3"], s[name + "l3"], s[name + "f3"]
        total = s3[pl.ds(z * piece, piece)].astype(F32)
        for d in range(nz - 1):
            total = total + l3[d].astype(F32)
        f3[z] = total.astype(BF16)
        progress[name] = [push(f3.at[z], f3.at[z], at_z(d), f3.at[(z + nz - d) % nz]) for d in range(1, nz)]

    def stage_back_second(name):
        _, n_p, n_q, scatter = group(name)
        up, uq = n_p // nlon, n_q // nlon
        settle(progress[name])
        fp, fq = s[name + "fp"], s[name + "fq"]
        at_p, at_q = x * (n_p // nx) + y * up, y * (n_q // ny) + x * uq
        if scatter:
            done = s[name + "f3"][...].reshape(up + uq, 16, 128)
        else:
            total = s[name + "l3"][0].astype(F32)
            for d in range(1, nz):
                total = total + s[name + "l3"][d].astype(F32)
            done = total.astype(BF16)
        fp[core, pl.ds(at_p, up)] = done[:up]
        fq[core, pl.ds(at_q, uq)] = done[up:]

        def from_p(d):
            return fp.at[core, pl.ds(x * (n_p // nx) + ((y + ny - d) % ny) * up, up)]

        def from_q(d):
            return fq.at[core, pl.ds(y * (n_q // ny) + ((x + nx - d) % nx) * uq, uq)]

        progress[name] = [push(from_p(0), from_p(0), at_y(d), from_p(d)) for d in range(1, ny)]
        progress[name] += [push(from_q(0), from_q(0), at_x(d), from_q(d)) for d in range(1, nx)]

    def stage_back_first(name):
        _, n_p, n_q, _ = group(name)
        settle(progress[name])
        fp, fq = s[name + "fp"], s[name + "fq"]
        hp, hq = n_p // nx, n_q // ny

        def from_p(d):
            return fp.at[core, pl.ds(((x + nx - d) % nx) * hp, hp)]

        def from_q(d):
            return fq.at[core, pl.ds(((y + ny - d) % ny) * hq, hq)]

        progress[name] = [push(from_p(0), from_p(0), at_x(d), from_p(d)) for d in range(1, nx)]
        progress[name] += [push(from_q(0), from_q(0), at_y(d), from_q(d)) for d in range(1, ny)]

    def stage_back_core(name):
        settle(progress[name])
        fp, fq = s[name + "fp"], s[name + "fq"]
        progress[name] = [
            push(fp.at[core], fp.at[core], at_core(), fp.at[1 - core]),
            push(fq.at[core], fq.at[core], at_core(), fq.at[1 - core]),
        ]

    def write_tall(out, fp):
        for h in range(2):
            for r in range(0, 64, 8):
                out[r * 16 : (r + 8) * 16, h * 128 : (h + 1) * 128] = fp[h, r : r + 8].astype(F32).reshape(128, 128)

    def finish(name):
        settle(progress[name])
        fp, fq = s[name + "fp"], s[name + "fq"]
        if name == "C":
            write_tall(o_patch, fp)
            for h in range(2):
                at = slice(h * 128, (h + 1) * 128)
                s["kg"][:, at] = fq[h, 0:7].astype(F32).reshape(112, 128)
                s["eg"][:, at] = fq[h, 7:9].astype(F32).reshape(32, 128)
            o_kernel[0] = s["kg"][0:49, :]
            o_kernel[1] = s["kg"][49:98, :]
            o_embed[...] = s["eg"][0 : OBSF + 1, :]
            return
        k = 1 if name == "A" else 0
        write_tall(o_reduce.at[k], fp)
        for lane in range(8):
            part = fq[lane // 4, (lane % 4) * 16 : (lane % 4 + 1) * 16]
            o_expand[k, :, lane * 128 : (lane + 1) * 128] = part.astype(F32).reshape(256, 128)

    def put_tall(name, left, right):
        for h in range(2):
            s[name + "gp"][h] = dot(left, right[:, h * 128 : (h + 1) * 128], TN).astype(BF16).reshape(64, 16, 128)

    def put_wide(name, left, right):
        for lane in range(8):
            part = dot(left, right[:, lane * 128 : (lane + 1) * 128], TN).astype(BF16)
            s[name + "gq"][lane // 4, (lane % 4) * 16 : (lane % 4 + 1) * 16] = part.reshape(16, 16, 128)

    cotangent = cot[...]
    for k in (1, 0):
        name = "A" if k == 1 else "B"
        hat, scale, normed, hidden, slope = stored[k]
        grad_act = (dot(cotangent, reduce_w[k], NT) * slope).astype(BF16)
        grad_depth = normalise_grad(hat, scale, dot(grad_act, expand_w[k], NT))
        copies = halo_send(2 + k, grad_depth)
        put_tall(name, hidden, cotangent)
        put_wide(name, normed, grad_act)
        begin(name)
        if k == 0:
            stage_second("A")
        pad_inner(2 + k, grad_depth)
        kernel_grad(k, grad_depth, k * KSIDE * KSIDE)
        halo_wait(2 + k, copies)
        cotangent = (cotangent.astype(F32) + convolve(2 + k, depth_k[k].astype(F32), True)).astype(BF16)
        if k == 0:
            stage_third("A")
        stage_first(name)

    parts = []
    for i in range(4):
        piece = normed_grid[i * CELLS : (i + 1) * CELLS]
        grad = dot(piece, cotangent, TN).astype(BF16)
        for h in range(2):
            s["Cgp"][h, i * 16 : (i + 1) * 16] = grad[:, h * 128 : (h + 1) * 128].reshape(16, 16, 128)
        parts.append(dot(cotangent, patch_w[i * CH : (i + 1) * CH, :], NT))
    grad_grid = normalise_grad(grid_hat, grid_scale, jnp.concatenate(parts, axis=0)).astype(BF16)
    grad_embed = dot(encoded, grad_grid).astype(BF16)
    grad_taps = s["kg"][...].astype(BF16)
    for h in range(2):
        at = slice(h * 128, (h + 1) * 128)
        s["Cgq"][h, 0:7] = grad_taps[:, at].reshape(7, 16, 128)
        s["Cgq"][h, 7:9] = grad_embed[:, at].reshape(2, 16, 128)
        s["Cgq"][h, 9:16] = jnp.zeros((7, 16, 128), BF16)
    begin("C")
    stage_gather("A")
    stage_second("B")
    stage_first("C")
    stage_back_second("A")
    stage_third("B")
    stage_second("C")
    stage_back_first("A")
    stage_gather("B")
    stage_third("C")
    stage_back_core("A")
    stage_back_second("B")
    stage_back_second("C")
    finish("A")
    stage_back_first("B")
    stage_back_first("C")
    stage_back_core("B")
    stage_back_core("C")
    finish("B")
    finish("C")
    for copy in sent:
        copy.wait_send()


def factor(lon):
    nx = math.isqrt(lon)
    while lon % nx:
        nx -= 1
    return nx, lon // nx


def on_device(values, coords, dest, count, embed_w, patch_w, depth_k, expand_w, reduce_w, cot):
    nx, ny = factor(lax.axis_size("lon"))
    nz = lax.axis_size("lat")
    p0, p1 = encode(nx, ny, nz, dest[0, 0, 0], count[0, 0, 0], values[0, 0, 0], coords[0, 0, 0])
    plan = scratch_plan(nx, ny, nz)
    copies = copy_count(nx, ny, nz)
    vmem = pl.BlockSpec(memory_space=pltpu.VMEM)
    outs = pl.pallas_call(
        functools.partial(net_kernel, nx, ny, nz, tuple(plan)),
        out_shape=(
            jax.ShapeDtypeStruct((CELLS, CH), BF16),
            jax.ShapeDtypeStruct((OBSF + 1, CH), F32),
            jax.ShapeDtypeStruct((4 * CH, CH), F32),
            jax.ShapeDtypeStruct((2, KSIDE * KSIDE, CH), F32),
            jax.ShapeDtypeStruct((2, CH, HID), F32),
            jax.ShapeDtypeStruct((2, HID, CH), F32),
        ),
        in_specs=[vmem] * 8,
        out_specs=(vmem,) * 6,
        scratch_shapes=list(plan.values())
        + [pltpu.SemaphoreType.DMA((copies,)), pltpu.SemaphoreType.DMA((copies,))],
        compiler_params=pltpu.CompilerParams(
            collective_id=0, has_side_effects=True, vmem_limit_bytes=56 * 2**20
        ),
    )(p0, p1, embed_w, patch_w, depth_k, expand_w, reduce_w, cot[0].reshape(CELLS, CH))
    return (outs[0].reshape(1, SIDE, SIDE, CH),) + tuple(outs[1:])


def solution(mesh):
    in_specs = (
        P("dp", "lon", "lat", None, None, None),
        P("dp", "lon", "lat", None, None, None),
        P("dp", "lon", "lat", None),
        P("dp", "lon", "lat", None),
        P(),
        P(),
        P(),
        P(),
        P(),
        P("dp", "lon", "lat", None),
    )
    out_specs = (P("dp", "lon", "lat", None), P(), P(), P(), P(), P())
    return jax.shard_map(
        on_device, mesh=mesh, in_specs=in_specs, out_specs=out_specs, check_vma=False
    )
```

```python
import functools
import math

import jax
import jax.numpy as jnp
from jax import lax
from jax.experimental import pallas as pl
from jax.experimental.pallas import tpu as pltpu
from jax.sharding import PartitionSpec as P

MESH = pl.DeviceIdType.MESH
F32 = jnp.float32
BF16 = jnp.bfloat16
OBSF = 16
KSIDE = 7
REACH = 3
TILE = 16
SIDE = 8
CELLS = 64
CH = 256
HID = 1024
INVERSE = 0.5 / (0.7 * 0.7)
PADW = 16
NT = (((1,), (1,)), ((), ()))
TN = (((0,), (0,)), ((), ()))


def dot(a, b, dims=(((1,), (0,)), ((), ()))):
    return lax.dot_general(a, b, dims, preferred_element_type=F32)


PARTS = 4


def in_hbm(array):
    return pltpu.with_memory_space_constraint(array, pltpu.HBM)


def encode_kernel(
    nx, ny, nz, dest_hbm, count_hbm, values_hbm, coords_hbm, p0_ref, p1_ref, dens_ref,
    dest_ref, count_ref, values_ref, coords_ref, sems,
):
    blocks = values_ref.shape[0]
    parts = PARTS if blocks % PARTS == 0 else 1
    share = blocks // parts
    small = [
        pltpu.make_async_copy(dest_hbm, dest_ref, sems.at[0]),
        pltpu.make_async_copy(count_hbm, count_ref, sems.at[1]),
    ]
    large = []
    for part in range(parts):
        at = pl.ds(part * share, share)
        large.append(
            (
                pltpu.make_async_copy(values_hbm.at[at], values_ref.at[at], sems.at[2 + 2 * part]),
                pltpu.make_async_copy(coords_hbm.at[at], coords_ref.at[at], sems.at[3 + 2 * part]),
            )
        )
    for copy in small:
        copy.start()
    for pair in large:
        for copy in pair:
            copy.start()
    p0_ref[...] = jnp.zeros_like(p0_ref)
    p1_ref[...] = jnp.zeros_like(p1_ref)
    dens_ref[...] = jnp.zeros_like(dens_ref)
    rows = values_ref.shape[2]
    order = lax.broadcasted_iota(jnp.int32, (TILE, rows), 0)
    cell = (2 * (order % SIDE) + order // SIDE).astype(F32)
    lane = lax.broadcasted_iota(jnp.int32, (TILE, rows), 1)
    ones = jnp.ones((OBSF, rows), BF16)

    def one_block(block, carry):
        tile = dest_ref[block]
        pair = coords_ref[block]
        a = jnp.exp(-jnp.square(pair[0:1, :] - cell) * INVERSE)
        a = jnp.where(lane < count_ref[block], a, 0.0)
        b = jnp.exp(-jnp.square(pair[1:2, :] - cell) * INVERSE)
        parts = []
        for i in range(2):
            for j in range(2):
                left = a[i * SIDE : (i + 1) * SIDE]
                right = b[j * SIDE : (j + 1) * SIDE]
                parts.append((left[:, None, :] * right[None]).reshape(CELLS, rows))
        weight = jnp.concatenate(parts, axis=0).astype(BF16)
        sums = dot(jnp.concatenate([values_ref[block], ones], axis=0), weight, NT)
        lon = tile // nz
        lat = tile % nz
        x = lon // ny
        y = lon % ny
        p0_ref[lon * (nz + 1) + lat] = sums[:OBSF, :128].astype(BF16)
        p1_ref[(y * nx + x) * nz + lat] = sums[:OBSF, 128:].astype(BF16)
        dens_ref[lon, pl.ds(lat, 1), :] = sums[OBSF : OBSF + 1, :128]
        dens_ref[lon, pl.ds(SIDE + lat, 1), :] = sums[OBSF : OBSF + 1, 128:]
        return carry

    for copy in small:
        copy.wait()
    for part in range(parts):
        for copy in large[part]:
            copy.wait()
        lax.fori_loop(part * share, (part + 1) * share, one_block, 0, unroll=min(share, 4))
    for lon in range(nx * ny):
        p0_ref[lon * (nz + 1) + nz] = dens_ref[lon].astype(BF16)


def encode(nx, ny, nz, dest, count, values, coords):
    lon = nx * ny
    return pl.pallas_call(
        functools.partial(encode_kernel, nx, ny, nz),
        out_shape=(
            jax.ShapeDtypeStruct((lon * (nz + 1), 16, 128), BF16),
            jax.ShapeDtypeStruct((lon * nz, 16, 128), BF16),
        ),
        in_specs=[pl.BlockSpec(memory_space=pltpu.HBM)] * 4,
        out_specs=(pl.BlockSpec(memory_space=pltpu.VMEM),) * 2,
        scratch_shapes=[
            pltpu.VMEM((lon, 16, 128), F32),
            pltpu.SMEM(dest.shape, jnp.int32),
            pltpu.SMEM(count.shape, jnp.int32),
            pltpu.VMEM(values.shape, values.dtype),
            pltpu.VMEM(coords.shape, coords.dtype),
            pltpu.SemaphoreType.DMA((2 + 2 * PARTS,)),
        ],
        compiler_params=pltpu.CompilerParams(vmem_limit_bytes=24 * 2**20),
    )(*(in_hbm(leaf) for leaf in (dest, count, values, coords)))


def normalise(field):
    center = jnp.mean(field, axis=-1, keepdims=True)
    shifted = field - center
    scale = lax.rsqrt(jnp.mean(jnp.square(shifted), axis=-1, keepdims=True) + 1e-05)
    return shifted * scale, scale


def normalise_grad(normed, scale, grad):
    return scale * (
        grad
        - jnp.mean(grad, axis=-1, keepdims=True)
        - normed * jnp.mean(grad * normed, axis=-1, keepdims=True)
    )


def cdf(field):
    return 0.5 * (1.0 + lax.erf(field * math.sqrt(0.5)))


def group_sizes(nx, ny, nz, np_half, nq_half):
    return np_half // (nx * ny), nq_half // (nx * ny)


def group_scratch(nx, ny, nz, n_p, n_q, scatter):
    up, uq = n_p // (nx * ny), n_q // (nx * ny)

    def units(*lead):
        return pltpu.VMEM(tuple(lead) + (16, 128), BF16)

    plan = {
        "gp": units(2, n_p), "gq": units(2, n_q),
        "cp": units(n_p), "cq": units(n_q),
        "sp": units(n_p), "sq": units(n_q),
        "l1p": units(nx - 1, n_p // nx), "l1q": units(ny - 1, n_q // ny),
        "s2p": units(n_p // nx), "s2q": units(n_q // ny),
        "l2p": units(ny - 1, up), "l2q": units(nx - 1, uq),
        "s3": units(up + uq),
    }
    if scatter:
        piece = (up + uq) // nz
        plan["l3"] = units(nz - 1, piece)
        plan["f3"] = units(nz, piece)
    else:
        plan["l3"] = units(nz, up + uq)
    return plan


GROUPS = (("A", 64, 64, True), ("B", 64, 64, True), ("C", 32, 48, False))


def scratch_plan(nx, ny, nz):
    def units(*lead):
        return pltpu.VMEM(tuple(lead) + (16, 128), BF16)

    plan = {
        "r0": units(nx - 1, ny * (nz + 1)), "r1": units(ny - 1, nx * nz),
        "q0": units(ny * (nz + 1)), "q1": units(nx * nz),
        "t0": units(ny - 1, nz + 1), "t1": units(nx - 1, nz),
        "zbuf": units(nz, 3), "zr": units(nz - 1, 3),
        "dens": pltpu.VMEM((16, 128), F32),
        "ew": pltpu.VMEM((32, CH), F32),
        "kg": pltpu.VMEM((2, 112, 128), F32),
        "tap": pltpu.VMEM((KSIDE * KSIDE, 8, CH), F32),
    }
    for k in range(4):
        plan["halo_src%d" % k] = pltpu.VMEM((2, CELLS, CH), BF16)
        plan["halo_dst%d" % k] = pltpu.VMEM((8, CELLS // 2, CH), BF16)
        plan["pad%d" % k] = pltpu.VMEM((2, 14 * PADW, 128), F32)
    plan["cols"] = pltpu.VMEM((CELLS, CH), F32)
    for name, n_p, n_q, scatter in GROUPS:
        for key, value in group_scratch(nx, ny, nz, n_p, n_q, scatter).items():
            plan[name + key] = value
    return plan


def copy_count(nx, ny, nz):
    total = 2 * (nx + ny - 2) + (nz - 1) + 4 * 8
    for _, _, _, scatter in GROUPS:
        total += 2 * 2 + 4 * (nx + ny - 2) + (nz - 1) * (2 if scatter else 1)
    return total


FINALS = ("Afp", "Afq", "Bfp", "Bfq", "Cfp", "Cfq")
HALOS = tuple((i, j) for i in (-1, 0, 1) for j in (-1, 0, 1) if (i, j) != (0, 0))


def net_kernel(nx, ny, nz, names, *refs):
    p0, p1 = refs[:2]
    feat = refs[8]
    s = dict(zip(FINALS, refs[9:15]))
    s.update(zip(names, refs[15:]))
    local = refs[15 + len(names) : 21 + len(names)]
    embed_w, patch_w, depth_k, expand_w, reduce_w, cot = local
    send_sem, recv_sem, load_sem = refs[21 + len(names) :]
    loads = [
        pltpu.make_async_copy(far, near, load_sem.at[i]) for i, (far, near) in enumerate(zip(refs[2:8], local))
    ]
    core = lax.axis_index("dp")
    lon = lax.axis_index("lon")
    z = lax.axis_index("lat")
    x = lon // ny
    y = lon % ny
    nlon = nx * ny

    def at_core():
        return (1 - core, lon, z)

    def at_x(d):
        return (core, ((x + d) % nx) * ny + y, z)

    def at_y(d):
        return (core, x * ny + (y + d) % ny, z)

    def at_z(d):
        return (core, lon, (z + d) % nz)

    def at_halo(i, j):
        return (core, (lon + i + nlon) % nlon, (z + j + nz) % nz)

    barrier = pltpu.get_barrier_semaphore()
    peers = [at_core()] + [at_x(d) for d in range(1, nx)] + [at_y(d) for d in range(1, ny)]
    peers += [at_z(d) for d in range(1, nz)] + [at_halo(i, j) for i, j in HALOS]
    for peer in peers:
        pl.semaphore_signal(barrier, inc=1, device_id=peer, device_id_type=MESH)
    pl.semaphore_wait(barrier, len(peers))

    sent = []

    def push(src, dst, device, land=None):
        index = len(sent)

        def make(target):
            return pltpu.make_async_remote_copy(
                src_ref=src, dst_ref=target, send_sem=send_sem.at[index], recv_sem=recv_sem.at[index],
                device_id=device, device_id_type=MESH,
            )

        copy = make(dst)
        copy.start()
        sent.append(copy)
        return copy if land is None else make(land)

    def settle(copies):
        for copy in copies:
            copy.wait_recv()

    def spread(src, land, size, count, target):
        position = {"x": x, "y": y}[target]
        where = {"x": at_x, "y": at_y}[target]
        return [
            push(src.at[pl.ds(((position + d) % count) * size, size)], land.at[d - 1], where(d))
            for d in range(1, count)
        ]

    def fold(out, first, land, count, offset, size, step):
        for i in range(0, size, step):
            total = first[pl.ds(offset + i, step)].astype(F32)
            for d in range(count - 1):
                total = total + land[d, i : i + step].astype(F32)
            out[i : i + step] = total.astype(BF16)

    w0, w1 = nz + 1, nz
    copies = spread(p0, s["r0"], ny * w0, nx, "x") + spread(p1, s["r1"], nx * w1, ny, "y")
    for load in loads:
        load.start()
    s["ew"][...] = jnp.zeros_like(s["ew"])
    for load in loads:
        load.wait()
    s["ew"][0 : OBSF + 1, :] = embed_w[...].astype(F32)
    s["kg"][...] = jnp.zeros_like(s["kg"])
    embed_m = s["ew"][...].astype(BF16)
    settle(copies)
    fold(s["q0"], p0, s["r0"], nx, x * (ny * w0), ny * w0, w0)
    fold(s["q1"], p1, s["r1"], ny, y * (nx * w1), nx * w1, w1)
    copies = spread(s["q0"], s["t0"], w0, ny, "y") + spread(s["q1"], s["t1"], w1, nx, "x")
    settle(copies)
    total0 = s["q0"][pl.ds(y * w0, w0)].astype(F32)
    for d in range(ny - 1):
        total0 = total0 + s["t0"][d].astype(F32)
    total0 = total0.astype(BF16)
    total1 = s["q1"][pl.ds(x * w1, w1)].astype(F32)
    for d in range(nx - 1):
        total1 = total1 + s["t1"][d].astype(F32)
    total1 = total1.astype(BF16)
    for k in range(nz):
        s["zbuf"][k, 0] = total0[k]
        s["zbuf"][k, 1] = total1[k]
        s["zbuf"][k, 2] = total0[nz]
    copies = [push(s["zbuf"].at[(z + d) % nz], s["zr"].at[d - 1], at_z(d)) for d in range(1, nz)]
    settle(copies)
    sums = s["zbuf"][z].astype(F32)
    for d in range(nz - 1):
        sums = sums + s["zr"][d].astype(F32)
    s["dens"][...] = sums[2]
    density = jnp.concatenate([s["dens"][pl.ds(z, 1), :], s["dens"][pl.ds(SIDE + z, 1), :]], axis=1)
    scaled = jnp.concatenate([sums[0], sums[1]], axis=1) * lax.rsqrt(1.0 + density)
    level = jnp.where(
        lax.broadcasted_iota(jnp.int32, (16, CH), 0) == 0,
        jnp.broadcast_to(0.25 * jnp.log(1.0 + density), (16, CH)), 0.0,
    )
    encoded = jnp.concatenate([scaled, level], axis=0).astype(BF16)

    grid_hat, grid_scale = normalise(dot(encoded, embed_m, TN))
    normed_grid = grid_hat.astype(BF16)
    first = jnp.zeros((CELLS, CH), F32)
    for i in range(4):
        first = first + dot(normed_grid[i * CELLS : (i + 1) * CELLS], patch_w[i * CH : (i + 1) * CH, :])
    state = first.astype(BF16)

    def halo_send(which, field):
        src, dst = s["halo_src%d" % which], s["halo_dst%d" % which]
        src[0] = field.astype(BF16)
        src[1] = jnp.swapaxes(field.reshape(SIDE, SIDE, CH), 0, 1).reshape(CELLS, CH).astype(BF16)
        found = []
        for index, (i, j) in enumerate(HALOS):
            if j == 0:
                piece = src.at[0, pl.ds(32 if i > 0 else 0, 32)]
            else:
                piece = src.at[1, pl.ds(32 if j > 0 else 0, 32)]
            found.append(push(piece, dst.at[index], at_halo(i, j)))
        return found

    def pad_inner(which, field):
        pad = s["pad%d" % which]
        pad[...] = jnp.zeros_like(pad)
        for p in range(SIDE):
            for h in range(2):
                pad[h, pl.ds((REACH + p) * PADW + REACH, SIDE), :] = field[
                    p * SIDE : (p + 1) * SIDE, h * 128 : (h + 1) * 128
                ]

    def halo_wait(which, copies):
        pad, dst = s["pad%d" % which], s["halo_dst%d" % which]
        settle(copies)
        for index, (i, j) in enumerate(HALOS):
            if j == 0:
                for r in range(REACH):
                    if i > 0:
                        row, at = r, 1 + r
                    else:
                        row, at = REACH + SIDE + r, r
                    strip = dst[index].astype(F32)[at * SIDE : (at + 1) * SIDE]
                    for h in range(2):
                        pad[h, pl.ds(row * PADW + REACH, SIDE), :] = strip[:, h * 128 : (h + 1) * 128]
                continue
            inside = (z > 0) if j > 0 else (z < nz - 1)
            keep = jnp.where(inside, 1.0, 0.0).astype(F32)
            block = dst[index].astype(F32) * keep
            for r in range(REACH):
                if j > 0:
                    column, at = r, 1 + r
                else:
                    column, at = REACH + SIDE + r, r
                strip = block[at * SIDE : (at + 1) * SIDE]
                if i == 0:
                    top, strip = REACH, strip
                elif i > 0:
                    top, strip = 0, strip[SIDE - REACH :]
                else:
                    top, strip = REACH + SIDE, strip[:REACH]
                for h in range(2):
                    pad[h, pl.ds(top * PADW + column, strip.shape[0], PADW), :] = strip[:, h * 128 : (h + 1) * 128]

    def window(which, column):
        pad = s["pad%d" % which]
        return jnp.stack(
            [
                jnp.concatenate([pad[h, pl.ds(p * PADW + column, SIDE), :] for h in range(2)], axis=1)
                for p in range(14)
            ],
            axis=0,
        )

    def taps_of(k):
        return [depth_k[tap].astype(F32)[k : k + 1].reshape(1, 1, CH) for tap in range(KSIDE * KSIDE)]

    def convolve(which, kernel, flip):
        total = jnp.zeros((SIDE, SIDE, CH), F32)
        for b in range(KSIDE):
            part = window(which, b)
            for a in range(KSIDE):
                tap = KSIDE * a + b
                if flip:
                    tap = KSIDE * KSIDE - 1 - tap
                total = total + part[a : a + SIDE] * kernel[tap]
        return total.reshape(CELLS, CH)

    def kernel_grad(which, grad):
        grad = grad.reshape(SIDE, SIDE, CH)
        for b in range(KSIDE):
            part = window(which, b)
            for a in range(KSIDE):
                s["tap"][KSIDE * a + b] = jnp.sum(part[a : a + SIDE] * grad, axis=0)
        taps = jnp.sum(s["tap"][...], axis=1)
        for h in range(2):
            s["kg"][h, pl.ds(which, KSIDE * KSIDE, 2), :] = taps[:, h * 128 : (h + 1) * 128]

    stored = []
    for k in range(2):
        field = state.astype(F32)
        copies = halo_send(k, field)
        pad_inner(k, field)
        kernel = taps_of(k)
        halo_wait(k, copies)
        hat, scale = normalise(convolve(k, kernel, False))
        normed = hat.astype(BF16)
        act = dot(normed, expand_w[k])
        share = cdf(act)
        hidden = (act * share).astype(BF16)
        state = (field + dot(hidden, reduce_w[k])).astype(BF16)
        slope = share + act * jnp.exp(-0.5 * jnp.square(act)) * (1.0 / math.sqrt(2.0 * math.pi))
        stored.append((hat, scale, normed, hidden, slope))
    feat[...] = state

    progress = {}

    def group(name):
        return next(entry for entry in GROUPS if entry[0] == name)

    def begin(name):
        gp, gq = s[name + "gp"], s[name + "gq"]
        progress[name] = [
            push(gp.at[1 - core], s[name + "cp"], at_core()),
            push(gq.at[1 - core], s[name + "cq"], at_core()),
        ]

    def stage_first(name):
        _, n_p, n_q, _ = group(name)
        settle(progress[name])
        for key, n in (("p", n_p), ("q", n_q)):
            own, got, out = s[name + "g" + key], s[name + "c" + key], s[name + "s" + key]

            def body(i, carry, own=own, got=got, out=out):
                at = pl.ds(pl.multiple_of(i * 8, 8), 8)
                out[at] = (own[core, at].astype(F32) + got[at].astype(F32)).astype(BF16)
                return carry

            lax.fori_loop(0, n // 8, body, 0)
        progress[name] = spread(s[name + "sp"], s[name + "l1p"], n_p // nx, nx, "x") + spread(
            s[name + "sq"], s[name + "l1q"], n_q // ny, ny, "y"
        )

    def stage_second(name):
        _, n_p, n_q, _ = group(name)
        settle(progress[name])
        fold(s[name + "s2p"], s[name + "sp"], s[name + "l1p"], nx, x * (n_p // nx), n_p // nx, math.gcd(8, n_p // nx))
        fold(s[name + "s2q"], s[name + "sq"], s[name + "l1q"], ny, y * (n_q // ny), n_q // ny, math.gcd(8, n_q // ny))
        progress[name] = spread(s[name + "s2p"], s[name + "l2p"], n_p // nlon, ny, "y") + spread(
            s[name + "s2q"], s[name + "l2q"], n_q // nlon, nx, "x"
        )

    def stage_third(name):
        _, n_p, n_q, scatter = group(name)
        up, uq = n_p // nlon, n_q // nlon
        settle(progress[name])
        s3 = s[name + "s3"]
        fold(s3.at[pl.ds(0, up)], s[name + "s2p"], s[name + "l2p"], ny, y * up, up, math.gcd(8, up))
        fold(s3.at[pl.ds(up, uq)], s[name + "s2q"], s[name + "l2q"], nx, x * uq, uq, math.gcd(8, uq))
        l3 = s[name + "l3"]
        if scatter:
            piece = (up + uq) // nz
            progress[name] = [
                push(s3.at[pl.ds(((z + d) % nz) * piece, piece)], l3.at[d - 1], at_z(d)) for d in range(1, nz)
            ]
        else:
            l3[z] = s3[...]
            progress[name] = [push(s3, l3.at[z], at_z(d), l3.at[(z + nz - d) % nz]) for d in range(1, nz)]

    def stage_gather(name):
        _, n_p, n_q, _ = group(name)
        piece = (n_p + n_q) // (nlon * nz)
        settle(progress[name])
        s3, l3, f3 = s[name + "s3"], s[name + "l3"], s[name + "f3"]
        total = s3[pl.ds(z * piece, piece)].astype(F32)
        for d in range(nz - 1):
            total = total + l3[d].astype(F32)
        f3[z] = total.astype(BF16)
        progress[name] = [push(f3.at[z], f3.at[z], at_z(d), f3.at[(z + nz - d) % nz]) for d in range(1, nz)]

    def stage_back_second(name):
        _, n_p, n_q, scatter = group(name)
        up, uq = n_p // nlon, n_q // nlon
        settle(progress[name])
        fp, fq = s[name + "fp"], s[name + "fq"]
        at_p, at_q = x * (n_p // nx) + y * up, y * (n_q // ny) + x * uq
        if scatter:
            done = s[name + "f3"][...].reshape(up + uq, 16, 128)
        else:
            total = s[name + "l3"][0].astype(F32)
            for d in range(1, nz):
                total = total + s[name + "l3"][d].astype(F32)
            done = total.astype(BF16)
        fp[core, pl.ds(at_p, up)] = done[:up]
        fq[core, pl.ds(at_q, uq)] = done[up:]

        def from_p(d):
            return fp.at[core, pl.ds(x * (n_p // nx) + ((y + ny - d) % ny) * up, up)]

        def from_q(d):
            return fq.at[core, pl.ds(y * (n_q // ny) + ((x + nx - d) % nx) * uq, uq)]

        progress[name] = [push(from_p(0), from_p(0), at_y(d), from_p(d)) for d in range(1, ny)]
        progress[name] += [push(from_q(0), from_q(0), at_x(d), from_q(d)) for d in range(1, nx)]

    def stage_back_first(name):
        _, n_p, n_q, _ = group(name)
        settle(progress[name])
        fp, fq = s[name + "fp"], s[name + "fq"]
        hp, hq = n_p // nx, n_q // ny

        def from_p(d):
            return fp.at[core, pl.ds(((x + nx - d) % nx) * hp, hp)]

        def from_q(d):
            return fq.at[core, pl.ds(((y + ny - d) % ny) * hq, hq)]

        progress[name] = [push(from_p(0), from_p(0), at_x(d), from_p(d)) for d in range(1, nx)]
        progress[name] += [push(from_q(0), from_q(0), at_y(d), from_q(d)) for d in range(1, ny)]

    def stage_back_core(name):
        settle(progress[name])
        fp, fq = s[name + "fp"], s[name + "fq"]
        progress[name] = [
            push(fp.at[core], fp.at[core], at_core(), fp.at[1 - core]),
            push(fq.at[core], fq.at[core], at_core(), fq.at[1 - core]),
        ]

    def put_tall(name, left, right):
        for h in range(2):
            s[name + "gp"][h] = dot(left, right[:, h * 128 : (h + 1) * 128], TN).astype(BF16).reshape(64, 16, 128)

    def put_wide(name, left, right):
        for lane in range(8):
            part = dot(left, right[:, lane * 128 : (lane + 1) * 128], TN).astype(BF16)
            s[name + "gq"][lane // 4, (lane % 4) * 16 : (lane % 4 + 1) * 16] = part.reshape(16, 16, 128)

    cotangent = cot[...]
    for k in (1, 0):
        name = "A" if k == 1 else "B"
        hat, scale, normed, hidden, slope = stored[k]
        grad_act = (dot(cotangent, reduce_w[k], NT) * slope).astype(BF16)
        grad_depth = normalise_grad(hat, scale, dot(grad_act, expand_w[k], NT))
        copies = halo_send(2 + k, grad_depth)
        put_tall(name, hidden, cotangent)
        put_wide(name, normed, grad_act)
        begin(name)
        pad_inner(2 + k, grad_depth)
        kernel_grad(k, grad_depth)
        if k == 0:
            stage_second("A")
        stage_first(name)
        halo_wait(2 + k, copies)
        cotangent = (cotangent.astype(F32) + convolve(2 + k, taps_of(k), True)).astype(BF16)

    parts = []
    for i in range(4):
        piece = normed_grid[i * CELLS : (i + 1) * CELLS]
        grad = dot(piece, cotangent, TN).astype(BF16)
        for h in range(2):
            target = s["Cgp"] if i < 2 else s["Cgq"]
            target[h, (i % 2) * 16 : (i % 2 + 1) * 16] = grad[:, h * 128 : (h + 1) * 128].reshape(16, 16, 128)
        parts.append(dot(cotangent, patch_w[i * CH : (i + 1) * CH, :], NT))
    grad_grid = normalise_grad(grid_hat, grid_scale, jnp.concatenate(parts, axis=0)).astype(BF16)
    grad_embed = dot(encoded, grad_grid).astype(BF16)
    for h in range(2):
        s["Cgq"][h, 32:39] = s["kg"][h].astype(BF16).reshape(7, 16, 128)
        s["Cgq"][h, 39:41] = grad_embed[:, h * 128 : (h + 1) * 128].reshape(2, 16, 128)
        s["Cgq"][h, 41:48] = jnp.zeros((7, 16, 128), BF16)
    begin("C")
    stage_third("A")
    stage_first("C")
    stage_second("B")
    stage_gather("A")
    stage_second("C")
    stage_third("B")
    stage_back_second("A")
    stage_third("C")
    stage_gather("B")
    stage_back_first("A")
    stage_back_second("B")
    stage_back_second("C")
    stage_back_core("A")
    stage_back_first("B")
    stage_back_first("C")
    stage_back_core("C")
    stage_back_core("B")
    for name in ("A", "C", "B"):
        settle(progress[name])
    for copy in sent:
        copy.wait_send()


def widen_kernel(feat, afp, afq, bfp, bfq, cfp, cfq, *refs):
    outs, stage, rows, sems = refs[:6], refs[6:12], refs[12], refs[13]
    s_feat, s_embed, s_patch, s_kernel, s_expand, s_reduce = stage
    s_feat[...] = feat[...]
    pending = []

    def ship(src, dst):
        copy = pltpu.make_async_copy(src, dst, sems.at[len(pending)])
        copy.start()
        pending.append(copy)

    def block(units):
        return units.astype(F32).reshape(units.shape[0] * 16, 128)

    ship(s_feat, outs[0])
    for k, fp, fq in ((1, afp, afq), (0, bfp, bfq)):
        for r in range(0, 64, 16):
            for h in range(2):
                s_reduce[k, r * 16 : (r + 16) * 16, h * 128 : (h + 1) * 128] = block(fp[h, r : r + 16])
        ship(s_reduce.at[k], outs[5].at[k])
        for lane in range(8):
            s_expand[k, :, lane * 128 : (lane + 1) * 128] = block(fq[lane // 4, (lane % 4) * 16 : (lane % 4 + 1) * 16])
        ship(s_expand.at[k], outs[4].at[k])
    for source, base in ((cfp, 0), (cfq, 512)):
        for r in range(0, 32, 16):
            for h in range(2):
                at = slice(base + r * 16, base + (r + 16) * 16)
                s_patch[at, h * 128 : (h + 1) * 128] = block(source[h, r : r + 16])
    ship(s_patch, outs[2])
    for h in range(2):
        at = slice(h * 128, (h + 1) * 128)
        rows[...] = block(cfq[h, 32:39])
        for tap in range(KSIDE * KSIDE):
            s_kernel[tap, :, at] = rows[2 * tap : 2 * tap + 2, :]
        s_embed[:, at] = block(cfq[h, 39:41])[: OBSF + 1]
    ship(s_kernel, outs[3])
    ship(s_embed, outs[1])
    for copy in pending:
        copy.wait()


def factor(lon):
    nx = math.isqrt(lon)
    while lon % nx:
        nx -= 1
    return nx, lon // nx


def on_device(values, coords, dest, count, embed_w, patch_w, depth_k, expand_w, reduce_w, cot):
    nx, ny = factor(lax.axis_size("lon"))
    nz = lax.axis_size("lat")
    p0, p1 = encode(nx, ny, nz, dest[0, 0, 0], count[0, 0, 0], values[0, 0, 0], coords[0, 0, 0])
    plan = scratch_plan(nx, ny, nz)
    copies = copy_count(nx, ny, nz)
    vmem = pl.BlockSpec(memory_space=pltpu.VMEM)
    operands = (embed_w, patch_w, jnp.transpose(depth_k, (1, 0, 2)), expand_w, reduce_w, cot[0].reshape(CELLS, CH))
    finals = []
    for _, n_p, n_q, _ in GROUPS:
        finals += [jax.ShapeDtypeStruct((2, n, 16, 128), BF16) for n in (n_p, n_q)]
    handed = pl.pallas_call(
        functools.partial(net_kernel, nx, ny, nz, tuple(plan)),
        out_shape=(jax.ShapeDtypeStruct((CELLS, CH), BF16),) + tuple(finals),
        in_specs=[vmem] * 2 + [pl.BlockSpec(memory_space=pltpu.HBM)] * 6,
        out_specs=(vmem,) * 7,
        scratch_shapes=list(plan.values())
        + [pltpu.VMEM(leaf.shape, leaf.dtype) for leaf in operands]
        + [pltpu.SemaphoreType.DMA((n,)) for n in (copies, copies, len(operands))],
        compiler_params=pltpu.CompilerParams(
            collective_id=0, has_side_effects=True, vmem_limit_bytes=32 * 2**20
        ),
    )(p0, p1, *(in_hbm(leaf) for leaf in operands))
    shapes = (
        jax.ShapeDtypeStruct((CELLS, CH), BF16),
        jax.ShapeDtypeStruct((OBSF + 1, CH), F32),
        jax.ShapeDtypeStruct((4 * CH, CH), F32),
        jax.ShapeDtypeStruct((KSIDE * KSIDE, 2, CH), F32),
        jax.ShapeDtypeStruct((2, CH, HID), F32),
        jax.ShapeDtypeStruct((2, HID, CH), F32),
    )
    outs = pl.pallas_call(
        widen_kernel,
        out_shape=shapes,
        in_specs=[vmem] * 7,
        out_specs=(pl.BlockSpec(memory_space=pltpu.HBM),) * 6,
        scratch_shapes=[pltpu.VMEM(leaf.shape, leaf.dtype) for leaf in shapes]
        + [pltpu.VMEM((112, 128), F32), pltpu.SemaphoreType.DMA((8,))],
        compiler_params=pltpu.CompilerParams(vmem_limit_bytes=24 * 2**20),
    )(*handed)
    return (
        outs[0].reshape(1, SIDE, SIDE, CH), outs[1], outs[2], jnp.transpose(outs[3], (1, 0, 2)), outs[4], outs[5],
    )


def solution(mesh):
    in_specs = (
        P("dp", "lon", "lat", None, None, None),
        P("dp", "lon", "lat", None, None, None),
        P("dp", "lon", "lat", None),
        P("dp", "lon", "lat", None),
        P(),
        P(),
        P(),
        P(),
        P(),
        P("dp", "lon", "lat", None),
    )
    out_specs = (P("dp", "lon", "lat", None), P(), P(), P(), P(), P())
    return jax.shard_map(
        on_device, mesh=mesh, in_specs=in_specs, out_specs=out_specs, check_vma=False
    )
```

```python
import functools
import math

import jax
import jax.numpy as jnp
from jax import lax
from jax.experimental import pallas as pl
from jax.experimental.pallas import tpu as pltpu
from jax.sharding import PartitionSpec as P

MESH = pl.DeviceIdType.MESH
F32 = jnp.float32
BF16 = jnp.bfloat16
OBSF = 16
KSIDE = 7
REACH = 3
TILE = 16
SIDE = 8
CELLS = 64
CH = 256
HID = 1024
INVERSE = 0.5 / (0.7 * 0.7)
PADW = 16
NT = (((1,), (1,)), ((), ()))
TN = (((0,), (0,)), ((), ()))


def dot(a, b, dims=(((1,), (0,)), ((), ()))):
    return lax.dot_general(a, b, dims, preferred_element_type=F32)


PARTS = 4


def in_hbm(array):
    return pltpu.with_memory_space_constraint(array, pltpu.HBM)


def encode_kernel(
    nx, ny, nz, dest_hbm, count_hbm, values_hbm, coords_hbm, p0_ref, p1_ref, dens_ref,
    dest_ref, count_ref, values_ref, coords_ref, sems,
):
    blocks = values_ref.shape[0]
    parts = PARTS if blocks % PARTS == 0 else 1
    share = blocks // parts
    small = [
        pltpu.make_async_copy(dest_hbm, dest_ref, sems.at[0]),
        pltpu.make_async_copy(count_hbm, count_ref, sems.at[1]),
    ]
    large = []
    for part in range(parts):
        at = pl.ds(part * share, share)
        large.append(
            (
                pltpu.make_async_copy(values_hbm.at[at], values_ref.at[at], sems.at[2 + 2 * part]),
                pltpu.make_async_copy(coords_hbm.at[at], coords_ref.at[at], sems.at[3 + 2 * part]),
            )
        )
    for copy in small:
        copy.start()
    for pair in large:
        for copy in pair:
            copy.start()
    p0_ref[...] = jnp.zeros_like(p0_ref)
    p1_ref[...] = jnp.zeros_like(p1_ref)
    dens_ref[...] = jnp.zeros_like(dens_ref)
    rows = values_ref.shape[2]
    order = lax.broadcasted_iota(jnp.int32, (TILE, rows), 0)
    cell = (2 * (order % SIDE) + order // SIDE).astype(F32)
    lane = lax.broadcasted_iota(jnp.int32, (TILE, rows), 1)
    ones = jnp.ones((OBSF, rows), BF16)

    def one_block(block, carry):
        tile = dest_ref[block]
        pair = coords_ref[block]
        a = jnp.exp(-jnp.square(pair[0:1, :] - cell) * INVERSE)
        a = jnp.where(lane < count_ref[block], a, 0.0)
        b = jnp.exp(-jnp.square(pair[1:2, :] - cell) * INVERSE)
        parts = []
        for i in range(2):
            for j in range(2):
                left = a[i * SIDE : (i + 1) * SIDE]
                right = b[j * SIDE : (j + 1) * SIDE].astype(BF16)
                right = jnp.concatenate([right, right], axis=0)
                for p in range(0, SIDE, 2):
                    pair_of = [jnp.broadcast_to(left[p + n : p + n + 1], (SIDE, rows)) for n in range(2)]
                    parts.append(jnp.concatenate(pair_of, axis=0).astype(BF16) * right)
        weight = jnp.concatenate(parts, axis=0)
        sums = dot(jnp.concatenate([values_ref[block], ones], axis=0), weight, NT)
        lon = tile // nz
        lat = tile % nz
        x = lon // ny
        y = lon % ny
        p0_ref[lon * (nz + 1) + lat] = sums[:OBSF, :128].astype(BF16)
        p1_ref[(y * nx + x) * nz + lat] = sums[:OBSF, 128:].astype(BF16)
        dens_ref[lon, pl.ds(lat, 1), :] = sums[OBSF : OBSF + 1, :128]
        dens_ref[lon, pl.ds(SIDE + lat, 1), :] = sums[OBSF : OBSF + 1, 128:]
        return carry

    for copy in small:
        copy.wait()
    for part in range(parts):
        for copy in large[part]:
            copy.wait()
        lax.fori_loop(part * share, (part + 1) * share, one_block, 0, unroll=share)
    for lon in range(nx * ny):
        p0_ref[lon * (nz + 1) + nz] = dens_ref[lon].astype(BF16)


def encode(nx, ny, nz, dest, count, values, coords):
    lon = nx * ny
    return pl.pallas_call(
        functools.partial(encode_kernel, nx, ny, nz),
        out_shape=(
            jax.ShapeDtypeStruct((lon * (nz + 1), 16, 128), BF16),
            jax.ShapeDtypeStruct((lon * nz, 16, 128), BF16),
        ),
        in_specs=[pl.BlockSpec(memory_space=pltpu.HBM)] * 4,
        out_specs=(pl.BlockSpec(memory_space=pltpu.VMEM),) * 2,
        scratch_shapes=[
            pltpu.VMEM((lon, 16, 128), F32),
            pltpu.SMEM(dest.shape, jnp.int32),
            pltpu.SMEM(count.shape, jnp.int32),
            pltpu.VMEM(values.shape, values.dtype),
            pltpu.VMEM(coords.shape, coords.dtype),
            pltpu.SemaphoreType.DMA((2 + 2 * PARTS,)),
        ],
        compiler_params=pltpu.CompilerParams(vmem_limit_bytes=24 * 2**20),
    )(*(in_hbm(leaf) for leaf in (dest, count, values, coords)))


def normalise(field):
    center = jnp.mean(field, axis=-1, keepdims=True)
    shifted = field - center
    scale = lax.rsqrt(jnp.mean(jnp.square(shifted), axis=-1, keepdims=True) + 1e-05)
    return shifted * scale, scale


def normalise_grad(normed, scale, grad):
    return scale * (
        grad
        - jnp.mean(grad, axis=-1, keepdims=True)
        - normed * jnp.mean(grad * normed, axis=-1, keepdims=True)
    )


def cdf(field):
    return 0.5 * (1.0 + lax.erf(field * math.sqrt(0.5)))


def group_sizes(nx, ny, nz, np_half, nq_half):
    return np_half // (nx * ny), nq_half // (nx * ny)


def group_scratch(nx, ny, nz, n_p, n_q, scatter):
    up, uq = n_p // (nx * ny), n_q // (nx * ny)

    def units(*lead):
        return pltpu.VMEM(tuple(lead) + (16, 128), BF16)

    plan = {
        "gp": units(2, n_p), "gq": units(2, n_q),
        "cp": units(n_p), "cq": units(n_q),
        "sp": units(n_p), "sq": units(n_q),
        "l1p": units(nx - 1, n_p // nx), "l1q": units(ny - 1, n_q // ny),
        "s2p": units(n_p // nx), "s2q": units(n_q // ny),
        "l2p": units(ny - 1, up), "l2q": units(nx - 1, uq),
        "s3": units(up + uq),
    }
    if scatter:
        piece = (up + uq) // nz
        plan["l3"] = units(nz - 1, piece)
        plan["f3"] = units(nz, piece)
    else:
        plan["l3"] = units(nz, up + uq)
    return plan


GROUPS = (("A", 64, 64, True), ("B", 64, 64, True), ("C", 32, 48, False))


def scratch_plan(nx, ny, nz):
    def units(*lead):
        return pltpu.VMEM(tuple(lead) + (16, 128), BF16)

    plan = {
        "r0": units(nx - 1, ny * (nz + 1)), "r1": units(ny - 1, nx * nz),
        "q0": units(ny * (nz + 1)), "q1": units(nx * nz),
        "t0": units(ny - 1, nz + 1), "t1": units(nx - 1, nz),
        "zbuf": units(nz, 3), "zr": units(nz - 1, 3),
        "dens": pltpu.VMEM((16, 128), F32),
        "ew": pltpu.VMEM((32, CH), F32),
        "kg": pltpu.VMEM((2, 112, 128), F32),
        "tap": pltpu.VMEM((KSIDE * KSIDE, 8, CH), F32),
    }
    for k in range(4):
        plan["halo_src%d" % k] = pltpu.VMEM((2, CELLS, CH), BF16)
        plan["halo_dst%d" % k] = pltpu.VMEM((8, CELLS // 2, CH), BF16)
        plan["pad%d" % k] = pltpu.VMEM((2, 14 * PADW, 128), F32)
    plan["cols"] = pltpu.VMEM((CELLS, CH), F32)
    for name, n_p, n_q, scatter in GROUPS:
        for key, value in group_scratch(nx, ny, nz, n_p, n_q, scatter).items():
            plan[name + key] = value
    return plan


def copy_count(nx, ny, nz):
    total = 2 * (nx + ny - 2) + (nz - 1) + 4 * 8
    for _, _, _, scatter in GROUPS:
        total += 2 * (nx + ny) + 4 * (nx + ny - 2) + (nz - 1) * (2 if scatter else 1)
    return total


FINALS = ("Afp", "Afq", "Bfp", "Bfq", "Cfp", "Cfq")
HALOS = tuple((i, j) for i in (-1, 0, 1) for j in (-1, 0, 1) if (i, j) != (0, 0))


def net_kernel(nx, ny, nz, names, *refs):
    p0, p1 = refs[:2]
    feat = refs[8]
    s = dict(zip(FINALS, refs[9:15]))
    s.update(zip(names, refs[15:]))
    local = refs[15 + len(names) : 21 + len(names)]
    embed_w, patch_w, depth_k, expand_w, reduce_w, cot = local
    send_sem, recv_sem, load_sem = refs[21 + len(names) :]
    loads = [
        pltpu.make_async_copy(far, near, load_sem.at[i]) for i, (far, near) in enumerate(zip(refs[2:8], local))
    ]
    core = lax.axis_index("dp")
    lon = lax.axis_index("lon")
    z = lax.axis_index("lat")
    x = lon // ny
    y = lon % ny
    nlon = nx * ny

    def at_core():
        return (1 - core, lon, z)

    def at_x(d):
        return (core, ((x + d) % nx) * ny + y, z)

    def at_y(d):
        return (core, x * ny + (y + d) % ny, z)

    def at_z(d):
        return (core, lon, (z + d) % nz)

    def at_halo(i, j):
        return (core, (lon + i + nlon) % nlon, (z + j + nz) % nz)

    barrier = pltpu.get_barrier_semaphore()
    peers = [at_core()] + [at_x(d) for d in range(1, nx)] + [at_y(d) for d in range(1, ny)]
    peers += [at_z(d) for d in range(1, nz)] + [at_halo(i, j) for i, j in HALOS]
    for peer in peers:
        pl.semaphore_signal(barrier, inc=1, device_id=peer, device_id_type=MESH)
    pl.semaphore_wait(barrier, len(peers))

    sent = []

    def push(src, dst, device, land=None):
        index = len(sent)

        def make(target):
            return pltpu.make_async_remote_copy(
                src_ref=src, dst_ref=target, send_sem=send_sem.at[index], recv_sem=recv_sem.at[index],
                device_id=device, device_id_type=MESH,
            )

        copy = make(dst)
        copy.start()
        sent.append(copy)
        return copy if land is None else make(land)

    def settle(copies):
        for copy in copies:
            copy.wait_recv()

    def spread(src, land, size, count, target):
        position = {"x": x, "y": y}[target]
        where = {"x": at_x, "y": at_y}[target]
        return [
            push(src.at[pl.ds(((position + d) % count) * size, size)], land.at[d - 1], where(d))
            for d in range(1, count)
        ]

    def fold(out, first, land, count, offset, size, step):
        for i in range(0, size, step):
            total = first[pl.ds(offset + i, step)].astype(F32)
            for d in range(count - 1):
                total = total + land[d, i : i + step].astype(F32)
            out[i : i + step] = total.astype(BF16)

    w0, w1 = nz + 1, nz
    copies = spread(p0, s["r0"], ny * w0, nx, "x") + spread(p1, s["r1"], nx * w1, ny, "y")
    for load in loads:
        load.start()
    s["ew"][...] = jnp.zeros_like(s["ew"])
    for load in loads:
        load.wait()
    s["ew"][0 : OBSF + 1, :] = embed_w[...].astype(F32)
    s["kg"][...] = jnp.zeros_like(s["kg"])
    embed_m = s["ew"][...].astype(BF16)
    settle(copies)
    fold(s["q0"], p0, s["r0"], nx, x * (ny * w0), ny * w0, w0)
    fold(s["q1"], p1, s["r1"], ny, y * (nx * w1), nx * w1, w1)
    copies = spread(s["q0"], s["t0"], w0, ny, "y") + spread(s["q1"], s["t1"], w1, nx, "x")
    settle(copies)
    total0 = s["q0"][pl.ds(y * w0, w0)].astype(F32)
    for d in range(ny - 1):
        total0 = total0 + s["t0"][d].astype(F32)
    total0 = total0.astype(BF16)
    total1 = s["q1"][pl.ds(x * w1, w1)].astype(F32)
    for d in range(nx - 1):
        total1 = total1 + s["t1"][d].astype(F32)
    total1 = total1.astype(BF16)
    for k in range(nz):
        s["zbuf"][k, 0] = total0[k]
        s["zbuf"][k, 1] = total1[k]
        s["zbuf"][k, 2] = total0[nz]
    copies = [push(s["zbuf"].at[(z + d) % nz], s["zr"].at[d - 1], at_z(d)) for d in range(1, nz)]
    settle(copies)
    sums = s["zbuf"][z].astype(F32)
    for d in range(nz - 1):
        sums = sums + s["zr"][d].astype(F32)
    s["dens"][...] = sums[2]
    density = jnp.concatenate([s["dens"][pl.ds(z, 1), :], s["dens"][pl.ds(SIDE + z, 1), :]], axis=1)
    scaled = jnp.concatenate([sums[0], sums[1]], axis=1) * lax.rsqrt(1.0 + density)
    level = jnp.where(
        lax.broadcasted_iota(jnp.int32, (16, CH), 0) == 0,
        jnp.broadcast_to(0.25 * jnp.log(1.0 + density), (16, CH)), 0.0,
    )
    encoded = jnp.concatenate([scaled, level], axis=0).astype(BF16)

    grid_hat, grid_scale = normalise(dot(encoded, embed_m, TN))
    normed_grid = grid_hat.astype(BF16)
    first = jnp.zeros((CELLS, CH), F32)
    for i in range(4):
        first = first + dot(normed_grid[i * CELLS : (i + 1) * CELLS], patch_w[i * CH : (i + 1) * CH, :])
    state = first.astype(BF16)

    def halo_send(which, field):
        src, dst = s["halo_src%d" % which], s["halo_dst%d" % which]
        src[0] = field.astype(BF16)
        src[1] = jnp.swapaxes(field.reshape(SIDE, SIDE, CH), 0, 1).reshape(CELLS, CH).astype(BF16)
        found = []
        for index, (i, j) in enumerate(HALOS):
            if j == 0:
                piece = src.at[0, pl.ds(32 if i > 0 else 0, 32)]
            else:
                piece = src.at[1, pl.ds(32 if j > 0 else 0, 32)]
            found.append(push(piece, dst.at[index], at_halo(i, j)))
        return found

    def pad_inner(which, field):
        pad = s["pad%d" % which]
        pad[...] = jnp.zeros_like(pad)
        for p in range(SIDE):
            for h in range(2):
                pad[h, pl.ds((REACH + p) * PADW + REACH, SIDE), :] = field[
                    p * SIDE : (p + 1) * SIDE, h * 128 : (h + 1) * 128
                ]

    def halo_wait(which, copies):
        pad, dst = s["pad%d" % which], s["halo_dst%d" % which]
        settle(copies)
        for index, (i, j) in enumerate(HALOS):
            if j == 0:
                for r in range(REACH):
                    if i > 0:
                        row, at = r, 1 + r
                    else:
                        row, at = REACH + SIDE + r, r
                    strip = dst[index].astype(F32)[at * SIDE : (at + 1) * SIDE]
                    for h in range(2):
                        pad[h, pl.ds(row * PADW + REACH, SIDE), :] = strip[:, h * 128 : (h + 1) * 128]
                continue
            inside = (z > 0) if j > 0 else (z < nz - 1)
            keep = jnp.where(inside, 1.0, 0.0).astype(F32)
            block = dst[index].astype(F32) * keep
            for r in range(REACH):
                if j > 0:
                    column, at = r, 1 + r
                else:
                    column, at = REACH + SIDE + r, r
                strip = block[at * SIDE : (at + 1) * SIDE]
                if i == 0:
                    top, strip = REACH, strip
                elif i > 0:
                    top, strip = 0, strip[SIDE - REACH :]
                else:
                    top, strip = REACH + SIDE, strip[:REACH]
                for h in range(2):
                    pad[h, pl.ds(top * PADW + column, strip.shape[0], PADW), :] = strip[:, h * 128 : (h + 1) * 128]

    def window(which, column):
        pad = s["pad%d" % which]
        return jnp.stack(
            [
                jnp.concatenate([pad[h, pl.ds(p * PADW + column, SIDE), :] for h in range(2)], axis=1)
                for p in range(14)
            ],
            axis=0,
        )

    def taps_of(k):
        return [depth_k[tap].astype(F32)[k : k + 1].reshape(1, 1, CH) for tap in range(KSIDE * KSIDE)]

    def convolve(which, kernel, flip):
        total = jnp.zeros((SIDE, SIDE, CH), F32)
        for b in range(KSIDE):
            part = window(which, b)
            for a in range(KSIDE):
                tap = KSIDE * a + b
                if flip:
                    tap = KSIDE * KSIDE - 1 - tap
                total = total + part[a : a + SIDE] * kernel[tap]
        return total.reshape(CELLS, CH)

    def kernel_grad(which, grad):
        grad = grad.reshape(SIDE, SIDE, CH)
        for b in range(KSIDE):
            part = window(which, b)
            for a in range(KSIDE):
                s["tap"][KSIDE * a + b] = jnp.sum(part[a : a + SIDE] * grad, axis=0)
        taps = jnp.sum(s["tap"][...], axis=1)
        for h in range(2):
            s["kg"][h, pl.ds(which, KSIDE * KSIDE, 2), :] = taps[:, h * 128 : (h + 1) * 128]

    stored = []
    for k in range(2):
        field = state.astype(F32)
        copies = halo_send(k, field)
        pad_inner(k, field)
        kernel = taps_of(k)
        halo_wait(k, copies)
        hat, scale = normalise(convolve(k, kernel, False))
        normed = hat.astype(BF16)
        act = dot(normed, expand_w[k])
        share = cdf(act)
        hidden = (act * share).astype(BF16)
        state = (field + dot(hidden, reduce_w[k])).astype(BF16)
        slope = share + act * jnp.exp(-0.5 * jnp.square(act)) * (1.0 / math.sqrt(2.0 * math.pi))
        stored.append((hat, scale, normed, hidden, slope))
    feat[...] = state

    progress = {}

    def group(name):
        return next(entry for entry in GROUPS if entry[0] == name)

    def lines(name):
        _, n_p, n_q, _ = group(name)
        return (("p", n_p, nx, x, at_x, ny, y, at_y), ("q", n_q, ny, y, at_y, nx, x, at_x))

    def begin(name):
        found = []
        for d in [*range(1, max(nx, ny)), 0]:
            for key, n, count, place, _, _, _, _ in lines(name):
                if d < count:
                    size = n // count
                    at = pl.ds(((place + d) % count) * size, size)
                    found.append((key, d, push(s[name + "g" + key].at[1 - core, at], s[name + "c" + key].at[at], at_core())))
        progress[name] = found

    def stage_first(name):
        found = []
        info = {line[0]: line for line in lines(name)}
        for key, d, copy in progress[name]:
            _, n, count, place, where, _, _, _ = info[key]
            size = n // count
            copy.wait_recv()
            own, got, out = s[name + "g" + key], s[name + "c" + key], s[name + "s" + key]
            base = ((place + d) % count) * size
            step = math.gcd(8, size)
            for i in range(0, size, step):
                at = pl.ds(base + i, step)
                out[at] = (own[core, at].astype(F32) + got[at].astype(F32)).astype(BF16)
            if d:
                found.append(push(out.at[pl.ds(base, size)], s[name + "l1" + key].at[d - 1], where(d)))
        progress[name] = found

    def stage_second(name):
        settle(progress[name])
        found = []
        for key, n, first, place, _, second, place_2, where in lines(name):
            size, small = n // first, n // (first * second)
            own, land, out = s[name + "s" + key], s[name + "l1" + key], s[name + "s2" + key]
            for d in [*range(1, second), 0]:
                base = ((place_2 + d) % second) * small
                total = own[pl.ds(place * size + base, small)].astype(F32)
                for e in range(first - 1):
                    total = total + land[e, pl.ds(base, small)].astype(F32)
                out[pl.ds(base, small)] = total.astype(BF16)
                if d:
                    found.append(push(out.at[pl.ds(base, small)], s[name + "l2" + key].at[d - 1], where(d)))
        progress[name] = found

    def stage_third(name):
        _, n_p, n_q, scatter = group(name)
        up, uq = n_p // nlon, n_q // nlon
        settle(progress[name])
        s3 = s[name + "s3"]
        fold(s3.at[pl.ds(0, up)], s[name + "s2p"], s[name + "l2p"], ny, y * up, up, math.gcd(8, up))
        fold(s3.at[pl.ds(up, uq)], s[name + "s2q"], s[name + "l2q"], nx, x * uq, uq, math.gcd(8, uq))
        l3 = s[name + "l3"]
        if scatter:
            piece = (up + uq) // nz
            progress[name] = [
                push(s3.at[pl.ds(((z + d) % nz) * piece, piece)], l3.at[d - 1], at_z(d)) for d in range(1, nz)
            ]
        else:
            l3[z] = s3[...]
            progress[name] = [push(s3, l3.at[z], at_z(d), l3.at[(z + nz - d) % nz]) for d in range(1, nz)]

    def stage_gather(name):
        _, n_p, n_q, _ = group(name)
        piece = (n_p + n_q) // (nlon * nz)
        settle(progress[name])
        s3, l3, f3 = s[name + "s3"], s[name + "l3"], s[name + "f3"]
        total = s3[pl.ds(z * piece, piece)].astype(F32)
        for d in range(nz - 1):
            total = total + l3[d].astype(F32)
        f3[z] = total.astype(BF16)
        progress[name] = [push(f3.at[z], f3.at[z], at_z(d), f3.at[(z + nz - d) % nz]) for d in range(1, nz)]

    def stage_back_second(name):
        _, n_p, n_q, scatter = group(name)
        up, uq = n_p // nlon, n_q // nlon
        settle(progress[name])
        fp, fq = s[name + "fp"], s[name + "fq"]
        at_p, at_q = x * (n_p // nx) + y * up, y * (n_q // ny) + x * uq
        if scatter:
            done = s[name + "f3"][...].reshape(up + uq, 16, 128)
        else:
            total = s[name + "l3"][0].astype(F32)
            for d in range(1, nz):
                total = total + s[name + "l3"][d].astype(F32)
            done = total.astype(BF16)
        fp[core, pl.ds(at_p, up)] = done[:up]
        fq[core, pl.ds(at_q, uq)] = done[up:]

        def from_p(d):
            return fp.at[core, pl.ds(x * (n_p // nx) + ((y + ny - d) % ny) * up, up)]

        def from_q(d):
            return fq.at[core, pl.ds(y * (n_q // ny) + ((x + nx - d) % nx) * uq, uq)]

        progress[name] = [push(from_p(0), from_p(0), at_y(d), from_p(d)) for d in range(1, ny)]
        progress[name] += [push(from_q(0), from_q(0), at_x(d), from_q(d)) for d in range(1, nx)]

    def stage_back_first(name):
        settle(progress[name])
        found, handed = [], []
        for d in range(0, max(nx, ny)):
            for key, n, count, place, where, _, _, _ in lines(name):
                if d >= count:
                    continue
                size, whole = n // count, s[name + "f" + key]
                own = whole.at[core, pl.ds(place * size, size)]
                at = pl.ds(((place + count - d) % count) * size, size)
                if d:
                    found.append((whole, at, push(own, own, where(d), whole.at[core, at])))
                else:
                    handed.append((whole, at))
        hand_over(name, handed)
        progress[name] = (found, progress[name])

    def hand_over(name, handed):
        progress[name] = [
            push(whole.at[core, at], whole.at[core, at], at_core(), whole.at[1 - core, at]) for whole, at in handed
        ]

    def stage_back_core(name):
        found, earlier = progress[name]
        for whole, at, copy in found:
            copy.wait_recv()
            hand_over(name, [(whole, at)])
            earlier = earlier + progress[name]
        progress[name] = earlier

    def put_tall(name, left, right):
        for h in range(2):
            s[name + "gp"][h] = dot(left, right[:, h * 128 : (h + 1) * 128], TN).astype(BF16).reshape(64, 16, 128)

    def put_wide(name, left, right):
        for lane in range(8):
            part = dot(left, right[:, lane * 128 : (lane + 1) * 128], TN).astype(BF16)
            s[name + "gq"][lane // 4, (lane % 4) * 16 : (lane % 4 + 1) * 16] = part.reshape(16, 16, 128)

    cotangent = cot[...]
    for k in (1, 0):
        name = "A" if k == 1 else "B"
        hat, scale, normed, hidden, slope = stored[k]
        grad_act = (dot(cotangent, reduce_w[k], NT) * slope).astype(BF16)
        grad_depth = normalise_grad(hat, scale, dot(grad_act, expand_w[k], NT))
        copies = halo_send(2 + k, grad_depth)
        put_tall(name, hidden, cotangent)
        put_wide(name, normed, grad_act)
        begin(name)
        pad_inner(2 + k, grad_depth)
        kernel_grad(k, grad_depth)
        if k == 0:
            stage_second("A")
        stage_first(name)
        halo_wait(2 + k, copies)
        cotangent = (cotangent.astype(F32) + convolve(2 + k, taps_of(k), True)).astype(BF16)

    parts = []
    for i in range(4):
        piece = normed_grid[i * CELLS : (i + 1) * CELLS]
        grad = dot(piece, cotangent, TN).astype(BF16)
        for h in range(2):
            target = s["Cgp"] if i < 2 else s["Cgq"]
            target[h, (i % 2) * 16 : (i % 2 + 1) * 16] = grad[:, h * 128 : (h + 1) * 128].reshape(16, 16, 128)
        parts.append(dot(cotangent, patch_w[i * CH : (i + 1) * CH, :], NT))
    grad_grid = normalise_grad(grid_hat, grid_scale, jnp.concatenate(parts, axis=0)).astype(BF16)
    grad_embed = dot(encoded, grad_grid).astype(BF16)
    for h in range(2):
        s["Cgq"][h, 32:39] = s["kg"][h].astype(BF16).reshape(7, 16, 128)
        s["Cgq"][h, 39:41] = grad_embed[:, h * 128 : (h + 1) * 128].reshape(2, 16, 128)
        s["Cgq"][h, 41:48] = jnp.zeros((7, 16, 128), BF16)
    begin("C")
    stage_third("A")
    stage_first("C")
    stage_second("B")
    stage_gather("A")
    stage_second("C")
    stage_third("B")
    stage_back_second("A")
    stage_third("C")
    stage_gather("B")
    stage_back_first("A")
    stage_back_second("B")
    stage_back_second("C")
    stage_back_core("A")
    stage_back_first("B")
    stage_back_first("C")
    stage_back_core("C")
    stage_back_core("B")
    for name in ("A", "C", "B"):
        settle(progress[name])
    for copy in sent:
        copy.wait_send()


def widen_kernel(feat, afp, afq, bfp, bfq, cfp, cfq, *refs):
    outs, stage, rows, sems = refs[:6], refs[6:12], refs[12], refs[13]
    s_feat, s_embed, s_patch, s_kernel, s_expand, s_reduce = stage
    s_feat[...] = feat[...]
    pending = []

    def ship(src, dst):
        copy = pltpu.make_async_copy(src, dst, sems.at[len(pending)])
        copy.start()
        pending.append(copy)

    def block(units):
        return units.astype(F32).reshape(units.shape[0] * 16, 128)

    ship(s_feat, outs[0])
    for k, fp, fq in ((1, afp, afq), (0, bfp, bfq)):
        for r in range(0, 64, 16):
            for h in range(2):
                s_reduce[k, r * 16 : (r + 16) * 16, h * 128 : (h + 1) * 128] = block(fp[h, r : r + 16])
        ship(s_reduce.at[k], outs[5].at[k])
        for lane in range(8):
            s_expand[k, :, lane * 128 : (lane + 1) * 128] = block(fq[lane // 4, (lane % 4) * 16 : (lane % 4 + 1) * 16])
        ship(s_expand.at[k], outs[4].at[k])
    for source, base in ((cfp, 0), (cfq, 512)):
        for r in range(0, 32, 16):
            for h in range(2):
                at = slice(base + r * 16, base + (r + 16) * 16)
                s_patch[at, h * 128 : (h + 1) * 128] = block(source[h, r : r + 16])
    ship(s_patch, outs[2])
    for h in range(2):
        at = slice(h * 128, (h + 1) * 128)
        rows[...] = block(cfq[h, 32:39])
        for tap in range(KSIDE * KSIDE):
            s_kernel[tap, :, at] = rows[2 * tap : 2 * tap + 2, :]
        s_embed[:, at] = block(cfq[h, 39:41])[: OBSF + 1]
    ship(s_kernel, outs[3])
    ship(s_embed, outs[1])
    for copy in pending:
        copy.wait()


def factor(lon):
    nx = math.isqrt(lon)
    while lon % nx:
        nx -= 1
    return nx, lon // nx


def on_device(values, coords, dest, count, embed_w, patch_w, depth_k, expand_w, reduce_w, cot):
    nx, ny = factor(lax.axis_size("lon"))
    nz = lax.axis_size("lat")
    p0, p1 = encode(nx, ny, nz, dest[0, 0, 0], count[0, 0, 0], values[0, 0, 0], coords[0, 0, 0])
    plan = scratch_plan(nx, ny, nz)
    copies = copy_count(nx, ny, nz)
    vmem = pl.BlockSpec(memory_space=pltpu.VMEM)
    operands = (embed_w, patch_w, jnp.transpose(depth_k, (1, 0, 2)), expand_w, reduce_w, cot[0].reshape(CELLS, CH))
    finals = []
    for _, n_p, n_q, _ in GROUPS:
        finals += [jax.ShapeDtypeStruct((2, n, 16, 128), BF16) for n in (n_p, n_q)]
    handed = pl.pallas_call(
        functools.partial(net_kernel, nx, ny, nz, tuple(plan)),
        out_shape=(jax.ShapeDtypeStruct((CELLS, CH), BF16),) + tuple(finals),
        in_specs=[vmem] * 2 + [pl.BlockSpec(memory_space=pltpu.HBM)] * 6,
        out_specs=(vmem,) * 7,
        scratch_shapes=list(plan.values())
        + [pltpu.VMEM(leaf.shape, leaf.dtype) for leaf in operands]
        + [pltpu.SemaphoreType.DMA((n,)) for n in (copies, copies, len(operands))],
        compiler_params=pltpu.CompilerParams(
            collective_id=0, has_side_effects=True, vmem_limit_bytes=32 * 2**20
        ),
    )(p0, p1, *(in_hbm(leaf) for leaf in operands))
    shapes = (
        jax.ShapeDtypeStruct((CELLS, CH), BF16),
        jax.ShapeDtypeStruct((OBSF + 1, CH), F32),
        jax.ShapeDtypeStruct((4 * CH, CH), F32),
        jax.ShapeDtypeStruct((KSIDE * KSIDE, 2, CH), F32),
        jax.ShapeDtypeStruct((2, CH, HID), F32),
        jax.ShapeDtypeStruct((2, HID, CH), F32),
    )
    outs = pl.pallas_call(
        widen_kernel,
        out_shape=shapes,
        in_specs=[vmem] * 7,
        out_specs=(pl.BlockSpec(memory_space=pltpu.HBM),) * 6,
        scratch_shapes=[pltpu.VMEM(leaf.shape, leaf.dtype) for leaf in shapes]
        + [pltpu.VMEM((112, 128), F32), pltpu.SemaphoreType.DMA((8,))],
        compiler_params=pltpu.CompilerParams(vmem_limit_bytes=24 * 2**20),
    )(*handed)
    return (
        outs[0].reshape(1, SIDE, SIDE, CH), outs[1], outs[2], jnp.transpose(outs[3], (1, 0, 2)), outs[4], outs[5],
    )


def solution(mesh):
    in_specs = (
        P("dp", "lon", "lat", None, None, None),
        P("dp", "lon", "lat", None, None, None),
        P("dp", "lon", "lat", None),
        P("dp", "lon", "lat", None),
        P(),
        P(),
        P(),
        P(),
        P(),
        P("dp", "lon", "lat", None),
    )
    out_specs = (P("dp", "lon", "lat", None), P(), P(), P(), P(), P())
    return jax.shard_map(
        on_device, mesh=mesh, in_specs=in_specs, out_specs=out_specs, check_vma=False
    )
```

```python
import functools
import math

import jax
import jax.numpy as jnp
from jax import lax
from jax.experimental import pallas as pl
from jax.experimental.pallas import tpu as pltpu
from jax.sharding import PartitionSpec as P

MESH = pl.DeviceIdType.MESH
F32 = jnp.float32
BF16 = jnp.bfloat16
OBSF = 16
KSIDE = 7
REACH = 3
TILE = 16
SIDE = 8
CELLS = 64
CH = 256
HID = 1024
INVERSE = 0.5 / (0.7 * 0.7)
PADW = 16
NT = (((1,), (1,)), ((), ()))
TN = (((0,), (0,)), ((), ()))


def dot(a, b, dims=(((1,), (0,)), ((), ()))):
    return lax.dot_general(a, b, dims, preferred_element_type=F32)


PARTS = 4
SLOTS = 128


def in_hbm(array):
    return pltpu.with_memory_space_constraint(array, pltpu.HBM)


def encode_block(block, count_ref, values_ref, coords_ref):
    rows = values_ref.shape[2]
    order = lax.broadcasted_iota(jnp.int32, (TILE, rows), 0)
    cell = (2 * (order % SIDE) + order // SIDE).astype(F32)
    lane = lax.broadcasted_iota(jnp.int32, (TILE, rows), 1)
    pair = coords_ref[block]
    a = jnp.exp(-jnp.square(pair[0:1, :] - cell) * INVERSE)
    a = jnp.where(lane < count_ref[block], a, 0.0)
    b = jnp.exp(-jnp.square(pair[1:2, :] - cell) * INVERSE)
    parts = []
    for i in range(2):
        for j in range(2):
            left = a[i * SIDE : (i + 1) * SIDE]
            right = b[j * SIDE : (j + 1) * SIDE].astype(BF16)
            right = jnp.concatenate([right, right], axis=0)
            for p in range(0, SIDE, 2):
                pair_of = [jnp.broadcast_to(left[p + n : p + n + 1], (SIDE, rows)) for n in range(2)]
                parts.append(jnp.concatenate(pair_of, axis=0).astype(BF16) * right)
    weight = jnp.concatenate(parts, axis=0)
    ones = jnp.ones((OBSF, rows), BF16)
    return dot(jnp.concatenate([values_ref[block], ones], axis=0), weight, NT)


def encode_part(part, share, count_ref, values_ref, coords_ref, res0, res1, resd):
    def body(block, carry):
        sums = encode_block(block, count_ref, values_ref, coords_ref)
        res0[block + 1] = sums[:OBSF, :128].astype(BF16)
        res1[block + 1] = sums[:OBSF, 128:].astype(BF16)
        resd[block + 1, 0:1, :] = sums[OBSF : OBSF + 1, :128]
        resd[block + 1, 1:2, :] = sums[OBSF : OBSF + 1, 128:]
        return carry

    lax.fori_loop(part * share, (part + 1) * share, body, 0, unroll=share)


def slot_of_tile(dest, blocks):
    row = lax.broadcasted_iota(jnp.int32, (blocks, blocks), 0)
    column = lax.broadcasted_iota(jnp.int32, (blocks, blocks), 1)
    spread = jnp.where(row == column, jnp.broadcast_to(dest, (blocks, blocks)), 0)
    upright = jnp.sum(spread, axis=1, keepdims=True)
    tile = lax.broadcasted_iota(jnp.int32, (blocks, SLOTS), 1)
    number = lax.broadcasted_iota(jnp.int32, (blocks, SLOTS), 0) + 1
    return jnp.minimum(jnp.sum(jnp.where(upright == tile, number, 0), axis=0, keepdims=True), blocks)


def normalise(field):
    center = jnp.mean(field, axis=-1, keepdims=True)
    shifted = field - center
    scale = lax.rsqrt(jnp.mean(jnp.square(shifted), axis=-1, keepdims=True) + 1e-05)
    return shifted * scale, scale


def normalise_grad(normed, scale, grad):
    return scale * (
        grad
        - jnp.mean(grad, axis=-1, keepdims=True)
        - normed * jnp.mean(grad * normed, axis=-1, keepdims=True)
    )


def cdf(field):
    return 0.5 * (1.0 + lax.erf(field * math.sqrt(0.5)))


def group_sizes(nx, ny, nz, np_half, nq_half):
    return np_half // (nx * ny), nq_half // (nx * ny)


def group_scratch(nx, ny, nz, n_p, n_q, scatter):
    up, uq = n_p // (nx * ny), n_q // (nx * ny)

    def units(*lead):
        return pltpu.VMEM(tuple(lead) + (16, 128), BF16)

    plan = {
        "gp": units(2, n_p), "gq": units(2, n_q),
        "cp": units(n_p), "cq": units(n_q),
        "sp": units(n_p), "sq": units(n_q),
        "l1p": units(nx - 1, n_p // nx), "l1q": units(ny - 1, n_q // ny),
        "s2p": units(n_p // nx), "s2q": units(n_q // ny),
        "l2p": units(ny - 1, up), "l2q": units(nx - 1, uq),
        "s3": units(up + uq),
    }
    if scatter:
        piece = (up + uq) // nz
        plan["l3"] = units(nz - 1, piece)
        plan["f3"] = units(nz, piece)
    else:
        plan["l3"] = units(nz, up + uq)
    return plan


GROUPS = (("A", 64, 64, True), ("B", 64, 64, True), ("C", 32, 48, False))


def scratch_plan(nx, ny, nz, blocks):
    def units(*lead):
        return pltpu.VMEM(tuple(lead) + (16, 128), BF16)

    lon = nx * ny
    plan = {
        "p0": units(lon * (nz + 1)), "p1": units(lon * nz),
        "res0": units(blocks + 1), "res1": units(blocks + 1),
        "resd": pltpu.VMEM((blocks + 1, 2, 128), F32),
        "densities": pltpu.VMEM((lon, 16, 128), F32),
        "slots_v": pltpu.VMEM((1, SLOTS), jnp.int32),
        "slots": pltpu.SMEM((1, SLOTS), jnp.int32),
        "corner": pltpu.VMEM((16, CH), F32),
        "r0": units(nx - 1, ny * (nz + 1)), "r1": units(ny - 1, nx * nz),
        "q0": units(ny * (nz + 1)), "q1": units(nx * nz),
        "t0": units(ny - 1, nz + 1), "t1": units(nx - 1, nz),
        "zbuf": units(nz, 3), "zr": units(nz - 1, 3),
        "dens": pltpu.VMEM((16, 128), F32),
        "ew": pltpu.VMEM((32, CH), F32),
        "kg": pltpu.VMEM((2, 112, 128), F32),
        "tap": pltpu.VMEM((KSIDE * KSIDE, 8, CH), F32),
    }
    for k in range(4):
        plan["halo_src%d" % k] = pltpu.VMEM((2, CELLS, CH), BF16)
        plan["halo_corner%d" % k] = pltpu.VMEM((4, 16, CH), BF16)
        plan["halo_dst%d" % k] = pltpu.VMEM((8, CELLS // 2, CH), BF16)
        plan["pad%d" % k] = pltpu.VMEM((2, 14 * PADW, 128), F32)
    plan["cols"] = pltpu.VMEM((CELLS, CH), F32)
    for name, n_p, n_q, scatter in GROUPS:
        for key, value in group_scratch(nx, ny, nz, n_p, n_q, scatter).items():
            plan[name + key] = value
    return plan


def copy_count(nx, ny, nz):
    total = 2 * (nx + ny - 2) + (nz - 1) + 4 * 8
    for _, _, _, scatter in GROUPS:
        total += 2 * (nx + ny) + 4 * (nx + ny - 2) + (nz - 1) * (2 if scatter else 1)
    return total


INPUTS = 10
FINALS = ("Afp", "Afq", "Bfp", "Bfq", "Cfp", "Cfq")
HALOS = tuple((i, j) for i in (-1, 0, 1) for j in (-1, 0, 1) if (i, j) != (0, 0))


def net_kernel(nx, ny, nz, names, *refs):
    far, feat, rest = refs[:INPUTS], refs[INPUTS], refs[INPUTS + 1 :]
    s = dict(zip(FINALS, rest[: len(FINALS)]))
    rest = rest[len(FINALS) :]
    s.update(zip(names, rest))
    rest = rest[len(names) :]
    near = rest[:INPUTS]
    dest_ref, count_ref, values_ref, coords_ref, embed_w, patch_w, depth_k, expand_w, reduce_w, cot = near
    send_sem, recv_sem, load_sem = rest[INPUTS:]
    blocks = values_ref.shape[0]
    parts = PARTS if blocks % PARTS == 0 else 1
    share = blocks // parts
    first_loads = [pltpu.make_async_copy(far[i], near[i], load_sem.at[i]) for i in range(2)]
    block_loads = []
    for part in range(parts):
        at = pl.ds(part * share, share)
        block_loads.append(
            [
                pltpu.make_async_copy(far[i].at[at], near[i].at[at], load_sem.at[i + 2 * part])
                for i in (2, 3)
            ]
        )
    loads = [
        pltpu.make_async_copy(far[i], near[i], load_sem.at[i + 2 * PARTS]) for i in range(4, INPUTS)
    ]
    slot_load = pltpu.make_async_copy(s["slots_v"], s["slots"], load_sem.at[INPUTS + 2 * PARTS])
    for load in first_loads + [load for part in block_loads for load in part]:
        load.start()
    core = lax.axis_index("dp")
    lon = lax.axis_index("lon")
    z = lax.axis_index("lat")
    x = lon // ny
    y = lon % ny
    nlon = nx * ny

    def at_core():
        return (1 - core, lon, z)

    def at_x(d):
        return (core, ((x + d) % nx) * ny + y, z)

    def at_y(d):
        return (core, x * ny + (y + d) % ny, z)

    def at_z(d):
        return (core, lon, (z + d) % nz)

    def at_halo(i, j):
        return (core, (lon + i + nlon) % nlon, (z + j + nz) % nz)

    barrier = pltpu.get_barrier_semaphore()
    peers = [at_core()] + [at_x(d) for d in range(1, nx)] + [at_y(d) for d in range(1, ny)]
    peers += [at_z(d) for d in range(1, nz)] + [at_halo(i, j) for i, j in HALOS]
    for peer in peers:
        pl.semaphore_signal(barrier, inc=1, device_id=peer, device_id_type=MESH)
    for load in loads:
        load.start()

    for load in first_loads:
        load.wait()
    s["slots_v"][...] = slot_of_tile(dest_ref[...], blocks)
    slot_load.start()
    res0, res1, resd = s["res0"], s["res1"], s["resd"]
    res0[0] = jnp.zeros((16, 128), BF16)
    res1[0] = jnp.zeros((16, 128), BF16)
    resd[0] = jnp.zeros((2, 128), F32)
    for part in range(parts):
        for load in block_loads[part]:
            load.wait()
        encode_part(part, share, count_ref, values_ref, coords_ref, res0, res1, resd)
    slot_load.wait()
    p0, p1, densities = s["p0"], s["p1"], s["densities"]

    def fill(tile_lon, carry):
        tile_x, tile_y = tile_lon // ny, tile_lon % ny
        for tile_z in range(nz):
            slot = jnp.clip(s["slots"][0, tile_lon * nz + tile_z], 0, blocks)
            p0[tile_lon * (nz + 1) + tile_z] = res0[slot]
            p1[(tile_y * nx + tile_x) * nz + tile_z] = res1[slot]
            density = resd[slot]
            densities[tile_lon, tile_z : tile_z + 1, :] = density[0:1]
            densities[tile_lon, SIDE + tile_z : SIDE + tile_z + 1, :] = density[1:2]
        p0[tile_lon * (nz + 1) + nz] = densities[tile_lon].astype(BF16)
        return carry

    if nz < SIDE:
        densities[...] = jnp.zeros_like(densities)
    lax.fori_loop(0, nlon, fill, 0, unroll=2)
    pl.semaphore_wait(barrier, len(peers))

    sent = []

    def push(src, dst, device, land=None):
        index = len(sent)

        def make(target):
            return pltpu.make_async_remote_copy(
                src_ref=src, dst_ref=target, send_sem=send_sem.at[index], recv_sem=recv_sem.at[index],
                device_id=device, device_id_type=MESH,
            )

        copy = make(dst)
        copy.start()
        sent.append(copy)
        return copy if land is None else make(land)

    def settle(copies):
        for copy in copies:
            copy.wait_recv()

    def spread(src, land, size, count, target):
        position = {"x": x, "y": y}[target]
        where = {"x": at_x, "y": at_y}[target]
        return [
            push(src.at[pl.ds(((position + d) % count) * size, size)], land.at[d - 1], where(d))
            for d in range(1, count)
        ]

    def fold(out, first, land, count, offset, size, step):
        for i in range(0, size, step):
            total = first[pl.ds(offset + i, step)].astype(F32)
            for d in range(count - 1):
                total = total + land[d, i : i + step].astype(F32)
            out[i : i + step] = total.astype(BF16)

    w0, w1 = nz + 1, nz
    copies = spread(p0, s["r0"], ny * w0, nx, "x") + spread(p1, s["r1"], nx * w1, ny, "y")
    s["ew"][...] = jnp.zeros_like(s["ew"])
    for load in loads:
        load.wait()
    s["ew"][0 : OBSF + 1, :] = embed_w[...].astype(F32)
    s["kg"][...] = jnp.zeros_like(s["kg"])
    embed_m = s["ew"][...].astype(BF16)
    settle(copies)
    fold(s["q0"], p0, s["r0"], nx, x * (ny * w0), ny * w0, w0)
    fold(s["q1"], p1, s["r1"], ny, y * (nx * w1), nx * w1, w1)
    copies = spread(s["q0"], s["t0"], w0, ny, "y") + spread(s["q1"], s["t1"], w1, nx, "x")
    settle(copies)
    total0 = s["q0"][pl.ds(y * w0, w0)].astype(F32)
    for d in range(ny - 1):
        total0 = total0 + s["t0"][d].astype(F32)
    total0 = total0.astype(BF16)
    total1 = s["q1"][pl.ds(x * w1, w1)].astype(F32)
    for d in range(nx - 1):
        total1 = total1 + s["t1"][d].astype(F32)
    total1 = total1.astype(BF16)
    for k in range(nz):
        s["zbuf"][k, 0] = total0[k]
        s["zbuf"][k, 1] = total1[k]
        s["zbuf"][k, 2] = total0[nz]
    copies = [push(s["zbuf"].at[(z + d) % nz], s["zr"].at[d - 1], at_z(d)) for d in range(1, nz)]
    settle(copies)
    sums = s["zbuf"][z].astype(F32)
    for d in range(nz - 1):
        sums = sums + s["zr"][d].astype(F32)
    s["dens"][...] = sums[2]
    density = jnp.concatenate([s["dens"][pl.ds(z, 1), :], s["dens"][pl.ds(SIDE + z, 1), :]], axis=1)
    scaled = jnp.concatenate([sums[0], sums[1]], axis=1) * lax.rsqrt(1.0 + density)
    level = jnp.where(
        lax.broadcasted_iota(jnp.int32, (16, CH), 0) == 0,
        jnp.broadcast_to(0.25 * jnp.log(1.0 + density), (16, CH)), 0.0,
    )
    encoded = jnp.concatenate([scaled, level], axis=0).astype(BF16)

    grid_hat, grid_scale = normalise(dot(encoded, embed_m, TN))
    normed_grid = grid_hat.astype(BF16)
    first = jnp.zeros((CELLS, CH), F32)
    for i in range(4):
        first = first + dot(normed_grid[i * CELLS : (i + 1) * CELLS], patch_w[i * CH : (i + 1) * CH, :])
    state = first.astype(BF16)

    def halo_send(which, field):
        src, dst = s["halo_src%d" % which], s["halo_dst%d" % which]
        src[0] = field.astype(BF16)
        turned = jnp.swapaxes(field.reshape(SIDE, SIDE, CH), 0, 1)
        src[1] = turned.reshape(CELLS, CH).astype(BF16)
        corner, corners = s["corner"], s["halo_corner%d" % which]
        found = []
        for index, (i, j) in enumerate(HALOS):
            if j == 0:
                piece = src.at[0, pl.ds(32 if i > 0 else 0, 32)]
                found.append(push(piece, dst.at[index], at_halo(i, j)))
            elif i == 0:
                piece = src.at[1, pl.ds(32 if j > 0 else 0, 32)]
                found.append(push(piece, dst.at[index], at_halo(i, j)))
            else:
                for r in range(4):
                    q, p = (4 if j > 0 else 0) + r, 4 if i > 0 else 0
                    corner[r * 4 : r * 4 + 4, :] = turned[q][p : p + 4]
                slot = (i > 0) * 2 + (j > 0)
                corners[slot] = corner[...].astype(BF16)
                found.append(push(corners.at[slot], dst.at[index, pl.ds(0, 16)], at_halo(i, j)))
        return found

    def pad_inner(which, field):
        pad = s["pad%d" % which]
        pad[...] = jnp.zeros_like(pad)
        for p in range(SIDE):
            for h in range(2):
                pad[h, pl.ds((REACH + p) * PADW + REACH, SIDE), :] = field[
                    p * SIDE : (p + 1) * SIDE, h * 128 : (h + 1) * 128
                ]

    def halo_wait(which, copies):
        pad, dst = s["pad%d" % which], s["halo_dst%d" % which]
        settle(copies)
        for index, (i, j) in enumerate(HALOS):
            if j == 0:
                for r in range(REACH):
                    if i > 0:
                        row, at = r, 1 + r
                    else:
                        row, at = REACH + SIDE + r, r
                    strip = dst[index].astype(F32)[at * SIDE : (at + 1) * SIDE]
                    for h in range(2):
                        pad[h, pl.ds(row * PADW + REACH, SIDE), :] = strip[:, h * 128 : (h + 1) * 128]
                continue
            inside = (z > 0) if j > 0 else (z < nz - 1)
            keep = jnp.where(inside, 1.0, 0.0).astype(F32)
            block = (dst[index] if i == 0 else dst[index, 0:16, :]).astype(F32) * keep
            for r in range(REACH):
                if j > 0:
                    column, at = r, 1 + r
                else:
                    column, at = REACH + SIDE + r, r
                if i == 0:
                    top, strip = REACH, block[at * SIDE : (at + 1) * SIDE]
                elif i > 0:
                    top, strip = 0, block[at * 4 + 1 : at * 4 + 4]
                else:
                    top, strip = REACH + SIDE, block[at * 4 : at * 4 + REACH]
                for h in range(2):
                    pad[h, pl.ds(top * PADW + column, strip.shape[0], PADW), :] = strip[:, h * 128 : (h + 1) * 128]

    def window(which, column):
        pad = s["pad%d" % which]
        return jnp.stack(
            [
                jnp.concatenate([pad[h, pl.ds(p * PADW + column, SIDE), :] for h in range(2)], axis=1)
                for p in range(14)
            ],
            axis=0,
        )

    def taps_of(k):
        return [depth_k[tap].astype(F32)[k : k + 1].reshape(1, 1, CH) for tap in range(KSIDE * KSIDE)]

    def convolve(which, kernel, flip):
        total = jnp.zeros((SIDE, SIDE, CH), F32)
        for b in range(KSIDE):
            part = window(which, b)
            for a in range(KSIDE):
                tap = KSIDE * a + b
                if flip:
                    tap = KSIDE * KSIDE - 1 - tap
                total = total + part[a : a + SIDE] * kernel[tap]
        return total.reshape(CELLS, CH)

    def kernel_grad(which, grad):
        grad = grad.reshape(SIDE, SIDE, CH)
        for b in range(KSIDE):
            part = window(which, b)
            for a in range(KSIDE):
                s["tap"][KSIDE * a + b] = jnp.sum(part[a : a + SIDE] * grad, axis=0)
        taps = jnp.sum(s["tap"][...], axis=1)
        for h in range(2):
            s["kg"][h, pl.ds(which, KSIDE * KSIDE, 2), :] = taps[:, h * 128 : (h + 1) * 128]

    stored = []
    for k in range(2):
        field = state.astype(F32)
        copies = halo_send(k, field)
        pad_inner(k, field)
        kernel = taps_of(k)
        halo_wait(k, copies)
        hat, scale = normalise(convolve(k, kernel, False))
        normed = hat.astype(BF16)
        act = dot(normed, expand_w[k])
        share = cdf(act)
        hidden = (act * share).astype(BF16)
        state = (field + dot(hidden, reduce_w[k])).astype(BF16)
        slope = share + act * jnp.exp(-0.5 * jnp.square(act)) * (1.0 / math.sqrt(2.0 * math.pi))
        stored.append((hat, scale, normed, hidden, slope))
    feat[...] = state

    progress = {}

    def group(name):
        return next(entry for entry in GROUPS if entry[0] == name)

    def lines(name):
        _, n_p, n_q, _ = group(name)
        return (("p", n_p, nx, x, at_x, ny, y, at_y), ("q", n_q, ny, y, at_y, nx, x, at_x))

    def begin(name):
        found = []
        for d in [*range(1, max(nx, ny)), 0]:
            for key, n, count, place, _, _, _, _ in lines(name):
                if d < count:
                    size = n // count
                    at = pl.ds(((place + d) % count) * size, size)
                    found.append((key, d, push(s[name + "g" + key].at[1 - core, at], s[name + "c" + key].at[at], at_core())))
        progress[name] = found

    def stage_first(name):
        found = []
        info = {line[0]: line for line in lines(name)}
        for key, d, copy in progress[name]:
            _, n, count, place, where, _, _, _ = info[key]
            size = n // count
            copy.wait_recv()
            own, got, out = s[name + "g" + key], s[name + "c" + key], s[name + "s" + key]
            base = ((place + d) % count) * size
            step = math.gcd(8, size)
            for i in range(0, size, step):
                at = pl.ds(base + i, step)
                out[at] = (own[core, at].astype(F32) + got[at].astype(F32)).astype(BF16)
            if d:
                found.append(push(out.at[pl.ds(base, size)], s[name + "l1" + key].at[d - 1], where(d)))
        progress[name] = found

    def stage_second(name):
        settle(progress[name])
        found = []
        for key, n, first, place, _, second, place_2, where in lines(name):
            size, small = n // first, n // (first * second)
            own, land, out = s[name + "s" + key], s[name + "l1" + key], s[name + "s2" + key]
            for d in [*range(1, second), 0]:
                base = ((place_2 + d) % second) * small
                total = own[pl.ds(place * size + base, small)].astype(F32)
                for e in range(first - 1):
                    total = total + land[e, pl.ds(base, small)].astype(F32)
                out[pl.ds(base, small)] = total.astype(BF16)
                if d:
                    found.append(push(out.at[pl.ds(base, small)], s[name + "l2" + key].at[d - 1], where(d)))
        progress[name] = found

    def stage_third(name):
        _, n_p, n_q, scatter = group(name)
        up, uq = n_p // nlon, n_q // nlon
        settle(progress[name])
        s3 = s[name + "s3"]
        fold(s3.at[pl.ds(0, up)], s[name + "s2p"], s[name + "l2p"], ny, y * up, up, math.gcd(8, up))
        fold(s3.at[pl.ds(up, uq)], s[name + "s2q"], s[name + "l2q"], nx, x * uq, uq, math.gcd(8, uq))
        l3 = s[name + "l3"]
        if scatter:
            piece = (up + uq) // nz
            progress[name] = [
                push(s3.at[pl.ds(((z + d) % nz) * piece, piece)], l3.at[d - 1], at_z(d)) for d in range(1, nz)
            ]
        else:
            l3[z] = s3[...]
            progress[name] = [push(s3, l3.at[z], at_z(d), l3.at[(z + nz - d) % nz]) for d in range(1, nz)]

    def stage_gather(name):
        _, n_p, n_q, _ = group(name)
        piece = (n_p + n_q) // (nlon * nz)
        settle(progress[name])
        s3, l3, f3 = s[name + "s3"], s[name + "l3"], s[name + "f3"]
        total = s3[pl.ds(z * piece, piece)].astype(F32)
        for d in range(nz - 1):
            total = total + l3[d].astype(F32)
        f3[z] = total.astype(BF16)
        progress[name] = [push(f3.at[z], f3.at[z], at_z(d), f3.at[(z + nz - d) % nz]) for d in range(1, nz)]

    def stage_back_second(name):
        _, n_p, n_q, scatter = group(name)
        up, uq = n_p // nlon, n_q // nlon
        settle(progress[name])
        fp, fq = s[name + "fp"], s[name + "fq"]
        at_p, at_q = x * (n_p // nx) + y * up, y * (n_q // ny) + x * uq
        if scatter:
            done = s[name + "f3"][...].reshape(up + uq, 16, 128)
        else:
            total = s[name + "l3"][0].astype(F32)
            for d in range(1, nz):
                total = total + s[name + "l3"][d].astype(F32)
            done = total.astype(BF16)
        fp[core, pl.ds(at_p, up)] = done[:up]
        fq[core, pl.ds(at_q, uq)] = done[up:]

        def from_p(d):
            return fp.at[core, pl.ds(x * (n_p // nx) + ((y + ny - d) % ny) * up, up)]

        def from_q(d):
            return fq.at[core, pl.ds(y * (n_q // ny) + ((x + nx - d) % nx) * uq, uq)]

        progress[name] = [push(from_p(0), from_p(0), at_y(d), from_p(d)) for d in range(1, ny)]
        progress[name] += [push(from_q(0), from_q(0), at_x(d), from_q(d)) for d in range(1, nx)]

    def stage_back_first(name):
        settle(progress[name])
        found, handed = [], []
        for d in range(0, max(nx, ny)):
            for key, n, count, place, where, _, _, _ in lines(name):
                if d >= count:
                    continue
                size, whole = n // count, s[name + "f" + key]
                own = whole.at[core, pl.ds(place * size, size)]
                at = pl.ds(((place + count - d) % count) * size, size)
                if d:
                    found.append((whole, at, push(own, own, where(d), whole.at[core, at])))
                else:
                    handed.append((whole, at))
        hand_over(name, handed)
        progress[name] = (found, progress[name])

    def hand_over(name, handed):
        progress[name] = [
            push(whole.at[core, at], whole.at[core, at], at_core(), whole.at[1 - core, at]) for whole, at in handed
        ]

    def stage_back_core(name):
        found, earlier = progress[name]
        for whole, at, copy in found:
            copy.wait_recv()
            hand_over(name, [(whole, at)])
            earlier = earlier + progress[name]
        progress[name] = earlier

    def put_tall(name, left, right):
        for h in range(2):
            s[name + "gp"][h] = dot(left, right[:, h * 128 : (h + 1) * 128], TN).astype(BF16).reshape(64, 16, 128)

    def put_wide(name, left, right):
        for lane in range(8):
            part = dot(left, right[:, lane * 128 : (lane + 1) * 128], TN).astype(BF16)
            s[name + "gq"][lane // 4, (lane % 4) * 16 : (lane % 4 + 1) * 16] = part.reshape(16, 16, 128)

    cotangent = cot[...]
    for k in (1, 0):
        name = "A" if k == 1 else "B"
        hat, scale, normed, hidden, slope = stored[k]
        grad_act = (dot(cotangent, reduce_w[k], NT) * slope).astype(BF16)
        grad_depth = normalise_grad(hat, scale, dot(grad_act, expand_w[k], NT))
        copies = halo_send(2 + k, grad_depth)
        put_tall(name, hidden, cotangent)
        put_wide(name, normed, grad_act)
        begin(name)
        pad_inner(2 + k, grad_depth)
        kernel_grad(k, grad_depth)
        if k == 0:
            stage_second("A")
        stage_first(name)
        halo_wait(2 + k, copies)
        cotangent = (cotangent.astype(F32) + convolve(2 + k, taps_of(k), True)).astype(BF16)
    stage_third("A")

    parts = []
    for i in range(4):
        piece = normed_grid[i * CELLS : (i + 1) * CELLS]
        grad = dot(piece, cotangent, TN).astype(BF16)
        for h in range(2):
            target = s["Cgp"] if i < 2 else s["Cgq"]
            target[h, (i % 2) * 16 : (i % 2 + 1) * 16] = grad[:, h * 128 : (h + 1) * 128].reshape(16, 16, 128)
        parts.append(dot(cotangent, patch_w[i * CH : (i + 1) * CH, :], NT))
    grad_grid = normalise_grad(grid_hat, grid_scale, jnp.concatenate(parts, axis=0)).astype(BF16)
    grad_embed = dot(encoded, grad_grid).astype(BF16)
    for h in range(2):
        s["Cgq"][h, 32:39] = s["kg"][h].astype(BF16).reshape(7, 16, 128)
        s["Cgq"][h, 39:41] = grad_embed[:, h * 128 : (h + 1) * 128].reshape(2, 16, 128)
        s["Cgq"][h, 41:48] = jnp.zeros((7, 16, 128), BF16)
    begin("C")
    stage_first("C")
    stage_second("B")
    stage_gather("A")
    stage_second("C")
    stage_third("B")
    stage_back_second("A")
    stage_third("C")
    stage_gather("B")
    stage_back_first("A")
    stage_back_second("B")
    stage_back_second("C")
    stage_back_core("A")
    stage_back_first("B")
    stage_back_first("C")
    stage_back_core("C")
    stage_back_core("B")
    for name in ("A", "C", "B"):
        settle(progress[name])
    for copy in sent:
        copy.wait_send()


def widen_kernel(feat, afp, afq, bfp, bfq, cfp, cfq, *refs):
    outs, stage, rows, sems = refs[:6], refs[6:12], refs[12], refs[13]
    s_feat, s_embed, s_patch, s_kernel, s_expand, s_reduce = stage
    s_feat[...] = feat[...]
    pending = []

    def ship(src, dst):
        copy = pltpu.make_async_copy(src, dst, sems.at[len(pending)])
        copy.start()
        pending.append(copy)

    def block(units):
        return units.astype(F32).reshape(units.shape[0] * 16, 128)

    ship(s_feat, outs[0])
    for k, fp, fq in ((1, afp, afq), (0, bfp, bfq)):
        for r in range(0, 64, 16):
            for h in range(2):
                s_reduce[k, r * 16 : (r + 16) * 16, h * 128 : (h + 1) * 128] = block(fp[h, r : r + 16])
        ship(s_reduce.at[k], outs[5].at[k])
        for lane in range(8):
            s_expand[k, :, lane * 128 : (lane + 1) * 128] = block(fq[lane // 4, (lane % 4) * 16 : (lane % 4 + 1) * 16])
        ship(s_expand.at[k], outs[4].at[k])
    for source, base in ((cfp, 0), (cfq, 512)):
        for r in range(0, 32, 16):
            for h in range(2):
                at = slice(base + r * 16, base + (r + 16) * 16)
                s_patch[at, h * 128 : (h + 1) * 128] = block(source[h, r : r + 16])
    ship(s_patch, outs[2])
    for h in range(2):
        at = slice(h * 128, (h + 1) * 128)
        rows[...] = block(cfq[h, 32:39])
        for tap in range(KSIDE * KSIDE):
            s_kernel[tap, :, at] = rows[2 * tap : 2 * tap + 2, :]
        s_embed[:, at] = block(cfq[h, 39:41])[: OBSF + 1]
    ship(s_kernel, outs[3])
    ship(s_embed, outs[1])
    for copy in pending:
        copy.wait()


def factor(lon):
    nx = math.isqrt(lon)
    while lon % nx:
        nx -= 1
    return nx, lon // nx


def on_device(values, coords, dest, count, embed_w, patch_w, depth_k, expand_w, reduce_w, cot):
    nx, ny = factor(lax.axis_size("lon"))
    nz = lax.axis_size("lat")
    operands = (
        dest[0, 0], count[0, 0, 0], values[0, 0, 0], coords[0, 0, 0],
        embed_w, patch_w, jnp.transpose(depth_k, (1, 0, 2)), expand_w, reduce_w, cot[0].reshape(CELLS, CH),
    )
    plan = scratch_plan(nx, ny, nz, values.shape[3])
    copies = copy_count(nx, ny, nz)
    vmem = pl.BlockSpec(memory_space=pltpu.VMEM)
    finals = []
    for _, n_p, n_q, _ in GROUPS:
        finals += [jax.ShapeDtypeStruct((2, n, 16, 128), BF16) for n in (n_p, n_q)]
    handed = pl.pallas_call(
        functools.partial(net_kernel, nx, ny, nz, tuple(plan)),
        out_shape=(jax.ShapeDtypeStruct((CELLS, CH), BF16),) + tuple(finals),
        in_specs=[pl.BlockSpec(memory_space=pltpu.HBM)] * INPUTS,
        out_specs=(vmem,) * 7,
        scratch_shapes=list(plan.values())
        + [(pltpu.SMEM if i == 1 else pltpu.VMEM)(leaf.shape, leaf.dtype) for i, leaf in enumerate(operands)]
        + [pltpu.SemaphoreType.DMA((n,)) for n in (copies, copies, INPUTS + 2 * PARTS + 1)],
        compiler_params=pltpu.CompilerParams(
            collective_id=0, has_side_effects=True, vmem_limit_bytes=32 * 2**20
        ),
    )(*(in_hbm(leaf) for leaf in operands))
    shapes = (
        jax.ShapeDtypeStruct((CELLS, CH), BF16),
        jax.ShapeDtypeStruct((OBSF + 1, CH), F32),
        jax.ShapeDtypeStruct((4 * CH, CH), F32),
        jax.ShapeDtypeStruct((KSIDE * KSIDE, 2, CH), F32),
        jax.ShapeDtypeStruct((2, CH, HID), F32),
        jax.ShapeDtypeStruct((2, HID, CH), F32),
    )
    outs = pl.pallas_call(
        widen_kernel,
        out_shape=shapes,
        in_specs=[vmem] * 7,
        out_specs=(pl.BlockSpec(memory_space=pltpu.HBM),) * 6,
        scratch_shapes=[pltpu.VMEM(leaf.shape, leaf.dtype) for leaf in shapes]
        + [pltpu.VMEM((112, 128), F32), pltpu.SemaphoreType.DMA((8,))],
        compiler_params=pltpu.CompilerParams(vmem_limit_bytes=24 * 2**20),
    )(*handed)
    return (
        outs[0].reshape(1, SIDE, SIDE, CH), outs[1], outs[2], jnp.transpose(outs[3], (1, 0, 2)), outs[4], outs[5],
    )


def solution(mesh):
    in_specs = (
        P("dp", "lon", "lat", None, None, None),
        P("dp", "lon", "lat", None, None, None),
        P("dp", "lon", "lat", None),
        P("dp", "lon", "lat", None),
        P(),
        P(),
        P(),
        P(),
        P(),
        P("dp", "lon", "lat", None),
    )
    out_specs = (P("dp", "lon", "lat", None), P(), P(), P(), P(), P())
    return jax.shard_map(
        on_device, mesh=mesh, in_specs=in_specs, out_specs=out_specs, check_vma=False
    )
```

```python
import functools
import math

import jax
import jax.numpy as jnp
from jax import lax
from jax.experimental import pallas as pl
from jax.experimental.pallas import tpu as pltpu
from jax.sharding import PartitionSpec as P

MESH = pl.DeviceIdType.MESH
F32 = jnp.float32
BF16 = jnp.bfloat16
OBSF = 16
KSIDE = 7
REACH = 3
TILE = 16
SIDE = 8
CELLS = 64
CH = 256
HID = 1024
INVERSE = 0.5 / (0.7 * 0.7)
PADW = 16
NT = (((1,), (1,)), ((), ()))
TN = (((0,), (0,)), ((), ()))


def dot(a, b, dims=(((1,), (0,)), ((), ()))):
    return lax.dot_general(a, b, dims, preferred_element_type=F32)


PARTS = 4
SLOTS = 128


def in_hbm(array):
    return pltpu.with_memory_space_constraint(array, pltpu.HBM)


def encode_block(block, count_ref, values_ref, coords_ref):
    rows = values_ref.shape[2]
    order = lax.broadcasted_iota(jnp.int32, (TILE, rows), 0)
    cell = (2 * (order % SIDE) + order // SIDE).astype(F32)
    lane = lax.broadcasted_iota(jnp.int32, (TILE, rows), 1)
    pair = coords_ref[block]
    a = jnp.exp(-jnp.square(pair[0:1, :] - cell) * INVERSE)
    a = jnp.where(lane < count_ref[block], a, 0.0)
    b = jnp.exp(-jnp.square(pair[1:2, :] - cell) * INVERSE)
    parts = []
    for i in range(2):
        for j in range(2):
            left = a[i * SIDE : (i + 1) * SIDE]
            right = b[j * SIDE : (j + 1) * SIDE].astype(BF16)
            right = jnp.concatenate([right, right], axis=0)
            for p in range(0, SIDE, 2):
                pair_of = [jnp.broadcast_to(left[p + n : p + n + 1], (SIDE, rows)) for n in range(2)]
                parts.append(jnp.concatenate(pair_of, axis=0).astype(BF16) * right)
    weight = jnp.concatenate(parts, axis=0)
    ones = jnp.ones((OBSF, rows), BF16)
    return dot(jnp.concatenate([values_ref[block], ones], axis=0), weight, NT)


def encode_part(part, share, count_ref, values_ref, coords_ref, res0, res1, resd):
    def body(block, carry):
        sums = encode_block(block, count_ref, values_ref, coords_ref)
        res0[block + 1] = sums[:OBSF, :128].astype(BF16)
        res1[block + 1] = sums[:OBSF, 128:].astype(BF16)
        resd[block + 1, 0:1, :] = sums[OBSF : OBSF + 1, :128]
        resd[block + 1, 1:2, :] = sums[OBSF : OBSF + 1, 128:]
        return carry

    lax.fori_loop(part * share, (part + 1) * share, body, 0, unroll=share)


def slot_of_tile(dest, blocks):
    row = lax.broadcasted_iota(jnp.int32, (blocks, blocks), 0)
    column = lax.broadcasted_iota(jnp.int32, (blocks, blocks), 1)
    spread = jnp.where(row == column, jnp.broadcast_to(dest, (blocks, blocks)), 0)
    upright = jnp.sum(spread, axis=1, keepdims=True)
    tile = lax.broadcasted_iota(jnp.int32, (blocks, SLOTS), 1)
    number = lax.broadcasted_iota(jnp.int32, (blocks, SLOTS), 0) + 1
    return jnp.minimum(jnp.sum(jnp.where(upright == tile, number, 0), axis=0, keepdims=True), blocks)


def normalise(field):
    center = jnp.mean(field, axis=-1, keepdims=True)
    shifted = field - center
    scale = lax.rsqrt(jnp.mean(jnp.square(shifted), axis=-1, keepdims=True) + 1e-05)
    return shifted * scale, scale


def normalise_grad(normed, scale, grad):
    return scale * (
        grad
        - jnp.mean(grad, axis=-1, keepdims=True)
        - normed * jnp.mean(grad * normed, axis=-1, keepdims=True)
    )


def cdf(field):
    return 0.5 * (1.0 + lax.erf(field * math.sqrt(0.5)))


def group_sizes(nx, ny, nz, np_half, nq_half):
    return np_half // (nx * ny), nq_half // (nx * ny)


def group_scratch(nx, ny, nz, n_p, n_q, scatter):
    up, uq = n_p // (nx * ny), n_q // (nx * ny)

    def units(*lead):
        return pltpu.VMEM(tuple(lead) + (16, 128), BF16)

    plan = {
        "gp": units(2, n_p), "gq": units(2, n_q),
        "cp": units(n_p), "cq": units(n_q),
        "sp": units(n_p), "sq": units(n_q),
        "l1p": units(nx - 1, n_p // nx), "l1q": units(ny - 1, n_q // ny),
        "s2p": units(n_p // nx), "s2q": units(n_q // ny),
        "l2p": units(ny - 1, up), "l2q": units(nx - 1, uq),
        "s3": units(up + uq),
    }
    if scatter:
        piece = (up + uq) // nz
        plan["l3"] = units(nz - 1, piece)
        plan["f3"] = units(nz, piece)
    else:
        plan["l3"] = units(nz, up + uq)
    return plan


GROUPS = (("A", 64, 64, True), ("B", 64, 64, True), ("C", 32, 48, False))


def scratch_plan(nx, ny, nz, blocks):
    def units(*lead):
        return pltpu.VMEM(tuple(lead) + (16, 128), BF16)

    lon = nx * ny
    plan = {
        "p0": units(lon * (nz + 1)), "p1": units(lon * nz),
        "res0": units(blocks + 1), "res1": units(blocks + 1),
        "resd": pltpu.VMEM((blocks + 1, 2, 128), F32),
        "densities": pltpu.VMEM((lon, 16, 128), F32),
        "slots_v": pltpu.VMEM((1, SLOTS), jnp.int32),
        "slots": pltpu.SMEM((1, SLOTS), jnp.int32),
        "corner": pltpu.VMEM((16, CH), F32),
        "r0": units(nx - 1, ny * (nz + 1)), "r1": units(ny - 1, nx * nz),
        "q0": units(ny * (nz + 1)), "q1": units(nx * nz),
        "t0": units(ny - 1, nz + 1), "t1": units(nx - 1, nz),
        "zbuf": units(nz, 3), "zr": units(nz - 1, 3),
        "dens": pltpu.VMEM((16, 128), F32),
        "ew": pltpu.VMEM((32, CH), F32),
        "kg": pltpu.VMEM((2, 112, 128), F32),
        "tap": pltpu.VMEM((KSIDE * KSIDE, 8, CH), F32),
    }
    for k in range(4):
        plan["halo_src%d" % k] = pltpu.VMEM((2, CELLS, CH), BF16)
        plan["halo_corner%d" % k] = pltpu.VMEM((4, 16, CH), BF16)
        plan["halo_dst%d" % k] = pltpu.VMEM((8, CELLS // 2, CH), BF16)
        plan["pad%d" % k] = pltpu.VMEM((2, 14 * PADW, 128), F32)
    plan["cols"] = pltpu.VMEM((CELLS, CH), F32)
    for name, n_p, n_q, scatter in GROUPS:
        for key, value in group_scratch(nx, ny, nz, n_p, n_q, scatter).items():
            plan[name + key] = value
    return plan


def copy_count(nx, ny, nz):
    total = 2 * (nx + ny - 2) + (nz - 1) + 4 * 8
    for _, _, _, scatter in GROUPS:
        total += 2 * (nx + ny) + 4 * (nx + ny - 2) + (nz - 1) * (2 if scatter else 1)
    return total


INPUTS = 10
FINALS = ("Afp", "Afq", "Bfp", "Bfq", "Cfp", "Cfq")
HALOS = tuple((i, j) for i in (-1, 0, 1) for j in (-1, 0, 1) if (i, j) != (0, 0))


def net_kernel(nx, ny, nz, names, *refs):
    far, feat, rest = refs[:INPUTS], refs[INPUTS], refs[INPUTS + 1 :]
    s = dict(zip(FINALS, rest[: len(FINALS)]))
    rest = rest[len(FINALS) :]
    s.update(zip(names, rest))
    rest = rest[len(names) :]
    near = rest[:INPUTS]
    dest_ref, count_ref, values_ref, coords_ref, embed_w, patch_w, depth_k, expand_w, reduce_w, cot = near
    send_sem, recv_sem, load_sem = rest[INPUTS:]
    blocks = values_ref.shape[0]
    parts = PARTS if blocks % PARTS == 0 else 1
    share = blocks // parts
    first_loads = [pltpu.make_async_copy(far[i], near[i], load_sem.at[i]) for i in range(2)]
    block_loads = []
    for part in range(parts):
        at = pl.ds(part * share, share)
        block_loads.append(
            [
                pltpu.make_async_copy(far[i].at[at], near[i].at[at], load_sem.at[i + 2 * part])
                for i in (2, 3)
            ]
        )
    loads = [
        pltpu.make_async_copy(far[i], near[i], load_sem.at[i + 2 * PARTS]) for i in range(4, INPUTS)
    ]
    slot_load = pltpu.make_async_copy(s["slots_v"], s["slots"], load_sem.at[INPUTS + 2 * PARTS])
    for load in first_loads + [load for part in block_loads for load in part]:
        load.start()
    core = lax.axis_index("dp")
    lon = lax.axis_index("lon")
    z = lax.axis_index("lat")
    x = lon // ny
    y = lon % ny
    nlon = nx * ny

    def at_core():
        return (1 - core, lon, z)

    def at_x(d):
        return (core, ((x + d) % nx) * ny + y, z)

    def at_y(d):
        return (core, x * ny + (y + d) % ny, z)

    def at_z(d):
        return (core, lon, (z + d) % nz)

    def at_halo(i, j):
        return (core, (lon + i + nlon) % nlon, (z + j + nz) % nz)

    barrier = pltpu.get_barrier_semaphore()
    peers = [at_core()] + [at_x(d) for d in range(1, nx)] + [at_y(d) for d in range(1, ny)]
    peers += [at_z(d) for d in range(1, nz)] + [at_halo(i, j) for i, j in HALOS]
    for peer in peers:
        pl.semaphore_signal(barrier, inc=1, device_id=peer, device_id_type=MESH)
    for load in loads:
        load.start()

    for load in first_loads:
        load.wait()
    s["slots_v"][...] = slot_of_tile(dest_ref[...], blocks)
    slot_load.start()
    res0, res1, resd = s["res0"], s["res1"], s["resd"]
    res0[0] = jnp.zeros((16, 128), BF16)
    res1[0] = jnp.zeros((16, 128), BF16)
    resd[0] = jnp.zeros((2, 128), F32)
    for part in range(parts):
        for load in block_loads[part]:
            load.wait()
        encode_part(part, share, count_ref, values_ref, coords_ref, res0, res1, resd)
    slot_load.wait()
    p0, p1, densities = s["p0"], s["p1"], s["densities"]

    def fill(tile_lon, carry):
        tile_x, tile_y = tile_lon // ny, tile_lon % ny
        for tile_z in range(nz):
            slot = jnp.clip(s["slots"][0, tile_lon * nz + tile_z], 0, blocks)
            p0[tile_lon * (nz + 1) + tile_z] = res0[slot]
            p1[(tile_y * nx + tile_x) * nz + tile_z] = res1[slot]
            density = resd[slot]
            densities[tile_lon, tile_z : tile_z + 1, :] = density[0:1]
            densities[tile_lon, SIDE + tile_z : SIDE + tile_z + 1, :] = density[1:2]
        p0[tile_lon * (nz + 1) + nz] = densities[tile_lon].astype(BF16)
        return carry

    if nz < SIDE:
        densities[...] = jnp.zeros_like(densities)
    lax.fori_loop(0, nlon, fill, 0, unroll=2)
    pl.semaphore_wait(barrier, len(peers))

    sent = []

    def push(src, dst, device, land=None):
        index = len(sent)

        def make(target):
            return pltpu.make_async_remote_copy(
                src_ref=src, dst_ref=target, send_sem=send_sem.at[index], recv_sem=recv_sem.at[index],
                device_id=device, device_id_type=MESH,
            )

        copy = make(dst)
        copy.start()
        sent.append(copy)
        return copy if land is None else make(land)

    def settle(copies):
        for copy in copies:
            copy.wait_recv()

    def spread(src, land, size, count, target):
        position = {"x": x, "y": y}[target]
        where = {"x": at_x, "y": at_y}[target]
        return [
            push(src.at[pl.ds(((position + d) % count) * size, size)], land.at[d - 1], where(d))
            for d in range(1, count)
        ]

    def fold(out, first, land, count, offset, size, step):
        for i in range(0, size, step):
            total = first[pl.ds(offset + i, step)].astype(F32)
            for d in range(count - 1):
                total = total + land[d, i : i + step].astype(F32)
            out[i : i + step] = total.astype(BF16)

    w0, w1 = nz + 1, nz
    copies = spread(p0, s["r0"], ny * w0, nx, "x") + spread(p1, s["r1"], nx * w1, ny, "y")
    s["ew"][...] = jnp.zeros_like(s["ew"])
    for load in loads:
        load.wait()
    s["ew"][0 : OBSF + 1, :] = embed_w[...].astype(F32)
    s["kg"][...] = jnp.zeros_like(s["kg"])
    embed_m = s["ew"][...].astype(BF16)
    settle(copies)
    fold(s["q0"], p0, s["r0"], nx, x * (ny * w0), ny * w0, w0)
    fold(s["q1"], p1, s["r1"], ny, y * (nx * w1), nx * w1, w1)
    copies = spread(s["q0"], s["t0"], w0, ny, "y") + spread(s["q1"], s["t1"], w1, nx, "x")
    settle(copies)
    total0 = s["q0"][pl.ds(y * w0, w0)].astype(F32)
    for d in range(ny - 1):
        total0 = total0 + s["t0"][d].astype(F32)
    total0 = total0.astype(BF16)
    total1 = s["q1"][pl.ds(x * w1, w1)].astype(F32)
    for d in range(nx - 1):
        total1 = total1 + s["t1"][d].astype(F32)
    total1 = total1.astype(BF16)
    for k in range(nz):
        s["zbuf"][k, 0] = total0[k]
        s["zbuf"][k, 1] = total1[k]
        s["zbuf"][k, 2] = total0[nz]
    copies = [push(s["zbuf"].at[(z + d) % nz], s["zr"].at[d - 1], at_z(d)) for d in range(1, nz)]
    settle(copies)
    sums = s["zbuf"][z].astype(F32)
    for d in range(nz - 1):
        sums = sums + s["zr"][d].astype(F32)
    s["dens"][...] = sums[2]
    density = jnp.concatenate([s["dens"][pl.ds(z, 1), :], s["dens"][pl.ds(SIDE + z, 1), :]], axis=1)
    scaled = jnp.concatenate([sums[0], sums[1]], axis=1) * lax.rsqrt(1.0 + density)
    level = jnp.where(
        lax.broadcasted_iota(jnp.int32, (16, CH), 0) == 0,
        jnp.broadcast_to(0.25 * jnp.log(1.0 + density), (16, CH)), 0.0,
    )
    encoded = jnp.concatenate([scaled, level], axis=0).astype(BF16)

    grid_hat, grid_scale = normalise(dot(encoded, embed_m, TN))
    normed_grid = grid_hat.astype(BF16)
    first = jnp.zeros((CELLS, CH), F32)
    for i in range(4):
        first = first + dot(normed_grid[i * CELLS : (i + 1) * CELLS], patch_w[i * CH : (i + 1) * CH, :])
    state = first.astype(BF16)

    def halo_send(which, field):
        src, dst = s["halo_src%d" % which], s["halo_dst%d" % which]
        src[0] = field.astype(BF16)
        turned = jnp.swapaxes(field.reshape(SIDE, SIDE, CH), 0, 1)
        src[1] = turned.reshape(CELLS, CH).astype(BF16)
        corner, corners = s["corner"], s["halo_corner%d" % which]
        found = []
        for index, (i, j) in enumerate(HALOS):
            if j == 0:
                piece = src.at[0, pl.ds(32 if i > 0 else 0, 32)]
                found.append(push(piece, dst.at[index], at_halo(i, j)))
            elif i == 0:
                piece = src.at[1, pl.ds(32 if j > 0 else 0, 32)]
                found.append(push(piece, dst.at[index], at_halo(i, j)))
            else:
                for r in range(4):
                    q, p = (4 if j > 0 else 0) + r, 4 if i > 0 else 0
                    corner[r * 4 : r * 4 + 4, :] = turned[q][p : p + 4]
                slot = (i > 0) * 2 + (j > 0)
                corners[slot] = corner[...].astype(BF16)
                found.append(push(corners.at[slot], dst.at[index, pl.ds(0, 16)], at_halo(i, j)))
        return found

    def pad_inner(which, field):
        pad = s["pad%d" % which]
        pad[...] = jnp.zeros_like(pad)
        for p in range(SIDE):
            for h in range(2):
                pad[h, pl.ds((REACH + p) * PADW + REACH, SIDE), :] = field[
                    p * SIDE : (p + 1) * SIDE, h * 128 : (h + 1) * 128
                ]

    def halo_wait(which, copies):
        pad, dst = s["pad%d" % which], s["halo_dst%d" % which]
        settle(copies)
        for index, (i, j) in enumerate(HALOS):
            if j == 0:
                for r in range(REACH):
                    if i > 0:
                        row, at = r, 1 + r
                    else:
                        row, at = REACH + SIDE + r, r
                    strip = dst[index].astype(F32)[at * SIDE : (at + 1) * SIDE]
                    for h in range(2):
                        pad[h, pl.ds(row * PADW + REACH, SIDE), :] = strip[:, h * 128 : (h + 1) * 128]
                continue
            inside = (z > 0) if j > 0 else (z < nz - 1)
            keep = jnp.where(inside, 1.0, 0.0).astype(F32)
            block = (dst[index] if i == 0 else dst[index, 0:16, :]).astype(F32) * keep
            for r in range(REACH):
                if j > 0:
                    column, at = r, 1 + r
                else:
                    column, at = REACH + SIDE + r, r
                if i == 0:
                    top, strip = REACH, block[at * SIDE : (at + 1) * SIDE]
                elif i > 0:
                    top, strip = 0, block[at * 4 + 1 : at * 4 + 4]
                else:
                    top, strip = REACH + SIDE, block[at * 4 : at * 4 + REACH]
                for h in range(2):
                    pad[h, pl.ds(top * PADW + column, strip.shape[0], PADW), :] = strip[:, h * 128 : (h + 1) * 128]

    def window(which, column):
        pad = s["pad%d" % which]
        return jnp.stack(
            [
                jnp.concatenate([pad[h, pl.ds(p * PADW + column, SIDE), :] for h in range(2)], axis=1)
                for p in range(14)
            ],
            axis=0,
        )

    def taps_of(k):
        return [depth_k[tap].astype(F32)[k : k + 1].reshape(1, 1, CH) for tap in range(KSIDE * KSIDE)]

    def convolve(which, kernel, flip):
        total = jnp.zeros((SIDE, SIDE, CH), F32)
        for b in range(KSIDE):
            part = window(which, b)
            for a in range(KSIDE):
                tap = KSIDE * a + b
                if flip:
                    tap = KSIDE * KSIDE - 1 - tap
                total = total + part[a : a + SIDE] * kernel[tap]
        return total.reshape(CELLS, CH)

    def kernel_grad(which, grad):
        grad = grad.reshape(SIDE, SIDE, CH)
        for b in range(KSIDE):
            part = window(which, b)
            for a in range(KSIDE):
                s["tap"][KSIDE * a + b] = jnp.sum(part[a : a + SIDE] * grad, axis=0)
        taps = jnp.sum(s["tap"][...], axis=1)
        for h in range(2):
            s["kg"][h, pl.ds(which, KSIDE * KSIDE, 2), :] = taps[:, h * 128 : (h + 1) * 128]

    stored = []
    for k in range(2):
        field = state.astype(F32)
        copies = halo_send(k, field)
        pad_inner(k, field)
        kernel = taps_of(k)
        halo_wait(k, copies)
        hat, scale = normalise(convolve(k, kernel, False))
        normed = hat.astype(BF16)
        act = dot(normed, expand_w[k])
        share = cdf(act)
        hidden = (act * share).astype(BF16)
        state = (field + dot(hidden, reduce_w[k])).astype(BF16)
        slope = share + act * jnp.exp(-0.5 * jnp.square(act)) * (1.0 / math.sqrt(2.0 * math.pi))
        stored.append((hat, scale, normed, hidden, slope))
    feat[...] = state

    progress = {}

    def group(name):
        return next(entry for entry in GROUPS if entry[0] == name)

    def lines(name):
        _, n_p, n_q, _ = group(name)
        return (("p", n_p, nx, x, at_x, ny, y, at_y), ("q", n_q, ny, y, at_y, nx, x, at_x))

    def begin(name):
        found = []
        for d in [*range(1, max(nx, ny)), 0]:
            for key, n, count, place, _, _, _, _ in lines(name):
                if d < count:
                    size = n // count
                    at = pl.ds(((place + d) % count) * size, size)
                    found.append((key, d, push(s[name + "g" + key].at[1 - core, at], s[name + "c" + key].at[at], at_core())))
        progress[name] = found

    def stage_first(name):
        found = []
        info = {line[0]: line for line in lines(name)}
        for key, d, copy in progress[name]:
            _, n, count, place, where, _, _, _ = info[key]
            size = n // count
            copy.wait_recv()
            own, got, out = s[name + "g" + key], s[name + "c" + key], s[name + "s" + key]
            base = ((place + d) % count) * size
            step = math.gcd(8, size)
            for i in range(0, size, step):
                at = pl.ds(base + i, step)
                out[at] = (own[core, at].astype(F32) + got[at].astype(F32)).astype(BF16)
            if d:
                found.append(push(out.at[pl.ds(base, size)], s[name + "l1" + key].at[d - 1], where(d)))
        progress[name] = found

    def stage_second(name):
        settle(progress[name])
        found = []
        for key, n, first, place, _, second, place_2, where in lines(name):
            size, small = n // first, n // (first * second)
            own, land, out = s[name + "s" + key], s[name + "l1" + key], s[name + "s2" + key]
            for d in [*range(1, second), 0]:
                base = ((place_2 + d) % second) * small
                total = own[pl.ds(place * size + base, small)].astype(F32)
                for e in range(first - 1):
                    total = total + land[e, pl.ds(base, small)].astype(F32)
                out[pl.ds(base, small)] = total.astype(BF16)
                if d:
                    found.append(push(out.at[pl.ds(base, small)], s[name + "l2" + key].at[d - 1], where(d)))
        progress[name] = found

    def stage_third(name):
        _, n_p, n_q, scatter = group(name)
        up, uq = n_p // nlon, n_q // nlon
        settle(progress[name])
        s3 = s[name + "s3"]
        fold(s3.at[pl.ds(0, up)], s[name + "s2p"], s[name + "l2p"], ny, y * up, up, math.gcd(8, up))
        fold(s3.at[pl.ds(up, uq)], s[name + "s2q"], s[name + "l2q"], nx, x * uq, uq, math.gcd(8, uq))
        l3 = s[name + "l3"]
        if scatter:
            piece = (up + uq) // nz
            progress[name] = [
                push(s3.at[pl.ds(((z + d) % nz) * piece, piece)], l3.at[d - 1], at_z(d)) for d in range(1, nz)
            ]
        else:
            l3[z] = s3[...]
            progress[name] = [push(s3, l3.at[z], at_z(d), l3.at[(z + nz - d) % nz]) for d in range(1, nz)]

    def stage_gather(name):
        _, n_p, n_q, _ = group(name)
        piece = (n_p + n_q) // (nlon * nz)
        settle(progress[name])
        s3, l3, f3 = s[name + "s3"], s[name + "l3"], s[name + "f3"]
        total = s3[pl.ds(z * piece, piece)].astype(F32)
        for d in range(nz - 1):
            total = total + l3[d].astype(F32)
        f3[z] = total.astype(BF16)
        progress[name] = [push(f3.at[z], f3.at[z], at_z(d), f3.at[(z + nz - d) % nz]) for d in range(1, nz)]

    def stage_back_second(name):
        _, n_p, n_q, scatter = group(name)
        up, uq = n_p // nlon, n_q // nlon
        settle(progress[name])
        fp, fq = s[name + "fp"], s[name + "fq"]
        at_p, at_q = x * (n_p // nx) + y * up, y * (n_q // ny) + x * uq
        if scatter:
            done = s[name + "f3"][...].reshape(up + uq, 16, 128)
        else:
            total = s[name + "l3"][0].astype(F32)
            for d in range(1, nz):
                total = total + s[name + "l3"][d].astype(F32)
            done = total.astype(BF16)
        fp[core, pl.ds(at_p, up)] = done[:up]
        fq[core, pl.ds(at_q, uq)] = done[up:]

        def from_p(d):
            return fp.at[core, pl.ds(x * (n_p // nx) + ((y + ny - d) % ny) * up, up)]

        def from_q(d):
            return fq.at[core, pl.ds(y * (n_q // ny) + ((x + nx - d) % nx) * uq, uq)]

        progress[name] = [push(from_p(0), from_p(0), at_y(d), from_p(d)) for d in range(1, ny)]
        progress[name] += [push(from_q(0), from_q(0), at_x(d), from_q(d)) for d in range(1, nx)]

    def stage_back_first(name):
        settle(progress[name])
        found, handed = [], []
        for d in range(0, max(nx, ny)):
            for key, n, count, place, where, _, _, _ in lines(name):
                if d >= count:
                    continue
                size, whole = n // count, s[name + "f" + key]
                own = whole.at[core, pl.ds(place * size, size)]
                at = pl.ds(((place + count - d) % count) * size, size)
                if d:
                    found.append((whole, at, push(own, own, where(d), whole.at[core, at])))
                else:
                    handed.append((whole, at))
        hand_over(name, handed)
        progress[name] = (found, progress[name])

    def hand_over(name, handed):
        progress[name] = [
            push(whole.at[core, at], whole.at[core, at], at_core(), whole.at[1 - core, at]) for whole, at in handed
        ]

    def stage_back_core(name):
        found, earlier = progress[name]
        for whole, at, copy in found:
            copy.wait_recv()
            hand_over(name, [(whole, at)])
            earlier = earlier + progress[name]
        progress[name] = earlier

    def put_tall(name, left, right):
        for h in range(2):
            s[name + "gp"][h] = dot(left, right[:, h * 128 : (h + 1) * 128], TN).astype(BF16).reshape(64, 16, 128)

    def put_wide(name, left, right):
        for lane in range(8):
            part = dot(left, right[:, lane * 128 : (lane + 1) * 128], TN).astype(BF16)
            s[name + "gq"][lane // 4, (lane % 4) * 16 : (lane % 4 + 1) * 16] = part.reshape(16, 16, 128)

    cotangent = cot[...]
    for k in (1, 0):
        name = "A" if k == 1 else "B"
        hat, scale, normed, hidden, slope = stored[k]
        grad_act = (dot(cotangent, reduce_w[k], NT) * slope).astype(BF16)
        grad_depth = normalise_grad(hat, scale, dot(grad_act, expand_w[k], NT))
        copies = halo_send(2 + k, grad_depth)
        put_tall(name, hidden, cotangent)
        put_wide(name, normed, grad_act)
        begin(name)
        pad_inner(2 + k, grad_depth)
        kernel_grad(k, grad_depth)
        if k == 0:
            stage_second("A")
        stage_first(name)
        halo_wait(2 + k, copies)
        cotangent = (cotangent.astype(F32) + convolve(2 + k, taps_of(k), True)).astype(BF16)
    stage_third("A")
    stage_second("B")

    parts = []
    for i in range(4):
        piece = normed_grid[i * CELLS : (i + 1) * CELLS]
        grad = dot(piece, cotangent, TN).astype(BF16)
        for h in range(2):
            target = s["Cgp"] if i < 2 else s["Cgq"]
            target[h, (i % 2) * 16 : (i % 2 + 1) * 16] = grad[:, h * 128 : (h + 1) * 128].reshape(16, 16, 128)
        parts.append(dot(cotangent, patch_w[i * CH : (i + 1) * CH, :], NT))
    grad_grid = normalise_grad(grid_hat, grid_scale, jnp.concatenate(parts, axis=0)).astype(BF16)
    grad_embed = dot(encoded, grad_grid).astype(BF16)
    for h in range(2):
        s["Cgq"][h, 32:39] = s["kg"][h].astype(BF16).reshape(7, 16, 128)
        s["Cgq"][h, 39:41] = grad_embed[:, h * 128 : (h + 1) * 128].reshape(2, 16, 128)
        s["Cgq"][h, 41:48] = jnp.zeros((7, 16, 128), BF16)
    begin("C")
    stage_first("C")
    stage_third("B")
    stage_gather("A")
    stage_second("C")
    stage_back_second("A")
    stage_gather("B")
    stage_third("C")
    stage_back_first("A")
    stage_back_second("B")
    stage_back_second("C")
    stage_back_first("B")
    stage_back_first("C")
    stage_back_core("A")
    stage_back_core("B")
    stage_back_core("C")
    for name in ("A", "C", "B"):
        settle(progress[name])
    for copy in sent:
        copy.wait_send()


def widen_kernel(feat, afp, afq, bfp, bfq, cfp, cfq, *refs):
    outs, stage, rows, sems = refs[:6], refs[6:12], refs[12], refs[13]
    s_feat, s_embed, s_patch, s_kernel, s_expand, s_reduce = stage
    s_feat[...] = feat[...]
    pending = []

    def ship(src, dst):
        copy = pltpu.make_async_copy(src, dst, sems.at[len(pending)])
        copy.start()
        pending.append(copy)

    def block(units):
        return units.astype(F32).reshape(units.shape[0] * 16, 128)

    ship(s_feat, outs[0])
    for k, fp, fq in ((1, afp, afq), (0, bfp, bfq)):
        for r in range(0, 64, 16):
            for h in range(2):
                s_reduce[k, r * 16 : (r + 16) * 16, h * 128 : (h + 1) * 128] = block(fp[h, r : r + 16])
        ship(s_reduce.at[k], outs[5].at[k])
        for lane in range(8):
            s_expand[k, :, lane * 128 : (lane + 1) * 128] = block(fq[lane // 4, (lane % 4) * 16 : (lane % 4 + 1) * 16])
        ship(s_expand.at[k], outs[4].at[k])
    for source, base in ((cfp, 0), (cfq, 512)):
        for r in range(0, 32, 16):
            for h in range(2):
                at = slice(base + r * 16, base + (r + 16) * 16)
                s_patch[at, h * 128 : (h + 1) * 128] = block(source[h, r : r + 16])
    ship(s_patch, outs[2])
    for h in range(2):
        at = slice(h * 128, (h + 1) * 128)
        rows[...] = block(cfq[h, 32:39])
        for tap in range(KSIDE * KSIDE):
            s_kernel[tap, :, at] = rows[2 * tap : 2 * tap + 2, :]
        s_embed[:, at] = block(cfq[h, 39:41])[: OBSF + 1]
    ship(s_kernel, outs[3])
    ship(s_embed, outs[1])
    for copy in pending:
        copy.wait()


def factor(lon):
    nx = math.isqrt(lon)
    while lon % nx:
        nx -= 1
    return nx, lon // nx


def on_device(values, coords, dest, count, embed_w, patch_w, depth_k, expand_w, reduce_w, cot):
    nx, ny = factor(lax.axis_size("lon"))
    nz = lax.axis_size("lat")
    operands = (
        dest[0, 0], count[0, 0, 0], values[0, 0, 0], coords[0, 0, 0],
        embed_w, patch_w, jnp.transpose(depth_k, (1, 0, 2)), expand_w, reduce_w, cot[0].reshape(CELLS, CH),
    )
    plan = scratch_plan(nx, ny, nz, values.shape[3])
    copies = copy_count(nx, ny, nz)
    vmem = pl.BlockSpec(memory_space=pltpu.VMEM)
    finals = []
    for _, n_p, n_q, _ in GROUPS:
        finals += [jax.ShapeDtypeStruct((2, n, 16, 128), BF16) for n in (n_p, n_q)]
    handed = pl.pallas_call(
        functools.partial(net_kernel, nx, ny, nz, tuple(plan)),
        out_shape=(jax.ShapeDtypeStruct((CELLS, CH), BF16),) + tuple(finals),
        in_specs=[pl.BlockSpec(memory_space=pltpu.HBM)] * INPUTS,
        out_specs=(vmem,) * 7,
        scratch_shapes=list(plan.values())
        + [(pltpu.SMEM if i == 1 else pltpu.VMEM)(leaf.shape, leaf.dtype) for i, leaf in enumerate(operands)]
        + [pltpu.SemaphoreType.DMA((n,)) for n in (copies, copies, INPUTS + 2 * PARTS + 1)],
        compiler_params=pltpu.CompilerParams(
            collective_id=0, has_side_effects=True, vmem_limit_bytes=32 * 2**20
        ),
    )(*(in_hbm(leaf) for leaf in operands))
    shapes = (
        jax.ShapeDtypeStruct((CELLS, CH), BF16),
        jax.ShapeDtypeStruct((OBSF + 1, CH), F32),
        jax.ShapeDtypeStruct((4 * CH, CH), F32),
        jax.ShapeDtypeStruct((KSIDE * KSIDE, 2, CH), F32),
        jax.ShapeDtypeStruct((2, CH, HID), F32),
        jax.ShapeDtypeStruct((2, HID, CH), F32),
    )
    outs = pl.pallas_call(
        widen_kernel,
        out_shape=shapes,
        in_specs=[vmem] * 7,
        out_specs=(pl.BlockSpec(memory_space=pltpu.HBM),) * 6,
        scratch_shapes=[pltpu.VMEM(leaf.shape, leaf.dtype) for leaf in shapes]
        + [pltpu.VMEM((112, 128), F32), pltpu.SemaphoreType.DMA((8,))],
        compiler_params=pltpu.CompilerParams(vmem_limit_bytes=24 * 2**20),
    )(*handed)
    return (
        outs[0].reshape(1, SIDE, SIDE, CH), outs[1], outs[2], jnp.transpose(outs[3], (1, 0, 2)), outs[4], outs[5],
    )


def solution(mesh):
    in_specs = (
        P("dp", "lon", "lat", None, None, None),
        P("dp", "lon", "lat", None, None, None),
        P("dp", "lon", "lat", None),
        P("dp", "lon", "lat", None),
        P(),
        P(),
        P(),
        P(),
        P(),
        P("dp", "lon", "lat", None),
    )
    out_specs = (P("dp", "lon", "lat", None), P(), P(), P(), P(), P())
    return jax.shard_map(
        on_device, mesh=mesh, in_specs=in_specs, out_specs=out_specs, check_vma=False
    )
```

```python
import functools
import math

import jax
import jax.numpy as jnp
from jax import lax
from jax.experimental import pallas as pl
from jax.experimental.pallas import tpu as pltpu
from jax.sharding import PartitionSpec as P

MESH = pl.DeviceIdType.MESH
F32 = jnp.float32
BF16 = jnp.bfloat16
OBSF = 16
KSIDE = 7
REACH = 3
TILE = 16
SIDE = 8
CELLS = 64
CH = 256
HID = 1024
INVERSE = 0.5 / (0.7 * 0.7)
PADW = 16
NT = (((1,), (1,)), ((), ()))
TN = (((0,), (0,)), ((), ()))


def dot(a, b, dims=(((1,), (0,)), ((), ()))):
    return lax.dot_general(a, b, dims, preferred_element_type=F32)


PARTS = 4
SLOTS = 128


def in_hbm(array):
    return pltpu.with_memory_space_constraint(array, pltpu.HBM)


def encode_block(block, count_ref, values_ref, coords_ref):
    rows = values_ref.shape[2]
    order = lax.broadcasted_iota(jnp.int32, (TILE, rows), 0)
    cell = (2 * (order % SIDE) + order // SIDE).astype(F32)
    lane = lax.broadcasted_iota(jnp.int32, (TILE, rows), 1)
    pair = coords_ref[block]
    a = jnp.exp(-jnp.square(pair[0:1, :] - cell) * INVERSE)
    a = jnp.where(lane < count_ref[block], a, 0.0)
    b = jnp.exp(-jnp.square(pair[1:2, :] - cell) * INVERSE)
    parts = []
    for i in range(2):
        for j in range(2):
            left = a[i * SIDE : (i + 1) * SIDE]
            right = b[j * SIDE : (j + 1) * SIDE].astype(BF16)
            right = jnp.concatenate([right, right], axis=0)
            for p in range(0, SIDE, 2):
                pair_of = [jnp.broadcast_to(left[p + n : p + n + 1], (SIDE, rows)) for n in range(2)]
                parts.append(jnp.concatenate(pair_of, axis=0).astype(BF16) * right)
    weight = jnp.concatenate(parts, axis=0)
    ones = jnp.ones((OBSF, rows), BF16)
    return dot(jnp.concatenate([values_ref[block], ones], axis=0), weight, NT)


def encode_part(part, share, count_ref, values_ref, coords_ref, res0, res1, resd):
    def body(block, carry):
        sums = encode_block(block, count_ref, values_ref, coords_ref)
        res0[block + 1] = sums[:OBSF, :128].astype(BF16)
        res1[block + 1] = sums[:OBSF, 128:].astype(BF16)
        resd[block + 1, 0:1, :] = sums[OBSF : OBSF + 1, :128]
        resd[block + 1, 1:2, :] = sums[OBSF : OBSF + 1, 128:]
        return carry

    lax.fori_loop(part * share, (part + 1) * share, body, 0, unroll=share)


def slot_of_tile(dest, blocks):
    row = lax.broadcasted_iota(jnp.int32, (blocks, blocks), 0)
    column = lax.broadcasted_iota(jnp.int32, (blocks, blocks), 1)
    spread = jnp.where(row == column, jnp.broadcast_to(dest, (blocks, blocks)), 0)
    upright = jnp.sum(spread, axis=1, keepdims=True)
    tile = lax.broadcasted_iota(jnp.int32, (blocks, SLOTS), 1)
    number = lax.broadcasted_iota(jnp.int32, (blocks, SLOTS), 0) + 1
    return jnp.minimum(jnp.sum(jnp.where(upright == tile, number, 0), axis=0, keepdims=True), blocks)


def normalise(field):
    center = jnp.mean(field, axis=-1, keepdims=True)
    shifted = field - center
    scale = lax.rsqrt(jnp.mean(jnp.square(shifted), axis=-1, keepdims=True) + 1e-05)
    return shifted * scale, scale


def normalise_grad(normed, scale, grad):
    return scale * (
        grad
        - jnp.mean(grad, axis=-1, keepdims=True)
        - normed * jnp.mean(grad * normed, axis=-1, keepdims=True)
    )


def cdf(field):
    return 0.5 * (1.0 + lax.erf(field * math.sqrt(0.5)))


def group_sizes(nx, ny, nz, np_half, nq_half):
    return np_half // (nx * ny), nq_half // (nx * ny)


def group_scratch(nx, ny, nz, n_p, n_q, scatter):
    up, uq = n_p // (nx * ny), n_q // (nx * ny)

    def units(*lead):
        return pltpu.VMEM(tuple(lead) + (16, 128), BF16)

    plan = {
        "gp": units(2, n_p), "gq": units(2, n_q),
        "cp": units(n_p), "cq": units(n_q),
        "sp": units(n_p), "sq": units(n_q),
        "l1p": units(nx - 1, n_p // nx), "l1q": units(ny - 1, n_q // ny),
        "s2p": units(n_p // nx), "s2q": units(n_q // ny),
        "l2p": units(ny - 1, up), "l2q": units(nx - 1, uq),
        "s3": units(up + uq),
    }
    if scatter:
        piece = (up + uq) // nz
        plan["l3"] = units(nz - 1, piece)
        plan["f3"] = units(nz, piece)
    else:
        plan["l3"] = units(nz, up + uq)
    return plan


GROUPS = (("A", 64, 64, True), ("B", 64, 64, True), ("C", 32, 48, False))


def scratch_plan(nx, ny, nz, blocks):
    def units(*lead):
        return pltpu.VMEM(tuple(lead) + (16, 128), BF16)

    lon = nx * ny
    plan = {
        "p0": units(lon * (nz + 1)), "p1": units(lon * nz),
        "res0": units(blocks + 1), "res1": units(blocks + 1),
        "resd": pltpu.VMEM((blocks + 1, 2, 128), F32),
        "densities": pltpu.VMEM((lon, 16, 128), F32),
        "slots_v": pltpu.VMEM((1, SLOTS), jnp.int32),
        "slots": pltpu.SMEM((1, SLOTS), jnp.int32),
        "corner": pltpu.VMEM((16, CH), F32),
        "r0": units(nx - 1, ny * (nz + 1)), "r1": units(ny - 1, nx * nz),
        "q0": units(ny * (nz + 1)), "q1": units(nx * nz),
        "t0": units(ny - 1, nz + 1), "t1": units(nx - 1, nz),
        "zbuf": units(nz, 3), "zr": units(nz - 1, 3),
        "dens": pltpu.VMEM((16, 128), F32),
        "ew": pltpu.VMEM((32, CH), F32),
        "kg": pltpu.VMEM((2, 112, 128), F32),
        "tap": pltpu.VMEM((KSIDE * KSIDE, 8, CH), F32),
    }
    for k in range(4):
        plan["halo_src%d" % k] = pltpu.VMEM((2, CELLS, CH), BF16)
        plan["halo_corner%d" % k] = pltpu.VMEM((4, 16, CH), BF16)
        plan["halo_dst%d" % k] = pltpu.VMEM((8, CELLS // 2, CH), BF16)
        plan["pad%d" % k] = pltpu.VMEM((2, 14 * PADW, 128), F32)
    plan["cols"] = pltpu.VMEM((CELLS, CH), F32)
    for name, n_p, n_q, scatter in GROUPS:
        for key, value in group_scratch(nx, ny, nz, n_p, n_q, scatter).items():
            plan[name + key] = value
    return plan


def copy_count(nx, ny, nz):
    total = 2 * (nx + ny - 2) + (nz - 1) + 4 * 8
    for _, _, _, scatter in GROUPS:
        total += 2 * (nx + ny) + 4 * (nx + ny - 2) + (nz - 1) * (2 if scatter else 1)
    return total


INPUTS = 10
FINALS = ("Afp", "Afq", "Bfp", "Bfq", "Cfp", "Cfq")
HALOS = tuple((i, j) for i in (-1, 0, 1) for j in (-1, 0, 1) if (i, j) != (0, 0))


def net_kernel(nx, ny, nz, names, *refs):
    far, feat, rest = refs[:INPUTS], refs[INPUTS], refs[INPUTS + 1 :]
    s = dict(zip(FINALS, rest[: len(FINALS)]))
    rest = rest[len(FINALS) :]
    s.update(zip(names, rest))
    rest = rest[len(names) :]
    near = rest[:INPUTS]
    dest_ref, count_ref, values_ref, coords_ref, embed_w, patch_w, depth_k, expand_w, reduce_w, cot = near
    send_sem, recv_sem, load_sem = rest[INPUTS:]
    blocks = values_ref.shape[0]
    parts = PARTS if blocks % PARTS == 0 else 1
    share = blocks // parts
    first_loads = [pltpu.make_async_copy(far[i], near[i], load_sem.at[i]) for i in range(2)]
    block_loads = []
    for part in range(parts):
        at = pl.ds(part * share, share)
        block_loads.append(
            [
                pltpu.make_async_copy(far[i].at[at], near[i].at[at], load_sem.at[i + 2 * part])
                for i in (2, 3)
            ]
        )
    loads = [
        pltpu.make_async_copy(far[i], near[i], load_sem.at[i + 2 * PARTS]) for i in range(4, INPUTS)
    ]
    slot_load = pltpu.make_async_copy(s["slots_v"], s["slots"], load_sem.at[INPUTS + 2 * PARTS])
    for load in first_loads + [load for part in block_loads for load in part]:
        load.start()
    core = lax.axis_index("dp")
    lon = lax.axis_index("lon")
    z = lax.axis_index("lat")
    x = lon // ny
    y = lon % ny
    nlon = nx * ny

    def at_core():
        return (1 - core, lon, z)

    def at_x(d):
        return (core, ((x + d) % nx) * ny + y, z)

    def at_y(d):
        return (core, x * ny + (y + d) % ny, z)

    def at_z(d):
        return (core, lon, (z + d) % nz)

    def at_halo(i, j):
        return (core, (lon + i + nlon) % nlon, (z + j + nz) % nz)

    barrier = pltpu.get_barrier_semaphore()
    peers = [at_core()] + [at_x(d) for d in range(1, nx)] + [at_y(d) for d in range(1, ny)]
    peers += [at_z(d) for d in range(1, nz)] + [at_halo(i, j) for i, j in HALOS]
    for peer in peers:
        pl.semaphore_signal(barrier, inc=1, device_id=peer, device_id_type=MESH)
    for load in loads:
        load.start()

    for load in first_loads:
        load.wait()
    s["slots_v"][...] = slot_of_tile(dest_ref[...], blocks)
    slot_load.start()
    res0, res1, resd = s["res0"], s["res1"], s["resd"]
    res0[0] = jnp.zeros((16, 128), BF16)
    res1[0] = jnp.zeros((16, 128), BF16)
    resd[0] = jnp.zeros((2, 128), F32)
    for part in range(parts):
        for load in block_loads[part]:
            load.wait()
        encode_part(part, share, count_ref, values_ref, coords_ref, res0, res1, resd)
    slot_load.wait()
    p0, p1, densities = s["p0"], s["p1"], s["densities"]

    def fill(tile_lon, carry):
        tile_x, tile_y = tile_lon // ny, tile_lon % ny
        for tile_z in range(nz):
            slot = jnp.clip(s["slots"][0, tile_lon * nz + tile_z], 0, blocks)
            p0[tile_lon * (nz + 1) + tile_z] = res0[slot]
            p1[(tile_y * nx + tile_x) * nz + tile_z] = res1[slot]
            density = resd[slot]
            densities[tile_lon, tile_z : tile_z + 1, :] = density[0:1]
            densities[tile_lon, SIDE + tile_z : SIDE + tile_z + 1, :] = density[1:2]
        p0[tile_lon * (nz + 1) + nz] = densities[tile_lon].astype(BF16)
        return carry

    if nz < SIDE:
        densities[...] = jnp.zeros_like(densities)
    lax.fori_loop(0, nlon, fill, 0, unroll=2)
    pl.semaphore_wait(barrier, len(peers))

    sent = []

    def push(src, dst, device, land=None):
        index = len(sent)

        def make(target):
            return pltpu.make_async_remote_copy(
                src_ref=src, dst_ref=target, send_sem=send_sem.at[index], recv_sem=recv_sem.at[index],
                device_id=device, device_id_type=MESH,
            )

        copy = make(dst)
        copy.start()
        sent.append(copy)
        return copy if land is None else make(land)

    def settle(copies):
        for copy in copies:
            copy.wait_recv()

    def spread(src, land, size, count, target):
        position = {"x": x, "y": y}[target]
        where = {"x": at_x, "y": at_y}[target]
        return [
            push(src.at[pl.ds(((position + d) % count) * size, size)], land.at[d - 1], where(d))
            for d in range(1, count)
        ]

    def fold(out, first, land, count, offset, size, step):
        for i in range(0, size, step):
            total = first[pl.ds(offset + i, step)].astype(F32)
            for d in range(count - 1):
                total = total + land[d, i : i + step].astype(F32)
            out[i : i + step] = total.astype(BF16)

    w0, w1 = nz + 1, nz
    copies = spread(p0, s["r0"], ny * w0, nx, "x") + spread(p1, s["r1"], nx * w1, ny, "y")
    s["ew"][...] = jnp.zeros_like(s["ew"])
    for load in loads:
        load.wait()
    s["ew"][0 : OBSF + 1, :] = embed_w[...].astype(F32)
    s["kg"][...] = jnp.zeros_like(s["kg"])
    embed_m = s["ew"][...].astype(BF16)
    settle(copies)
    fold(s["q0"], p0, s["r0"], nx, x * (ny * w0), ny * w0, w0)
    fold(s["q1"], p1, s["r1"], ny, y * (nx * w1), nx * w1, w1)
    copies = spread(s["q0"], s["t0"], w0, ny, "y") + spread(s["q1"], s["t1"], w1, nx, "x")
    settle(copies)
    total0 = s["q0"][pl.ds(y * w0, w0)].astype(F32)
    for d in range(ny - 1):
        total0 = total0 + s["t0"][d].astype(F32)
    total0 = total0.astype(BF16)
    total1 = s["q1"][pl.ds(x * w1, w1)].astype(F32)
    for d in range(nx - 1):
        total1 = total1 + s["t1"][d].astype(F32)
    total1 = total1.astype(BF16)
    for k in range(nz):
        s["zbuf"][k, 0] = total0[k]
        s["zbuf"][k, 1] = total1[k]
        s["zbuf"][k, 2] = total0[nz]
    copies = [push(s["zbuf"].at[(z + d) % nz], s["zr"].at[d - 1], at_z(d)) for d in range(1, nz)]
    settle(copies)
    sums = s["zbuf"][z].astype(F32)
    for d in range(nz - 1):
        sums = sums + s["zr"][d].astype(F32)
    s["dens"][...] = sums[2]
    density = jnp.concatenate([s["dens"][pl.ds(z, 1), :], s["dens"][pl.ds(SIDE + z, 1), :]], axis=1)
    scaled = jnp.concatenate([sums[0], sums[1]], axis=1) * lax.rsqrt(1.0 + density)
    level = jnp.where(
        lax.broadcasted_iota(jnp.int32, (16, CH), 0) == 0,
        jnp.broadcast_to(0.25 * jnp.log(1.0 + density), (16, CH)), 0.0,
    )
    encoded = jnp.concatenate([scaled, level], axis=0).astype(BF16)

    grid_hat, grid_scale = normalise(dot(encoded, embed_m, TN))
    normed_grid = grid_hat.astype(BF16)
    first = jnp.zeros((CELLS, CH), F32)
    for i in range(4):
        first = first + dot(normed_grid[i * CELLS : (i + 1) * CELLS], patch_w[i * CH : (i + 1) * CH, :])
    state = first.astype(BF16)

    def halo_send(which, field):
        src, dst = s["halo_src%d" % which], s["halo_dst%d" % which]
        src[0] = field.astype(BF16)
        turned = jnp.swapaxes(field.reshape(SIDE, SIDE, CH), 0, 1)
        src[1] = turned.reshape(CELLS, CH).astype(BF16)
        corner, corners = s["corner"], s["halo_corner%d" % which]
        found = []
        for index, (i, j) in enumerate(HALOS):
            if j == 0:
                piece = src.at[0, pl.ds(32 if i > 0 else 0, 32)]
                found.append(push(piece, dst.at[index], at_halo(i, j)))
            elif i == 0:
                piece = src.at[1, pl.ds(32 if j > 0 else 0, 32)]
                found.append(push(piece, dst.at[index], at_halo(i, j)))
            else:
                for r in range(4):
                    q, p = (4 if j > 0 else 0) + r, 4 if i > 0 else 0
                    corner[r * 4 : r * 4 + 4, :] = turned[q][p : p + 4]
                slot = (i > 0) * 2 + (j > 0)
                corners[slot] = corner[...].astype(BF16)
                found.append(push(corners.at[slot], dst.at[index, pl.ds(0, 16)], at_halo(i, j)))
        return found

    def pad_inner(which, field):
        pad = s["pad%d" % which]
        pad[...] = jnp.zeros_like(pad)
        for p in range(SIDE):
            for h in range(2):
                pad[h, pl.ds((REACH + p) * PADW + REACH, SIDE), :] = field[
                    p * SIDE : (p + 1) * SIDE, h * 128 : (h + 1) * 128
                ]

    def halo_wait(which, copies):
        pad, dst = s["pad%d" % which], s["halo_dst%d" % which]
        settle(copies)
        for index, (i, j) in enumerate(HALOS):
            if j == 0:
                for r in range(REACH):
                    if i > 0:
                        row, at = r, 1 + r
                    else:
                        row, at = REACH + SIDE + r, r
                    strip = dst[index].astype(F32)[at * SIDE : (at + 1) * SIDE]
                    for h in range(2):
                        pad[h, pl.ds(row * PADW + REACH, SIDE), :] = strip[:, h * 128 : (h + 1) * 128]
                continue
            inside = (z > 0) if j > 0 else (z < nz - 1)
            keep = jnp.where(inside, 1.0, 0.0).astype(F32)
            block = (dst[index] if i == 0 else dst[index, 0:16, :]).astype(F32) * keep
            for r in range(REACH):
                if j > 0:
                    column, at = r, 1 + r
                else:
                    column, at = REACH + SIDE + r, r
                if i == 0:
                    top, strip = REACH, block[at * SIDE : (at + 1) * SIDE]
                elif i > 0:
                    top, strip = 0, block[at * 4 + 1 : at * 4 + 4]
                else:
                    top, strip = REACH + SIDE, block[at * 4 : at * 4 + REACH]
                for h in range(2):
                    pad[h, pl.ds(top * PADW + column, strip.shape[0], PADW), :] = strip[:, h * 128 : (h + 1) * 128]

    def window(which, column):
        pad = s["pad%d" % which]
        return jnp.stack(
            [
                jnp.concatenate([pad[h, pl.ds(p * PADW + column, SIDE), :] for h in range(2)], axis=1)
                for p in range(14)
            ],
            axis=0,
        )

    def taps_of(k):
        return [depth_k[tap].astype(F32)[k : k + 1].reshape(1, 1, CH) for tap in range(KSIDE * KSIDE)]

    def convolve(which, kernel, flip):
        total = jnp.zeros((SIDE, SIDE, CH), F32)
        for b in range(KSIDE):
            part = window(which, b)
            for a in range(KSIDE):
                tap = KSIDE * a + b
                if flip:
                    tap = KSIDE * KSIDE - 1 - tap
                total = total + part[a : a + SIDE] * kernel[tap]
        return total.reshape(CELLS, CH)

    def kernel_grad(which, grad):
        grad = grad.reshape(SIDE, SIDE, CH)
        for b in range(KSIDE):
            part = window(which, b)
            for a in range(KSIDE):
                s["tap"][KSIDE * a + b] = jnp.sum(part[a : a + SIDE] * grad, axis=0)
        taps = jnp.sum(s["tap"][...], axis=1)
        for h in range(2):
            s["kg"][h, pl.ds(which, KSIDE * KSIDE, 2), :] = taps[:, h * 128 : (h + 1) * 128]

    stored = []
    for k in range(2):
        field = state.astype(F32)
        copies = halo_send(k, field)
        pad_inner(k, field)
        kernel = taps_of(k)
        halo_wait(k, copies)
        hat, scale = normalise(convolve(k, kernel, False))
        normed = hat.astype(BF16)
        act = dot(normed, expand_w[k])
        share = cdf(act)
        hidden = (act * share).astype(BF16)
        state = (field + dot(hidden, reduce_w[k])).astype(BF16)
        slope = share + act * jnp.exp(-0.5 * jnp.square(act)) * (1.0 / math.sqrt(2.0 * math.pi))
        stored.append((hat, scale, normed, hidden, slope))
    feat[...] = state

    progress = {}

    def group(name):
        return next(entry for entry in GROUPS if entry[0] == name)

    def lines(name):
        _, n_p, n_q, _ = group(name)
        return (("p", n_p, nx, x, at_x, ny, y, at_y), ("q", n_q, ny, y, at_y, nx, x, at_x))

    def begin(name):
        found = []
        for d in [*range(1, max(nx, ny)), 0]:
            for key, n, count, place, _, _, _, _ in lines(name):
                if d < count:
                    size = n // count
                    at = pl.ds(((place + d) % count) * size, size)
                    found.append((key, d, push(s[name + "g" + key].at[1 - core, at], s[name + "c" + key].at[at], at_core())))
        progress[name] = found

    def stage_first(name):
        found = []
        info = {line[0]: line for line in lines(name)}
        for key, d, copy in progress[name]:
            _, n, count, place, where, _, _, _ = info[key]
            size = n // count
            copy.wait_recv()
            own, got, out = s[name + "g" + key], s[name + "c" + key], s[name + "s" + key]
            base = ((place + d) % count) * size
            step = math.gcd(8, size)
            for i in range(0, size, step):
                at = pl.ds(base + i, step)
                out[at] = (own[core, at].astype(F32) + got[at].astype(F32)).astype(BF16)
            if d:
                found.append(push(out.at[pl.ds(base, size)], s[name + "l1" + key].at[d - 1], where(d)))
        progress[name] = found

    def stage_second(name):
        settle(progress[name])
        found = []
        for key, n, first, place, _, second, place_2, where in lines(name):
            size, small = n // first, n // (first * second)
            own, land, out = s[name + "s" + key], s[name + "l1" + key], s[name + "s2" + key]
            for d in [*range(1, second), 0]:
                base = ((place_2 + d) % second) * small
                total = own[pl.ds(place * size + base, small)].astype(F32)
                for e in range(first - 1):
                    total = total + land[e, pl.ds(base, small)].astype(F32)
                out[pl.ds(base, small)] = total.astype(BF16)
                if d:
                    found.append(push(out.at[pl.ds(base, small)], s[name + "l2" + key].at[d - 1], where(d)))
        progress[name] = found

    def stage_third(name):
        _, n_p, n_q, scatter = group(name)
        up, uq = n_p // nlon, n_q // nlon
        settle(progress[name])
        s3 = s[name + "s3"]
        fold(s3.at[pl.ds(0, up)], s[name + "s2p"], s[name + "l2p"], ny, y * up, up, math.gcd(8, up))
        fold(s3.at[pl.ds(up, uq)], s[name + "s2q"], s[name + "l2q"], nx, x * uq, uq, math.gcd(8, uq))
        l3 = s[name + "l3"]
        if scatter:
            piece = (up + uq) // nz
            progress[name] = [
                push(s3.at[pl.ds(((z + d) % nz) * piece, piece)], l3.at[d - 1], at_z(d)) for d in range(1, nz)
            ]
        else:
            l3[z] = s3[...]
            progress[name] = [push(s3, l3.at[z], at_z(d), l3.at[(z + nz - d) % nz]) for d in range(1, nz)]

    def stage_gather(name):
        _, n_p, n_q, _ = group(name)
        piece = (n_p + n_q) // (nlon * nz)
        settle(progress[name])
        s3, l3, f3 = s[name + "s3"], s[name + "l3"], s[name + "f3"]
        total = s3[pl.ds(z * piece, piece)].astype(F32)
        for d in range(nz - 1):
            total = total + l3[d].astype(F32)
        f3[z] = total.astype(BF16)
        progress[name] = [push(f3.at[z], f3.at[z], at_z(d), f3.at[(z + nz - d) % nz]) for d in range(1, nz)]

    def stage_back_second(name):
        _, n_p, n_q, scatter = group(name)
        up, uq = n_p // nlon, n_q // nlon
        settle(progress[name])
        fp, fq = s[name + "fp"], s[name + "fq"]
        at_p, at_q = x * (n_p // nx) + y * up, y * (n_q // ny) + x * uq
        if scatter:
            done = s[name + "f3"][...].reshape(up + uq, 16, 128)
        else:
            total = s[name + "l3"][0].astype(F32)
            for d in range(1, nz):
                total = total + s[name + "l3"][d].astype(F32)
            done = total.astype(BF16)
        fp[core, pl.ds(at_p, up)] = done[:up]
        fq[core, pl.ds(at_q, uq)] = done[up:]

        def from_p(d):
            return fp.at[core, pl.ds(x * (n_p // nx) + ((y + ny - d) % ny) * up, up)]

        def from_q(d):
            return fq.at[core, pl.ds(y * (n_q // ny) + ((x + nx - d) % nx) * uq, uq)]

        progress[name] = [push(from_p(0), from_p(0), at_y(d), from_p(d)) for d in range(1, ny)]
        progress[name] += [push(from_q(0), from_q(0), at_x(d), from_q(d)) for d in range(1, nx)]

    def stage_back_first(name):
        settle(progress[name])
        found, handed = [], []
        for d in range(0, max(nx, ny)):
            for key, n, count, place, where, _, _, _ in lines(name):
                if d >= count:
                    continue
                size, whole = n // count, s[name + "f" + key]
                own = whole.at[core, pl.ds(place * size, size)]
                at = pl.ds(((place + count - d) % count) * size, size)
                if d:
                    found.append((whole, at, push(own, own, where(d), whole.at[core, at])))
                else:
                    handed.append((whole, at))
        hand_over(name, handed)
        progress[name] = (found, progress[name])

    def hand_over(name, handed):
        progress[name] = [
            push(whole.at[core, at], whole.at[core, at], at_core(), whole.at[1 - core, at]) for whole, at in handed
        ]

    def stage_back_core(name):
        found, earlier = progress[name]
        for whole, at, copy in found:
            copy.wait_recv()
            hand_over(name, [(whole, at)])
            earlier = earlier + progress[name]
        progress[name] = earlier

    def put_tall(name, left, right):
        for h in range(2):
            s[name + "gp"][h] = dot(left, right[:, h * 128 : (h + 1) * 128], TN).astype(BF16).reshape(64, 16, 128)

    def put_wide(name, left, right):
        for lane in range(8):
            part = dot(left, right[:, lane * 128 : (lane + 1) * 128], TN).astype(BF16)
            s[name + "gq"][lane // 4, (lane % 4) * 16 : (lane % 4 + 1) * 16] = part.reshape(16, 16, 128)

    cotangent = cot[...]
    for k in (1, 0):
        name = "A" if k == 1 else "B"
        hat, scale, normed, hidden, slope = stored[k]
        grad_act = (dot(cotangent, reduce_w[k], NT) * slope).astype(BF16)
        grad_depth = normalise_grad(hat, scale, dot(grad_act, expand_w[k], NT))
        copies = halo_send(2 + k, grad_depth)
        if k == 0:
            stage_second("A")
        put_tall(name, hidden, cotangent)
        put_wide(name, normed, grad_act)
        begin(name)
        pad_inner(2 + k, grad_depth)
        kernel_grad(k, grad_depth)
        stage_first(name)
        if k == 0:
            stage_third("A")
        halo_wait(2 + k, copies)
        cotangent = (cotangent.astype(F32) + convolve(2 + k, taps_of(k), True)).astype(BF16)
    stage_second("B")

    parts = []
    for i in range(4):
        piece = normed_grid[i * CELLS : (i + 1) * CELLS]
        grad = dot(piece, cotangent, TN).astype(BF16)
        for h in range(2):
            target = s["Cgp"] if i < 2 else s["Cgq"]
            target[h, (i % 2) * 16 : (i % 2 + 1) * 16] = grad[:, h * 128 : (h + 1) * 128].reshape(16, 16, 128)
        parts.append(dot(cotangent, patch_w[i * CH : (i + 1) * CH, :], NT))
    grad_grid = normalise_grad(grid_hat, grid_scale, jnp.concatenate(parts, axis=0)).astype(BF16)
    grad_embed = dot(encoded, grad_grid).astype(BF16)
    for h in range(2):
        s["Cgq"][h, 32:39] = s["kg"][h].astype(BF16).reshape(7, 16, 128)
        s["Cgq"][h, 39:41] = grad_embed[:, h * 128 : (h + 1) * 128].reshape(2, 16, 128)
        s["Cgq"][h, 41:48] = jnp.zeros((7, 16, 128), BF16)
    begin("C")
    stage_first("C")
    stage_gather("A")
    stage_third("B")
    stage_second("C")
    stage_back_second("A")
    stage_gather("B")
    stage_third("C")
    stage_back_first("A")
    stage_back_second("B")
    stage_back_second("C")
    stage_back_first("B")
    stage_back_first("C")
    stage_back_core("A")
    stage_back_core("B")
    stage_back_core("C")
    for name in ("A", "C", "B"):
        settle(progress[name])
    for copy in sent:
        copy.wait_send()


def widen_kernel(feat, afp, afq, bfp, bfq, cfp, cfq, *refs):
    outs, stage, rows, sems = refs[:6], refs[6:12], refs[12], refs[13]
    s_feat, s_embed, s_patch, s_kernel, s_expand, s_reduce = stage
    s_feat[...] = feat[...]
    pending = []

    def ship(src, dst):
        copy = pltpu.make_async_copy(src, dst, sems.at[len(pending)])
        copy.start()
        pending.append(copy)

    def block(units):
        return units.astype(F32).reshape(units.shape[0] * 16, 128)

    ship(s_feat, outs[0])
    for k, fp, fq in ((1, afp, afq), (0, bfp, bfq)):
        for r in range(0, 64, 16):
            for h in range(2):
                s_reduce[k, r * 16 : (r + 16) * 16, h * 128 : (h + 1) * 128] = block(fp[h, r : r + 16])
        ship(s_reduce.at[k], outs[5].at[k])
        for lane in range(8):
            s_expand[k, :, lane * 128 : (lane + 1) * 128] = block(fq[lane // 4, (lane % 4) * 16 : (lane % 4 + 1) * 16])
        ship(s_expand.at[k], outs[4].at[k])
    for source, base in ((cfp, 0), (cfq, 512)):
        for r in range(0, 32, 16):
            for h in range(2):
                at = slice(base + r * 16, base + (r + 16) * 16)
                s_patch[at, h * 128 : (h + 1) * 128] = block(source[h, r : r + 16])
    ship(s_patch, outs[2])
    for h in range(2):
        at = slice(h * 128, (h + 1) * 128)
        rows[...] = block(cfq[h, 32:39])
        for tap in range(KSIDE * KSIDE):
            s_kernel[tap, :, at] = rows[2 * tap : 2 * tap + 2, :]
        s_embed[:, at] = block(cfq[h, 39:41])[: OBSF + 1]
    ship(s_kernel, outs[3])
    ship(s_embed, outs[1])
    for copy in pending:
        copy.wait()


def factor(lon):
    nx = math.isqrt(lon)
    while lon % nx:
        nx -= 1
    return nx, lon // nx


def on_device(values, coords, dest, count, embed_w, patch_w, depth_k, expand_w, reduce_w, cot):
    nx, ny = factor(lax.axis_size("lon"))
    nz = lax.axis_size("lat")
    operands = (
        dest[0, 0], count[0, 0, 0], values[0, 0, 0], coords[0, 0, 0],
        embed_w, patch_w, jnp.transpose(depth_k, (1, 0, 2)), expand_w, reduce_w, cot[0].reshape(CELLS, CH),
    )
    plan = scratch_plan(nx, ny, nz, values.shape[3])
    copies = copy_count(nx, ny, nz)
    vmem = pl.BlockSpec(memory_space=pltpu.VMEM)
    finals = []
    for _, n_p, n_q, _ in GROUPS:
        finals += [jax.ShapeDtypeStruct((2, n, 16, 128), BF16) for n in (n_p, n_q)]
    handed = pl.pallas_call(
        functools.partial(net_kernel, nx, ny, nz, tuple(plan)),
        out_shape=(jax.ShapeDtypeStruct((CELLS, CH), BF16),) + tuple(finals),
        in_specs=[pl.BlockSpec(memory_space=pltpu.HBM)] * INPUTS,
        out_specs=(vmem,) * 7,
        scratch_shapes=list(plan.values())
        + [(pltpu.SMEM if i == 1 else pltpu.VMEM)(leaf.shape, leaf.dtype) for i, leaf in enumerate(operands)]
        + [pltpu.SemaphoreType.DMA((n,)) for n in (copies, copies, INPUTS + 2 * PARTS + 1)],
        compiler_params=pltpu.CompilerParams(
            collective_id=0, has_side_effects=True, vmem_limit_bytes=32 * 2**20
        ),
    )(*(in_hbm(leaf) for leaf in operands))
    shapes = (
        jax.ShapeDtypeStruct((CELLS, CH), BF16),
        jax.ShapeDtypeStruct((OBSF + 1, CH), F32),
        jax.ShapeDtypeStruct((4 * CH, CH), F32),
        jax.ShapeDtypeStruct((KSIDE * KSIDE, 2, CH), F32),
        jax.ShapeDtypeStruct((2, CH, HID), F32),
        jax.ShapeDtypeStruct((2, HID, CH), F32),
    )
    outs = pl.pallas_call(
        widen_kernel,
        out_shape=shapes,
        in_specs=[vmem] * 7,
        out_specs=(pl.BlockSpec(memory_space=pltpu.HBM),) * 6,
        scratch_shapes=[pltpu.VMEM(leaf.shape, leaf.dtype) for leaf in shapes]
        + [pltpu.VMEM((112, 128), F32), pltpu.SemaphoreType.DMA((8,))],
        compiler_params=pltpu.CompilerParams(vmem_limit_bytes=24 * 2**20),
    )(*handed)
    return (
        outs[0].reshape(1, SIDE, SIDE, CH), outs[1], outs[2], jnp.transpose(outs[3], (1, 0, 2)), outs[4], outs[5],
    )


def solution(mesh):
    in_specs = (
        P("dp", "lon", "lat", None, None, None),
        P("dp", "lon", "lat", None, None, None),
        P("dp", "lon", "lat", None),
        P("dp", "lon", "lat", None),
        P(),
        P(),
        P(),
        P(),
        P(),
        P("dp", "lon", "lat", None),
    )
    out_specs = (P("dp", "lon", "lat", None), P(), P(), P(), P(), P())
    return jax.shard_map(
        on_device, mesh=mesh, in_specs=in_specs, out_specs=out_specs, check_vma=False
    )
```
